768 devices in a mesh: dp: 24 (over z_lo, x, core), fsdp: 32 (over z_hi, y).
Axes of the slice: x: 4, y: 8, z: 12 (z_hi: 4, z_lo: 3; z = z_hi * 3 + z_lo), core: 2. Of those that a mesh axis runs over, the one named last changes fastest.
Arguments:
- patches: bfloat16 [9216, 32, 1280], P(('dp', 'fsdp')), may hold values from -16 to 16
- values: bfloat16 [9216, 32, 640], P(('dp', 'fsdp')), may hold values from -6 to 6
- upstream: bfloat16 [9216, 32, 640], P(('dp', 'fsdp')), may hold values from -6 to 6
- coords: int32 [9216, 2, 32], P(('dp', 'fsdp')), may hold values from 0 to 31, as said below
- counts: int32 [9216], P(('dp', 'fsdp')), may hold values from 1 to 32
- dest: int32 [9216, 1], P(('dp', 'fsdp')), may hold values from 0 to 23; in each aligned block of 12 rows (0 to 11, 12 to 23, ...) no two rows name the same one
- weight: bfloat16 [1280, 1280], P('fsdp'), may hold values from -0.15625 to 0.15625
Outputs:
- context: bfloat16 [18432, 32, 640], P(('dp', 'fsdp'))
- grad_weight: float32 [1280, 1280], P('fsdp')
The draws below stay inside these ranges and needn't reach their ends.
Inputs may be any that keep to these rules, and one draw needn't show every extreme that they name: `dest`: the 12 windows of one device are assigned to different dp indices. `coords`: A patch's row and column in a grid of some width, in row-major order.
All inputs are finite; a program needn't handle non-finite values.
Results may differ from the reference program's by a relative error of at most 0.033.
The reference program's roundings to bfloat16 on the way count: a program that leaves them out, or rounds other values in their place, can miss the bound.
Values may be sent and summed in bfloat16 or wider, within the bound.
No kernel may reach another device: no remote copies, remote signals or barrier semaphores. Data moves between devices by JAX's collectives and lax.ppermute only.
A program may use at most 32 MiB of HBM per device.

```python
import math
import jax
import jax.numpy as jnp
import numpy as np
from jax import lax

D = 1280
HD = 80
HQ = 640
P_SIZE = 32
IMG_DEV = 12
IMAGES = 9216
N_DP = 24
N_FSDP = 32


def draw_patches(key, part):
    key = jax.random.fold_in(key, 11)
    base_key = jax.random.fold_in(key, 0)
    base = jax.random.normal(base_key, (IMAGES, P_SIZE, D), jnp.float32)
    return jnp.clip(base, -16.0, 16.0).astype(jnp.bfloat16)


def draw_counts(key, part):
    key = jax.random.fold_in(key, 23)
    drawn = jax.random.randint(key, (IMAGES,), 1, P_SIZE + 1, jnp.int32)
    return drawn.at[0].set(P_SIZE).at[1].set(1)


def draw_coords(key, part):
    key = jax.random.fold_in(key, 37)
    widths = jax.random.randint(key, (IMAGES, 1), 1, 9, jnp.int32)
    widths = widths.at[0, 0].set(1)
    order = jnp.arange(P_SIZE, dtype=jnp.int32)[None, :]
    return jnp.stack([order // widths, order % widths], axis=1).astype(jnp.int32)


def block_scale(own_key, extent, cuts, least, top_value):
    level, own = 1.0, jax.random.fold_in(own_key, 6)
    for axis_at, shards_of in cuts:
        heights = jnp.exp(jax.random.uniform(jax.random.fold_in(own, axis_at), (shards_of,), jnp.float32, least / len(cuts), top_value / len(cuts)))
        level = level * jnp.repeat(heights, extent[axis_at] // shards_of).reshape([-1 if axis == axis_at else 1 for axis in range(len(extent))])
    return level


def routed_block(stream_key, own, number, rows, count, top, limit, skew):
    sequence = jax.random.permutation(stream_key, count)
    heavy_load, ordinary = portions_of(count, rows * top, limit, skew, True), portions_of(count, rows * top, limit, skew, False)
    places = jnp.arange(count)

    def named(sizes, offset_by):
        used = int((sizes > 0).sum())
        fixed = max(1, used // 4)
        moved = fixed + (places - fixed + offset_by * (used - fixed)) % max(1, count - fixed)
        return jnp.zeros((count,), jnp.int32).at[sequence[jnp.where(places < fixed, places, moved)]].set(jnp.asarray(sizes, jnp.int32))

    sizes = jnp.where(number % 4 == 0, named(heavy_load, number // 4), named(ordinary, number - number // 4 - 1))
    mixed = jax.random.permutation(jax.random.fold_in(own, 3), count)
    donor, taker = mixed[0:count // 2 * 2:2], mixed[1:count // 2 * 2:2]
    slack = jnp.minimum(sizes[donor] - 1, limit - sizes[taker]) // 2
    slack = jnp.where((donor == sequence[0]) | (taker == sequence[0]) | (sizes[taker] == 0), 0, jnp.maximum(slack, 0))
    moved = jax.random.randint(jax.random.fold_in(own, 4), (count // 2,), 0, 1 << 20) % (slack + 1)
    sizes = sizes.at[donor].add(-moved).at[taker].add(moved)
    members = jnp.searchsorted(jnp.cumsum(sizes), jnp.arange(rows * top), side="right").astype(jnp.int32)
    grid = members.reshape(top, rows).T
    grid = grid[jax.random.permutation(jax.random.fold_in(own, 1), rows)]
    offset_by = jax.random.randint(jax.random.fold_in(own, 2), (rows, 1), 0, top)
    return jnp.take_along_axis(grid, (jnp.arange(top)[None, :] + offset_by) % top, axis=1)


def portions_of(amount, total, limit, skew, full):
    loads = [(1 << 20) // math.isqrt(standing ** skew) + 1 for standing in range(1, amount + 1)]
    largest = limit if full else min(limit, max(-(-total // amount), total * loads[0] // sum(loads)))
    least = 1 if total - largest >= amount - 1 else 0
    given, surplus = [largest] + [least] * (amount - 1), total - largest - least * (amount - 1)
    while surplus > 0:
        free = [i for i in range(1, amount) if given[i] < largest] or [i for i in range(1, amount) if given[i] < limit]
        pool, budget = sum([loads[i] for i in free]), surplus
        for i in free:
            extra = min(limit - given[i], max(1, budget * loads[i] // pool), surplus)
            given[i] = given[i] + extra
            surplus = surplus - extra
    return np.array(given)


def centred(own_key, dims, width, most, cuts=(), held_as=jnp.bfloat16):
    entries = width * jax.random.normal(own_key, dims, jnp.float32)
    if cuts:
        entries = entries * block_scale(own_key, dims, cuts, -0.22, 0.18)
    return jnp.clip(entries, -most, most).astype(held_as)


def setup_inputs(seed: int = 0) -> dict:
    streams_of = jax.random.split(jax.random.key(seed), 8)
    patches = draw_patches(jax.random.fold_in(streams_of[7], 71), 0)
    values = centred(streams_of[1], (IMAGES, P_SIZE, HQ), 1.0, 6.0, ((0, 768),))
    upstream = centred(streams_of[2], (IMAGES, P_SIZE, HQ), 1.0, 6.0, ((0, 768),))
    coords = draw_coords(jax.random.fold_in(streams_of[7], 71), 0)
    counts = draw_counts(jax.random.fold_in(streams_of[7], 71), 0)
    dest_keys = jax.random.split(jax.random.fold_in(streams_of[5], 1), IMAGES // IMG_DEV)
    dest_turns = jax.random.permutation(jax.random.fold_in(streams_of[5], 3), IMAGES // IMG_DEV)
    dest = jax.vmap(lambda own, number: routed_block(jax.random.fold_in(streams_of[5], 2), own, number, IMG_DEV, N_DP, 1, 1, 2))(dest_keys, dest_turns).reshape((IMAGES, 1))
    weight = centred(streams_of[6], (D, 2 * HQ), D ** -0.5, 0.15625, ((0, 32),))
    return {"patches": patches, "values": values, "upstream": upstream, "coords": coords, "counts": counts, "dest": dest, "weight": weight}


def rotary(tensor_in, row_pos, col_pos, turn_sign):
    quarter = tensor_in.shape[-1] // 4
    frequency = 10000.0 ** (-jnp.arange(quarter, dtype=jnp.float32) / quarter)
    pieces = []
    for position, section in ((row_pos, tensor_in[..., :2 * quarter]), (col_pos, tensor_in[..., 2 * quarter:])):
        angles = position[:, None] * frequency[None, :]
        cosine = jnp.cos(angles)[:, None, :]
        sine_part = turn_sign * jnp.sin(angles)[:, None, :]
        front_half = section[..., :quarter]
        back_half = section[..., quarter:]
        pieces.append(front_half * cosine - back_half * sine_part)
        pieces.append(back_half * cosine + front_half * sine_part)
    return jnp.concatenate(pieces, axis=-1)

def one_image(patches, values, upstream, coords, count, weight):
    patch_count = patches.shape[0]
    split_at = values.shape[-1]
    head_count = split_at // HD
    score_scale = 1.0 / math.sqrt(HD)
    is_live = jnp.arange(patch_count, dtype=jnp.int32) < count
    live_float = is_live.astype(jnp.float32)
    row_pos = coords[0].astype(jnp.float32)
    col_pos = coords[1].astype(jnp.float32)
    projected = jnp.dot(patches, weight, preferred_element_type=jnp.float32)
    queries = rotary(projected[:, :split_at].reshape(patch_count, head_count, HD), row_pos, col_pos, 1.0)
    keys_rot = rotary(projected[:, split_at:].reshape(patch_count, head_count, HD), row_pos, col_pos, 1.0)
    queries = lax.optimization_barrier(queries.astype(jnp.bfloat16)).astype(jnp.float32)
    keys_rot = lax.optimization_barrier(keys_rot.astype(jnp.bfloat16)).astype(jnp.float32)
    value_heads = values.reshape(patch_count, head_count, HD).astype(jnp.float32)
    upstream_heads = upstream.reshape(patch_count, head_count, HD).astype(jnp.float32)
    scores = jnp.einsum('qhd,khd->hqk', queries, keys_rot) * score_scale
    scores = jnp.where(is_live[None, None, :], scores, -1e+30)
    row_max = lax.optimization_barrier(jnp.max(scores, axis=-1, keepdims=True))
    exps = jnp.exp(scores - row_max)
    probs = exps / lax.optimization_barrier(jnp.sum(exps, axis=-1, keepdims=True)) * live_float[None, :, None]
    probs_low = lax.optimization_barrier(probs.astype(jnp.bfloat16)).astype(jnp.float32)
    context = jnp.einsum('hqk,khd->qhd', probs_low, value_heads).astype(jnp.bfloat16).reshape(patch_count, split_at)
    dprobs = jnp.einsum('qhd,khd->hqk', upstream_heads, value_heads)
    row_delta = lax.optimization_barrier(jnp.sum(probs * dprobs, axis=-1, keepdims=True))
    dscores = probs * (dprobs - row_delta) * score_scale
    dscores = lax.optimization_barrier(dscores.astype(jnp.bfloat16)).astype(jnp.float32)
    dquery = jnp.einsum('hqk,khd->qhd', dscores, keys_rot)
    dkey = jnp.einsum('hqk,qhd->khd', dscores, queries)
    grads_proj = jnp.concatenate([rotary(dquery, row_pos, col_pos, -1.0).reshape(patch_count, split_at), rotary(dkey, row_pos, col_pos, -1.0).reshape(patch_count, split_at)], axis=-1)
    return (context, grads_proj.astype(jnp.bfloat16))

def reference(patches, values, upstream, coords, counts, dest, weight):
    image_total = patches.shape[0]
    device_total = image_total // IMG_DEV
    image_ids = jnp.arange(image_total, dtype=jnp.int32)
    device_id = image_ids // IMG_DEV
    source_dp = device_id // N_FSDP
    source_fsdp = device_id % N_FSDP
    out_slot = ((dest[:, 0] * N_FSDP + source_fsdp) * N_DP + source_dp).astype(jnp.int32)
    zero_grad = jnp.zeros((weight.shape[0], weight.shape[1]), jnp.float32)

    def grouped(array):
        return array.reshape((device_total, IMG_DEV) + array.shape[1:])

    def per_device(running, block):
        take_patches, take_values, take_upstream, take_coords, take_counts = block
        contexts, grads = jax.vmap(one_image, in_axes=(0, 0, 0, 0, 0, None))(take_patches, take_values, take_upstream, take_coords, take_counts, weight)
        flat_patches = take_patches.reshape(-1, take_patches.shape[-1])
        flat_grads = grads.reshape(-1, grads.shape[-1])
        partial_value = jnp.dot(flat_patches.T, flat_grads, preferred_element_type=jnp.float32)
        rounded = lax.optimization_barrier(partial_value.astype(jnp.bfloat16)).astype(jnp.float32)
        return (running + rounded, contexts)
    grad_weight, contexts = lax.scan(per_device, zero_grad, (grouped(patches), grouped(values), grouped(upstream), grouped(coords), grouped(counts)))
    contexts = contexts.reshape((image_total,) + contexts.shape[2:])
    slot_total = N_DP * N_FSDP * N_DP
    context = jnp.zeros((slot_total,) + contexts.shape[1:], jnp.bfloat16).at[out_slot].set(contexts)
    return (context, grad_weight)
```

```python
import math

import jax
import jax.numpy as jnp
from jax import lax
from jax.sharding import Mesh
from jax.sharding import PartitionSpec as P

HD = 80
SPLIT = (3, 4, 2, 4, 8)
AXES = ("zl", "x", "c", "zh", "y")


def rotary(tensor_in, row_pos, col_pos, turn_sign):
    quarter = tensor_in.shape[-1] // 4
    frequency = 10000.0 ** (-jnp.arange(quarter, dtype=jnp.float32) / quarter)
    pieces = []
    for position, section in (
        (row_pos, tensor_in[..., : 2 * quarter]),
        (col_pos, tensor_in[..., 2 * quarter :]),
    ):
        angles = position[:, None] * frequency[None, :]
        cosine = jnp.cos(angles)[:, None, :]
        sine_part = turn_sign * jnp.sin(angles)[:, None, :]
        front_half = section[..., :quarter]
        back_half = section[..., quarter:]
        pieces.append(front_half * cosine - back_half * sine_part)
        pieces.append(back_half * cosine + front_half * sine_part)
    return jnp.concatenate(pieces, axis=-1)


def core_swap(array):
    return lax.ppermute(array, "c", [(0, 1), (1, 0)])


def swap_x_zh(array):
    nx, nz = lax.axis_size("x"), lax.axis_size("zh")
    pairs = [(i * nz + j, j * nz + i) for i in range(nx) for j in range(nz)]
    return lax.ppermute(array, ("x", "zh"), pairs)


def spread(array, axes):
    count = lax.axis_size(axes)
    copies = jnp.broadcast_to(array[None], (count,) + array.shape)
    return lax.all_to_all(copies, axes, split_axis=0, concat_axis=0, tiled=True)


def gather_weight(weight, core):
    width = weight.shape[1] // 2
    own = lax.dynamic_slice_in_dim(weight, core * width, width, axis=1)
    own = swap_x_zh(own)
    own = spread(own, "y").reshape(-1, width)
    own = spread(own, "x").reshape(-1, width)
    return own, core_swap(own)


def reduce_gradient(part, core):
    ny, nx = lax.axis_size("y"), lax.axis_size("x")
    rows, width = part.shape
    part = part.astype(jnp.bfloat16).reshape(nx, rows // nx, width)
    part = lax.all_to_all(part, "x", split_axis=0, concat_axis=0, tiled=True)
    part = jnp.sum(part.astype(jnp.float32), axis=0).astype(jnp.bfloat16)
    part = part.reshape(ny, rows // (nx * ny), width)
    part = lax.all_to_all(part, "y", split_axis=0, concat_axis=0, tiled=True)
    part = jnp.sum(part.astype(jnp.float32), axis=0).astype(jnp.bfloat16)
    part = swap_x_zh(part)
    part = spread(part, ("zl", "x"))
    part = jnp.sum(part.astype(jnp.float32), axis=0).astype(jnp.bfloat16)
    other = core_swap(part)
    first = jnp.where(core == 0, part, other)
    second = jnp.where(core == 0, other, part)
    return jnp.concatenate([first, second], axis=1).astype(jnp.float32)


def per_device(patches, values, upstream, coords, counts, dest, weight):
    core = lax.axis_index("c")
    peer_count = lax.axis_size(("zl", "x", "c"))
    window_count, patch_len, model_width = patches.shape
    value_width = values.shape[-1]
    head_count = value_width // HD
    score_scale = 1.0 / math.sqrt(HD)
    row_total = window_count * patch_len
    flat_patches = patches.reshape(row_total, model_width)
    other_patches = core_swap(flat_patches)
    own_w, other_w = gather_weight(weight, core)
    own_proj = jnp.dot(flat_patches, own_w, preferred_element_type=jnp.float32)
    other_proj = jnp.dot(flat_patches, other_w, preferred_element_type=jnp.float32)
    q_proj = jnp.where(core == 0, own_proj, other_proj)
    k_proj = jnp.where(core == 0, other_proj, own_proj)
    row_pos = coords[:, 0, :].reshape(row_total).astype(jnp.float32)
    col_pos = coords[:, 1, :].reshape(row_total).astype(jnp.float32)
    valid = (jnp.arange(patch_len, dtype=jnp.int32)[None, :] < counts[:, None]).reshape(row_total)
    group_size = math.gcd(window_count, max(1, 128 // patch_len))
    block_count = window_count // group_size
    block_rows = group_size * patch_len
    head_shape = (block_count, block_rows, head_count, HD)
    queries = rotary(q_proj.reshape(row_total, head_count, HD), row_pos, col_pos, 1.0)
    keys_rot = rotary(k_proj.reshape(row_total, head_count, HD), row_pos, col_pos, 1.0)
    queries = queries.astype(jnp.bfloat16).reshape(head_shape)
    keys_rot = keys_rot.astype(jnp.bfloat16).reshape(head_shape)
    value_heads = values.reshape(head_shape)
    upstream_heads = upstream.reshape(head_shape)
    window_of = jnp.arange(block_rows, dtype=jnp.int32) // patch_len
    same_window = window_of[:, None] == window_of[None, :]
    valid_blocks = valid.reshape(block_count, block_rows)
    key_ok = same_window[None, :, :] & valid_blocks[:, None, :]
    scores = (
        jnp.einsum("bqhd,bkhd->bhqk", queries, keys_rot, preferred_element_type=jnp.float32)
        * score_scale
    )
    scores = jnp.where(key_ok[:, None, :, :], scores, -1e30)
    row_max = jnp.max(scores, axis=-1, keepdims=True)
    exps = jnp.exp(scores - row_max)
    probs = (
        exps
        / jnp.sum(exps, axis=-1, keepdims=True)
        * valid_blocks.astype(jnp.float32)[:, None, :, None]
    )
    probs_low = probs.astype(jnp.bfloat16)
    context = jnp.einsum(
        "bhqk,bkhd->bqhd", probs_low, value_heads, preferred_element_type=jnp.float32
    )
    context = context.astype(jnp.bfloat16).reshape(window_count, patch_len * value_width)
    onehot = (dest[:, 0][:, None] == jnp.arange(peer_count, dtype=jnp.int32)[None, :]).astype(
        jnp.bfloat16
    )
    routed = jnp.einsum("sp,sc->pc", onehot, context, preferred_element_type=jnp.float32)
    routed = routed.astype(jnp.bfloat16).reshape(peer_count, patch_len, value_width)
    placed = lax.all_to_all(routed, ("zl", "x", "c"), split_axis=0, concat_axis=0, tiled=True)
    dprobs = jnp.einsum(
        "bqhd,bkhd->bhqk", upstream_heads, value_heads, preferred_element_type=jnp.float32
    )
    row_delta = jnp.sum(probs * dprobs, axis=-1, keepdims=True)
    dscores = (probs * (dprobs - row_delta) * score_scale).astype(jnp.bfloat16)
    dquery = jnp.einsum("bhqk,bkhd->bqhd", dscores, keys_rot, preferred_element_type=jnp.float32)
    dkey = jnp.einsum("bhqk,bqhd->bkhd", dscores, queries, preferred_element_type=jnp.float32)
    dquery = rotary(dquery.reshape(row_total, head_count, HD), row_pos, col_pos, -1.0)
    dkey = rotary(dkey.reshape(row_total, head_count, HD), row_pos, col_pos, -1.0)
    dquery = dquery.reshape(row_total, value_width).astype(jnp.bfloat16)
    dkey = dkey.reshape(row_total, value_width).astype(jnp.bfloat16)
    kept = jnp.where(core == 0, dquery, dkey)
    sent = jnp.where(core == 0, dkey, dquery)
    received = core_swap(sent)
    both_patches = jnp.concatenate([flat_patches, other_patches], axis=0)
    both_grads = jnp.concatenate([kept, received], axis=0)
    part = jnp.einsum("rd,rc->dc", both_patches, both_grads, preferred_element_type=jnp.float32)
    return (placed, reduce_gradient(part, core))


def solution(mesh):
    fine = Mesh(mesh.devices.reshape(SPLIT), AXES)
    return jax.shard_map(
        per_device,
        mesh=fine,
        in_specs=(
            P(AXES, None, None),
            P(AXES, None, None),
            P(AXES, None, None),
            P(AXES, None, None),
            P(AXES),
            P(AXES, None),
            P(("zh", "y"), None),
        ),
        out_specs=(P(AXES, None, None), P(("zh", "y"), None)),
        check_vma=False,
    )
```

```python
import functools
import math

import jax
import jax.numpy as jnp
from jax import lax
from jax.experimental import pallas as pl
from jax.experimental.pallas import tpu as pltpu
from jax.sharding import Mesh
from jax.sharding import PartitionSpec as P

HD = 80
SPLIT = (3, 4, 2, 4, 8)
AXES = ("zl", "x", "c", "zh", "y")


def core_swap(array):
    return lax.ppermute(array, "c", [(0, 1), (1, 0)])


def swap_x_zh(array):
    nx, nz = lax.axis_size("x"), lax.axis_size("zh")
    pairs = [(i * nz + j, j * nz + i) for i in range(nx) for j in range(nz)]
    return lax.ppermute(array, ("x", "zh"), pairs)


def spread(array, axes):
    count = lax.axis_size(axes)
    copies = jnp.broadcast_to(array[None], (count,) + array.shape)
    return lax.all_to_all(copies, axes, split_axis=0, concat_axis=0, tiled=True)


def gather_weight(weight, core):
    width = weight.shape[1] // 2
    own = lax.dynamic_slice_in_dim(weight, core * width, width, axis=1)
    own = swap_x_zh(own)
    own = spread(own, "y").reshape(-1, width)
    own = spread(own, "x").reshape(-1, width)
    return own, core_swap(own)


def reduce_gradient(part, core):
    ny, nx = lax.axis_size("y"), lax.axis_size("x")
    rows, width = part.shape
    part = part.astype(jnp.bfloat16).reshape(nx, rows // nx, width)
    part = lax.all_to_all(part, "x", split_axis=0, concat_axis=0, tiled=True)
    part = jnp.sum(part.astype(jnp.float32), axis=0).astype(jnp.bfloat16)
    part = part.reshape(ny, rows // (nx * ny), width)
    part = lax.all_to_all(part, "y", split_axis=0, concat_axis=0, tiled=True)
    part = jnp.sum(part.astype(jnp.float32), axis=0).astype(jnp.bfloat16)
    part = swap_x_zh(part)
    part = spread(part, ("zl", "x"))
    part = jnp.sum(part.astype(jnp.float32), axis=0).astype(jnp.bfloat16)
    other = core_swap(part)
    first = jnp.where(core == 0, part, other)
    second = jnp.where(core == 0, other, part)
    return jnp.concatenate([first, second], axis=1).astype(jnp.float32)


def partner(array):
    width = array.shape[1]
    quarter = HD // 4
    lane = lax.broadcasted_iota(jnp.int32, array.shape, 1)
    front = lax.rem(lane, 2 * quarter) < quarter
    ahead = pltpu.roll(array, width - quarter, 1)
    behind = pltpu.roll(array, quarter, 1)
    return jnp.where(front, -ahead, behind)


def dot(a, b, dims):
    return lax.dot_general(a, b, (dims, ((), ())), preferred_element_type=jnp.float32)


def attention_kernel(
    patch_len,
    group,
    scalars,
    patches_ref,
    weight_ref,
    own_ref,
    cos_ref,
    sin_ref,
    values_ref,
    upstream_ref,
    routed_ref,
    kept_ref,
    sent_ref,
    proj_ref,
    query_ref,
    key_ref,
    dquery_ref,
    dkey_ref,
    context_ref,
):
    rows, width = own_ref.shape
    windows = rows // patch_len
    heads = width // HD
    scale = 1.0 / math.sqrt(HD)
    is_first = scalars[0] == 0
    proj_ref[...] = dot(patches_ref[...], weight_ref[...], ((1,), (0,)))
    routed_ref[...] = jnp.zeros_like(routed_ref)
    block = group * patch_len
    step = 32
    for start in range(0, rows, step):
        span = pl.ds(start, step)
        own, other = own_ref[span, :], proj_ref[span, :]
        cosine, sine = cos_ref[span, :], sin_ref[span, :]
        query = jnp.where(is_first, own, other)
        key = jnp.where(is_first, other, own)
        query_ref[span, :] = (query * cosine + partner(query) * sine).astype(jnp.bfloat16)
        key_ref[span, :] = (key * cosine + partner(key) * sine).astype(jnp.bfloat16)
    row_at = lax.broadcasted_iota(jnp.int32, (block, block), 0)
    key_at = lax.broadcasted_iota(jnp.int32, (block, block), 1)
    row_win, key_win = row_at // patch_len, key_at // patch_len
    row_one = lax.broadcasted_iota(jnp.int32, (block, 1), 0)
    same = row_win == key_win
    for first in range(0, windows, group):
        key_count = jnp.full((block, block), scalars[1 + first], jnp.int32)
        row_count = jnp.full((block, 1), scalars[1 + first], jnp.int32)
        for later in range(1, group):
            count = scalars[1 + first + later]
            key_count = jnp.where(key_win == later, count, key_count)
            row_count = jnp.where(row_one // patch_len == later, count, row_count)
        key_ok = same & (key_at - key_win * patch_len < key_count)
        row_live = (row_one - row_one // patch_len * patch_len < row_count).astype(jnp.float32)
        span = pl.ds(first * patch_len, block)
        for head in range(heads):
            lanes = pl.ds(head * HD, HD)
            q, k = query_ref[span, lanes], key_ref[span, lanes]
            v, u = values_ref[span, lanes], upstream_ref[span, lanes]
            scores = jnp.where(key_ok, dot(q, k, ((1,), (1,))) * scale, -1e30)
            exps = jnp.exp(scores - jnp.max(scores, axis=1, keepdims=True))
            factor = row_live / jnp.sum(exps, axis=1, keepdims=True)
            probs = exps * factor
            low = probs.astype(jnp.bfloat16)
            context_ref[span, lanes] = dot(low, v, ((1,), (0,))).astype(jnp.bfloat16)
            dprobs = dot(u, v, ((1,), (1,)))
            delta = jnp.sum(probs * dprobs, axis=1, keepdims=True)
            dscores = (probs * (dprobs - delta) * scale).astype(jnp.bfloat16)
            dquery_ref[span, lanes] = dot(dscores, k, ((1,), (0,)))
            dkey_ref[span, lanes] = dot(dscores, q, ((0,), (0,)))
        for window in range(first, first + group):
            here = pl.ds(window * patch_len, patch_len)
            routed_ref[scalars[1 + windows + window]] = context_ref[here, :]
    for start in range(0, rows, step):
        span = pl.ds(start, step)
        cosine, sine = cos_ref[span, :], sin_ref[span, :]
        dquery, dkey = dquery_ref[span, :], dkey_ref[span, :]
        dquery = (dquery * cosine - partner(dquery) * sine).astype(jnp.bfloat16)
        dkey = (dkey * cosine - partner(dkey) * sine).astype(jnp.bfloat16)
        kept_ref[span, :] = jnp.where(is_first, dquery, dkey)
        sent_ref[span, :] = jnp.where(is_first, dkey, dquery)


def attention(scalars, patches, weight, own, cosine, sine, values, upstream, patch_len, slots):
    rows, width = own.shape
    windows = rows // patch_len
    group = math.gcd(windows, max(1, 128 // patch_len))
    vmem = pl.BlockSpec(memory_space=pltpu.VMEM)
    return pl.pallas_call(
        functools.partial(attention_kernel, patch_len, group),
        in_specs=[pl.BlockSpec(memory_space=pltpu.SMEM)] + [vmem] * 7,
        out_specs=[vmem] * 3,
        out_shape=[
            jax.ShapeDtypeStruct((slots, patch_len, width), jnp.bfloat16),
            jax.ShapeDtypeStruct((rows, width), jnp.bfloat16),
            jax.ShapeDtypeStruct((rows, width), jnp.bfloat16),
        ],
        scratch_shapes=[
            pltpu.VMEM((rows, width), jnp.float32),
            pltpu.VMEM((rows, width), jnp.bfloat16),
            pltpu.VMEM((rows, width), jnp.bfloat16),
            pltpu.VMEM((rows, width), jnp.float32),
            pltpu.VMEM((rows, width), jnp.float32),
            pltpu.VMEM((rows, width), jnp.bfloat16),
        ],
        compiler_params=pltpu.CompilerParams(vmem_limit_bytes=40 * 1024 * 1024),
        cost_estimate=pl.CostEstimate(
            flops=2 * rows * width * 1280 + 10 * rows * 128 * width,
            bytes_accessed=12_000_000,
            transcendentals=rows * 128 * 8,
        ),
        name="window_attention",
    )(scalars, patches, weight, own, cosine, sine, values, upstream)


def rotary_tables(coords, heads):
    quarter = HD // 4
    frequency = 10000.0 ** (-jnp.arange(quarter, dtype=jnp.float32) / quarter)
    position = coords.astype(jnp.float32)
    angles = position[:, :, :, None] * frequency
    angles = jnp.concatenate([angles[:, 0], angles[:, 0], angles[:, 1], angles[:, 1]], axis=-1)
    angles = angles.reshape(-1, HD)
    return jnp.tile(jnp.cos(angles), (1, heads)), jnp.tile(jnp.sin(angles), (1, heads))


def per_device(patches, values, upstream, coords, counts, dest, weight):
    core = lax.axis_index("c")
    slots = lax.axis_size(("zl", "x", "c"))
    window_count, patch_len, model_width = patches.shape
    value_width = values.shape[-1]
    row_total = window_count * patch_len
    flat_patches = patches.reshape(row_total, model_width)
    other_patches = core_swap(flat_patches)
    cosine, sine = rotary_tables(coords, value_width // HD)
    own_w, other_w = gather_weight(weight, core)
    own_proj = jnp.dot(flat_patches, own_w, preferred_element_type=jnp.float32)
    scalars = jnp.concatenate([core.astype(jnp.int32)[None], counts, dest[:, 0]])
    routed, kept, sent = attention(
        scalars,
        flat_patches,
        other_w,
        own_proj,
        cosine,
        sine,
        values.reshape(row_total, value_width),
        upstream.reshape(row_total, value_width),
        patch_len,
        slots,
    )
    received = core_swap(sent)
    both_patches = jnp.concatenate([flat_patches, other_patches], axis=0)
    both_grads = jnp.concatenate([kept, received], axis=0)
    part = jnp.einsum("rd,rc->dc", both_patches, both_grads, preferred_element_type=jnp.float32)
    placed = lax.all_to_all(routed, ("zl", "x", "c"), split_axis=0, concat_axis=0, tiled=True)
    return (placed, reduce_gradient(part, core))


def solution(mesh):
    fine = Mesh(mesh.devices.reshape(SPLIT), AXES)
    return jax.shard_map(
        per_device,
        mesh=fine,
        in_specs=(
            P(AXES, None, None),
            P(AXES, None, None),
            P(AXES, None, None),
            P(AXES, None, None),
            P(AXES),
            P(AXES, None),
            P(("zh", "y"), None),
        ),
        out_specs=(P(AXES, None, None), P(("zh", "y"), None)),
        check_vma=False,
    )
```

```python
import functools
import math

import jax
import jax.numpy as jnp
from jax import lax
from jax.experimental import pallas as pl
from jax.experimental.pallas import tpu as pltpu
from jax.sharding import Mesh
from jax.sharding import PartitionSpec as P

HD = 80
LANES = 128
SPLIT = (3, 4, 2, 4, 8)
AXES = ("zl", "x", "c", "zh", "y")
BF16 = jnp.bfloat16
F32 = jnp.float32


def core_swap(array):
    return lax.ppermute(array, "c", [(0, 1), (1, 0)])


def ring_x(array, step):
    count = lax.axis_size("x")
    return lax.ppermute(array, "x", [(i, (i + step) % count) for i in range(count)])


def exchange(array, axes):
    return lax.all_to_all(array, axes, split_axis=0, concat_axis=0, tiled=True)


def spread(array, axes):
    count = lax.axis_size(axes)
    return exchange(jnp.broadcast_to(array[None], (count,) + array.shape), axes)


def dot(a, b, dims):
    return lax.dot_general(a, b, (dims, ((), ())), preferred_element_type=F32)


def partner(array):
    quarter = HD // 4
    lane = lax.broadcasted_iota(jnp.int32, array.shape, 1)
    front = lax.rem(lane, 2 * quarter) < quarter
    ahead = pltpu.roll(array, LANES - quarter, 1)
    behind = pltpu.roll(array, quarter, 1)
    return jnp.where(front, -ahead, behind)


def head_kernel(
    patch_len,
    group,
    counts,
    weight_ref,
    patches_ref,
    turned_ref,
    cos_ref,
    sin_ref,
    values_ref,
    upstream_ref,
    context_ref,
    grad_ref,
    full_ref,
    proj_ref,
    dproj_ref,
):
    rows = patches_ref.shape[0]
    windows = rows // patch_len
    strip, strips = weight_ref.shape[0], weight_ref.shape[1] // (2 * HD)
    scale = 1.0 / math.sqrt(HD)
    full_ref[...] = jnp.zeros_like(full_ref)
    for z in range(strips):
        span, at = pl.ds(z * strip, strip), z * 2 * HD
        full_ref[span, pl.ds(0, HD)] = weight_ref[:, pl.ds(at, HD)]
        full_ref[span, pl.ds(LANES, HD)] = weight_ref[:, pl.ds(at + HD, HD)]
    proj_ref[...] = dot(patches_ref[...], full_ref[...], ((1,), (0,)))
    block = group * patch_len
    row_at = lax.broadcasted_iota(jnp.int32, (block, block), 0)
    key_at = lax.broadcasted_iota(jnp.int32, (block, block), 1)
    row_win, key_win = row_at // patch_len, key_at // patch_len
    row_one = lax.broadcasted_iota(jnp.int32, (block, 1), 0)
    same = row_win == key_win
    for first in range(0, windows, group):
        key_count = jnp.full((block, block), counts[first], jnp.int32)
        row_count = jnp.full((block, 1), counts[first], jnp.int32)
        for later in range(1, group):
            count = counts[first + later]
            key_count = jnp.where(key_win == later, count, key_count)
            row_count = jnp.where(row_one // patch_len == later, count, row_count)
        key_ok = same & (key_at - key_win * patch_len < key_count)
        row_live = (row_one - row_one // patch_len * patch_len < row_count).astype(F32)
        span = pl.ds(first * patch_len, block)
        cosine, sine = cos_ref[span, :], sin_ref[span, :]
        query, key = proj_ref[span, pl.ds(0, LANES)], proj_ref[span, pl.ds(LANES, LANES)]
        q = (query * cosine + partner(query) * sine).astype(BF16)
        k = (key * cosine + partner(key) * sine).astype(BF16)
        v, u = values_ref[span, :], upstream_ref[span, :]
        scores = jnp.where(key_ok, dot(q, k, ((1,), (1,))) * scale, -1e30)
        exps = jnp.exp(scores - jnp.max(scores, axis=1, keepdims=True))
        probs = exps * (row_live / jnp.sum(exps, axis=1, keepdims=True))
        context_ref[span, :] = dot(probs.astype(BF16), v, ((1,), (0,))).astype(BF16)
        dprobs = dot(u, v, ((1,), (1,)))
        delta = jnp.sum(probs * dprobs, axis=1, keepdims=True)
        dscores = (probs * (dprobs - delta) * scale).astype(BF16)
        dquery = dot(dscores, k, ((1,), (0,)))
        dkey = dot(dscores, q, ((0,), (0,)))
        dquery = dquery * cosine - partner(dquery) * sine
        dkey = dkey * cosine - partner(dkey) * sine
        dproj_ref[span, pl.ds(0, LANES)] = dquery.astype(BF16)
        dproj_ref[span, pl.ds(LANES, LANES)] = dkey.astype(BF16)
    for z in range(strips):
        at = z * 2 * HD
        part = dot(turned_ref[pl.ds(z * strip, strip), :], dproj_ref[...], ((1,), (0,)))
        part = part.astype(BF16)
        grad_ref[:, pl.ds(at, HD)] = part[:, :HD]
        grad_ref[:, pl.ds(at + HD, HD)] = part[:, LANES : LANES + HD]


def one_head(counts, weight, patches, turned, cosine, sine, values, upstream, patch_len):
    rows, model_width = patches.shape
    windows = rows // patch_len
    group = math.gcd(windows, max(1, 128 // patch_len))
    vmem = pl.BlockSpec(memory_space=pltpu.VMEM)
    return pl.pallas_call(
        functools.partial(head_kernel, patch_len, group),
        in_specs=[pl.BlockSpec(memory_space=pltpu.SMEM)] + [vmem] * 7,
        out_specs=[vmem] * 2,
        out_shape=[
            jax.ShapeDtypeStruct((rows, LANES), BF16),
            jax.ShapeDtypeStruct(weight.shape, BF16),
        ],
        scratch_shapes=[
            pltpu.VMEM((model_width, 2 * LANES), BF16),
            pltpu.VMEM((rows, 2 * LANES), F32),
            pltpu.VMEM((rows, 2 * LANES), BF16),
        ],
        compiler_params=pltpu.CompilerParams(vmem_limit_bytes=24 * 1024 * 1024),
        cost_estimate=pl.CostEstimate(
            flops=4_000_000_000, bytes_accessed=8_000_000, transcendentals=rows * 128
        ),
        name="one_head",
    )(counts, weight, patches, turned, cosine, sine, values, upstream)


def route_kernel(patch_len, dest, order, stack_ref, routed_ref):
    heads = stack_ref.shape[0]
    windows = stack_ref.shape[1] // patch_len // 2
    routed_ref[...] = jnp.zeros_like(routed_ref)
    for source in range(2):
        first = order[heads + source] * windows
        for window in range(windows):
            here = first + window
            rows = pl.ds(pl.multiple_of(here * patch_len, patch_len), patch_len)
            slot = dest[here]
            for head in range(heads):
                lanes = pl.ds((source * heads + head) * HD, HD)
                routed_ref[slot, :, lanes] = stack_ref[order[head], rows, :][:, :HD]


def route(dest, order, stack, slots, patch_len):
    heads = stack.shape[0]
    vmem = pl.BlockSpec(memory_space=pltpu.VMEM)
    smem = pl.BlockSpec(memory_space=pltpu.SMEM)
    return pl.pallas_call(
        functools.partial(route_kernel, patch_len),
        in_specs=[smem, smem, vmem],
        out_specs=vmem,
        out_shape=jax.ShapeDtypeStruct((slots, patch_len, 2 * heads * HD), BF16),
        compiler_params=pltpu.CompilerParams(vmem_limit_bytes=16 * 1024 * 1024),
        name="route",
    )(dest, order, stack)


def settle_kernel(arrived_ref, placed_ref):
    half = arrived_ref.shape[2] // 2
    for pair in range(0, arrived_ref.shape[0], 2):
        for source in range(2):
            lanes = pl.ds(source * half, half)
            for core in range(2):
                out = pl.ds(core * half, half)
                placed_ref[pair + source, :, out] = arrived_ref[pair + core, :, lanes]


def settle(arrived):
    vmem = pl.BlockSpec(memory_space=pltpu.VMEM)
    return pl.pallas_call(
        settle_kernel,
        in_specs=[vmem],
        out_specs=vmem,
        out_shape=jax.ShapeDtypeStruct(arrived.shape, BF16),
        compiler_params=pltpu.CompilerParams(vmem_limit_bytes=16 * 1024 * 1024),
        name="settle",
    )(arrived)


def rotary_tables(coords):
    quarter = HD // 4
    frequency = 10000.0 ** (-jnp.arange(quarter, dtype=F32) / quarter)
    angles = coords.astype(F32)[:, :, :, None] * frequency
    angles = jnp.concatenate([angles[:, 0], angles[:, 0], angles[:, 1], angles[:, 1]], axis=-1)
    angles = angles.reshape(-1, HD)
    pad = ((0, 0), (0, LANES - HD))
    return jnp.pad(jnp.cos(angles), pad), jnp.pad(jnp.sin(angles), pad)


def head_major(own, core, heads, order):
    rows = own.shape[0]
    width = heads * HD
    kept = lax.dynamic_slice_in_dim(own, core * width, width, axis=1)
    sent = lax.dynamic_slice_in_dim(own, (1 - core) * width, width, axis=1)
    both = jnp.concatenate([kept, core_swap(sent)], axis=0)
    both = jnp.pad(both.reshape(2 * rows, heads, HD), ((0, 0), (0, 0), (0, LANES - HD)))
    return [lax.dynamic_index_in_dim(both, at, axis=1, keepdims=False) for at in order]


def per_device(patches, values, upstream, coords, counts, dest, weight):
    core, here = lax.axis_index("c"), lax.axis_index("x")
    nx, ny, nz = lax.axis_size("x"), lax.axis_size("y"), lax.axis_size("zh")
    slots = lax.axis_size(("zl", "x", "c"))
    window_count, patch_len, model_width = patches.shape
    value_width = values.shape[-1]
    row_total = window_count * patch_len
    depth = weight.shape[0]
    steps = [0, 1, nx - 1] + list(range(2, nx - 1))
    order = [lax.rem(here + step, nx) for step in steps]

    head = core * nx + here
    slice_q = lax.dynamic_slice_in_dim(weight, head * HD, HD, axis=1)
    slice_k = lax.dynamic_slice_in_dim(weight, value_width + head * HD, HD, axis=1)
    own_w = spread(jnp.concatenate([slice_q, slice_k], axis=1), "zh")
    own_w = jnp.transpose(own_w, (1, 0, 2)).reshape(depth, nz * 2 * HD)
    own_w = spread(own_w, "y").reshape(ny * depth, nz * 2 * HD)
    weights = [own_w] + [ring_x(own_w, -step) for step in steps[1:]]

    flat = patches.reshape(row_total, model_width)
    both = jnp.concatenate([flat, core_swap(flat)], axis=0)
    turned = jnp.transpose(both)
    small = jnp.concatenate([coords.reshape(window_count, -1), counts[:, None], dest], axis=1)
    small = jnp.concatenate([small, core_swap(small)], axis=0)
    both_coords = small[:, : 2 * patch_len].reshape(2 * window_count, 2, patch_len)
    both_counts, both_dest = small[:, 2 * patch_len], small[:, 2 * patch_len + 1]
    cosine, sine = rotary_tables(both_coords)
    value_heads = head_major(values.reshape(row_total, value_width), core, nx, order)
    upstream_heads = head_major(upstream.reshape(row_total, value_width), core, nx, order)

    contexts, total = [], None
    for at, step in enumerate(steps):
        context, grad = one_head(
            both_counts,
            weights[at],
            both,
            turned,
            cosine,
            sine,
            value_heads[at],
            upstream_heads[at],
            patch_len,
        )
        contexts.append(context)
        if step:
            grad = ring_x(grad, step)
        total = grad.astype(F32) if total is None else total + grad.astype(F32)

    place = [jnp.int32(0)] * nx
    for at, head_at in enumerate(order):
        place = [jnp.where(head_at == h, at, place[h]) for h in range(nx)]
    place = jnp.stack(place + [core, 1 - core]).astype(jnp.int32)
    routed = route(both_dest, place, jnp.stack(contexts), slots, patch_len)
    placed = settle(exchange(routed, ("zl", "x", "c")))

    total = exchange(total.astype(BF16).reshape(ny, depth, nz * 2 * HD), "y")
    total = jnp.sum(total.astype(F32), axis=0).astype(BF16)
    total = jnp.transpose(total.reshape(depth, nz, 2 * HD), (1, 0, 2))
    copies = lax.axis_size("zl")
    total = jnp.broadcast_to(total[None], (copies,) + total.shape)
    total = exchange(total.reshape(copies * nz, depth, 2 * HD), ("zl", "zh"))
    total = jnp.sum(total.astype(F32), axis=0).astype(BF16)
    total = spread(total, ("x", "c")).reshape(nx, 2, depth, 2, HD)
    grad_weight = jnp.transpose(total, (2, 3, 1, 0, 4)).reshape(depth, 2 * value_width)
    return (placed, grad_weight.astype(F32))


def solution(mesh):
    fine = Mesh(mesh.devices.reshape(SPLIT), AXES)
    return jax.shard_map(
        per_device,
        mesh=fine,
        in_specs=(
            P(AXES, None, None),
            P(AXES, None, None),
            P(AXES, None, None),
            P(AXES, None, None),
            P(AXES),
            P(AXES, None),
            P(("zh", "y"), None),
        ),
        out_specs=(P(AXES, None, None), P(("zh", "y"), None)),
        check_vma=False,
    )
```

```python
import functools
import math

import jax
import jax.numpy as jnp
from jax import lax
from jax.experimental import pallas as pl
from jax.experimental.pallas import tpu as pltpu
from jax.sharding import Mesh
from jax.sharding import PartitionSpec as P

HD = 80
LANES = 128
SPLIT = (3, 4, 2, 4, 8)
AXES = ("zl", "x", "c", "zh", "y")
BF16 = jnp.bfloat16
F32 = jnp.float32


def core_swap(array):
    return lax.ppermute(array, "c", [(0, 1), (1, 0)])


def ring_x(array, step):
    count = lax.axis_size("x")
    return lax.ppermute(array, "x", [(i, (i + step) % count) for i in range(count)])


def exchange(array, axes):
    return lax.all_to_all(array, axes, split_axis=0, concat_axis=0, tiled=True)


def spread(array, axes):
    count = lax.axis_size(axes)
    return exchange(jnp.broadcast_to(array[None], (count,) + array.shape), axes)


def dot(a, b, dims):
    return lax.dot_general(a, b, (dims, ((), ())), preferred_element_type=F32)


def partner(array):
    quarter = HD // 4
    lane = lax.broadcasted_iota(jnp.int32, array.shape, 1)
    front = lax.rem(lane, 2 * quarter) < quarter
    ahead = pltpu.roll(array, LANES - quarter, 1)
    behind = pltpu.roll(array, quarter, 1)
    return jnp.where(front, -ahead, behind)


def head_kernel(
    patch_len,
    group,
    position,
    counts,
    order,
    weight_hbm,
    own_hbm,
    other_hbm,
    turned_hbm,
    cos_hbm,
    sin_hbm,
    values_hbm,
    upstream_hbm,
    context_ref,
    grad_ref,
    weight_ref,
    own_ref,
    other_ref,
    turned_ref,
    cos_ref,
    sin_ref,
    values_ref,
    upstream_ref,
    full_ref,
    proj_ref,
    dproj_ref,
    arrivals,
):
    rows = turned_ref.shape[1]
    windows = rows // patch_len
    head = order[position]
    strip, strips = weight_ref.shape[0], weight_ref.shape[1] // (2 * HD)
    moves = (
        (weight_hbm, weight_ref),
        (own_hbm, own_ref),
        (other_hbm, other_ref),
        (cos_hbm, cos_ref),
        (sin_hbm, sin_ref),
        (values_hbm.at[head], values_ref),
        (upstream_hbm.at[head], upstream_ref),
        (turned_hbm, turned_ref),
    )
    copies = [
        pltpu.make_async_copy(source, target, arrivals.at[at])
        for at, (source, target) in enumerate(moves)
    ]
    for copy in copies:
        copy.start()
    scale = 1.0 / math.sqrt(HD)
    full_ref[...] = jnp.zeros_like(full_ref)
    copies[0].wait()
    for z in range(strips):
        span, at = pl.ds(z * strip, strip), z * 2 * HD
        full_ref[span, pl.ds(0, HD)] = weight_ref[:, pl.ds(at, HD)]
        full_ref[span, pl.ds(LANES, HD)] = weight_ref[:, pl.ds(at + HD, HD)]
    half = rows // 2
    copies[1].wait()
    proj_ref[:half, :] = dot(own_ref[...], full_ref[...], ((1,), (0,)))
    copies[2].wait()
    proj_ref[half:, :] = dot(other_ref[...], full_ref[...], ((1,), (0,)))
    for copy in copies[3:7]:
        copy.wait()
    block = group * patch_len
    row_at = lax.broadcasted_iota(jnp.int32, (block, block), 0)
    key_at = lax.broadcasted_iota(jnp.int32, (block, block), 1)
    row_win, key_win = row_at // patch_len, key_at // patch_len
    row_one = lax.broadcasted_iota(jnp.int32, (block, 1), 0)
    same = row_win == key_win
    for start in range(0, windows, group * 3):
        firsts = [first for first in range(start, min(windows, start + group * 3), group)]
        spans = [pl.ds(first * patch_len, block) for first in firsts]
        each = range(len(firsts))
        masks, lives = [], []
        for first in firsts:
            key_count = jnp.full((block, block), counts[first], jnp.int32)
            row_count = jnp.full((block, 1), counts[first], jnp.int32)
            for later in range(1, group):
                count = counts[first + later]
                key_count = jnp.where(key_win == later, count, key_count)
                row_count = jnp.where(row_one // patch_len == later, count, row_count)
            masks.append(same & (key_at - key_win * patch_len < key_count))
            live = row_one - row_one // patch_len * patch_len < row_count
            lives.append(live.astype(F32))
        cosines, sines = [cos_ref[s, :] for s in spans], [sin_ref[s, :] for s in spans]
        q = [proj_ref[s, pl.ds(0, LANES)] for s in spans]
        k = [proj_ref[s, pl.ds(LANES, LANES)] for s in spans]
        q = [(q[i] * cosines[i] + partner(q[i]) * sines[i]).astype(BF16) for i in each]
        k = [(k[i] * cosines[i] + partner(k[i]) * sines[i]).astype(BF16) for i in each]
        scores = [dot(q[i], k[i], ((1,), (1,))) * scale for i in each]
        v = [values_ref[s, :] for s in spans]
        dprobs = [dot(upstream_ref[spans[i], :], v[i], ((1,), (1,))) for i in each]
        scores = [jnp.where(masks[i], scores[i], -1e30) for i in each]
        tops = [jnp.max(scores[i], axis=1, keepdims=True) for i in each]
        exps = [jnp.exp(scores[i] - tops[i]) for i in each]
        sums = [jnp.sum(exps[i], axis=1, keepdims=True) for i in each]
        probs = [exps[i] * (lives[i] / sums[i]) for i in each]
        context = [dot(probs[i].astype(BF16), v[i], ((1,), (0,))) for i in each]
        delta = [jnp.sum(probs[i] * dprobs[i], axis=1, keepdims=True) for i in each]
        dscores = [(probs[i] * (dprobs[i] - delta[i]) * scale).astype(BF16) for i in each]
        dquery = [dot(dscores[i], k[i], ((1,), (0,))) for i in each]
        dkey = [dot(dscores[i], q[i], ((0,), (0,))) for i in each]
        for i in each:
            context_ref[spans[i], :] = context[i].astype(BF16)
            back = dquery[i] * cosines[i] - partner(dquery[i]) * sines[i]
            dproj_ref[spans[i], pl.ds(0, LANES)] = back.astype(BF16)
            back = dkey[i] * cosines[i] - partner(dkey[i]) * sines[i]
            dproj_ref[spans[i], pl.ds(LANES, LANES)] = back.astype(BF16)
    copies[7].wait()
    for z in range(strips):
        at = z * 2 * HD
        part = dot(turned_ref[pl.ds(z * strip, strip), :], dproj_ref[...], ((1,), (0,)))
        part = part.astype(BF16)
        grad_ref[:, pl.ds(at, HD)] = part[:, :HD]
        grad_ref[:, pl.ds(at + HD, HD)] = part[:, LANES : LANES + HD]


def one_head(position, counts, order, weight, own, other, turned, tables, cotangents, patch_len):
    model_width, rows = turned.shape
    windows = rows // patch_len
    group = math.gcd(windows, max(1, 128 // patch_len))
    vmem = pl.BlockSpec(memory_space=pltpu.VMEM)
    smem = pl.BlockSpec(memory_space=pltpu.SMEM)
    return pl.pallas_call(
        functools.partial(head_kernel, patch_len, group, position),
        in_specs=[smem, smem] + [pl.BlockSpec(memory_space=pltpu.HBM)] * 8,
        out_specs=[vmem] * 2,
        out_shape=[
            jax.ShapeDtypeStruct((rows, LANES), BF16),
            jax.ShapeDtypeStruct(weight.shape, BF16),
        ],
        scratch_shapes=[
            pltpu.VMEM(weight.shape, BF16),
            pltpu.VMEM(own.shape, BF16),
            pltpu.VMEM(other.shape, BF16),
            pltpu.VMEM(turned.shape, BF16),
            pltpu.VMEM((rows, LANES), F32),
            pltpu.VMEM((rows, LANES), F32),
            pltpu.VMEM((rows, LANES), BF16),
            pltpu.VMEM((rows, LANES), BF16),
            pltpu.VMEM((model_width, 2 * LANES), BF16),
            pltpu.VMEM((rows, 2 * LANES), F32),
            pltpu.VMEM((rows, 2 * LANES), BF16),
            pltpu.SemaphoreType.DMA((8,)),
        ],
        compiler_params=pltpu.CompilerParams(vmem_limit_bytes=60 * 1024 * 1024),
        cost_estimate=pl.CostEstimate(
            flops=4_000_000_000, bytes_accessed=8_000_000, transcendentals=rows * 128
        ),
        name="one_head",
    )(counts, order, weight, own, other, turned, *tables, *cotangents)


def prepare_kernel(
    order,
    own_ref,
    other_ref,
    own_v_ref,
    other_v_ref,
    own_u_ref,
    other_u_ref,
    turned_ref,
    values_ref,
    upstream_ref,
):
    heads, rows = values_ref.shape[0], own_ref.shape[0]
    is_first = order[heads] == 0
    turned_ref[:, :rows] = jnp.transpose(own_ref[...])
    turned_ref[:, rows:] = jnp.transpose(other_ref[...])
    values_ref[...] = jnp.zeros_like(values_ref)
    upstream_ref[...] = jnp.zeros_like(upstream_ref)
    pairs = ((own_v_ref, other_v_ref, values_ref), (own_u_ref, other_u_ref, upstream_ref))
    for own, other, out in pairs:
        for at, source in ((0, own), (rows, other)):
            for head in range(heads):
                low = source[:, pl.ds(head * HD, HD)]
                high = source[:, pl.ds((heads + head) * HD, HD)]
                out[head, pl.ds(at, rows), pl.ds(0, HD)] = jnp.where(is_first, low, high)


def prepare(order, patches, values, upstream, heads):
    rows, model_width = patches[0].shape
    vmem = pl.BlockSpec(memory_space=pltpu.VMEM)
    smem = pl.BlockSpec(memory_space=pltpu.SMEM)
    spread_heads = jax.ShapeDtypeStruct((heads, 2 * rows, LANES), BF16)
    return pl.pallas_call(
        prepare_kernel,
        in_specs=[smem] + [vmem] * 6,
        out_specs=[vmem] * 3,
        out_shape=[
            jax.ShapeDtypeStruct((model_width, 2 * rows), BF16),
            spread_heads,
            spread_heads,
        ],
        compiler_params=pltpu.CompilerParams(vmem_limit_bytes=60 * 1024 * 1024),
        cost_estimate=pl.CostEstimate(flops=0, bytes_accessed=10_000_000, transcendentals=0),
        name="prepare",
    )(order, *patches, *values, *upstream)


def route_kernel(patch_len, dest, order, stack_ref, routed_ref):
    heads = stack_ref.shape[0]
    windows = stack_ref.shape[1] // patch_len // 2
    routed_ref[...] = jnp.zeros_like(routed_ref)
    for source in range(2):
        first = order[heads + source] * windows
        for window in range(windows):
            here = first + window
            rows = pl.ds(pl.multiple_of(here * patch_len, patch_len), patch_len)
            slot = dest[here]
            for head in range(heads):
                lanes = pl.ds((source * heads + head) * HD, HD)
                routed_ref[slot, :, lanes] = stack_ref[order[head], rows, :][:, :HD]


def route(dest, order, stack, slots, patch_len):
    heads = stack.shape[0]
    vmem = pl.BlockSpec(memory_space=pltpu.VMEM)
    smem = pl.BlockSpec(memory_space=pltpu.SMEM)
    return pl.pallas_call(
        functools.partial(route_kernel, patch_len),
        in_specs=[smem, smem, vmem],
        out_specs=vmem,
        out_shape=jax.ShapeDtypeStruct((slots, patch_len, 2 * heads * HD), BF16),
        compiler_params=pltpu.CompilerParams(vmem_limit_bytes=60 * 1024 * 1024),
        name="route",
    )(dest, order, stack)


def settle_kernel(arrived_ref, placed_ref):
    half = arrived_ref.shape[2] // 2
    for pair in range(0, arrived_ref.shape[0], 2):
        for source in range(2):
            lanes = pl.ds(source * half, half)
            for core in range(2):
                out = pl.ds(core * half, half)
                placed_ref[pair + source, :, out] = arrived_ref[pair + core, :, lanes]


def settle(arrived):
    vmem = pl.BlockSpec(memory_space=pltpu.VMEM)
    return pl.pallas_call(
        settle_kernel,
        in_specs=[vmem],
        out_specs=vmem,
        out_shape=jax.ShapeDtypeStruct(arrived.shape, BF16),
        compiler_params=pltpu.CompilerParams(vmem_limit_bytes=60 * 1024 * 1024),
        name="settle",
    )(arrived)


def rotary_tables(coords):
    quarter = HD // 4
    windows, _, patch_len = coords.shape
    lane = jnp.arange(LANES, dtype=jnp.int32)
    frequency = 10000.0 ** (-(lane % quarter).astype(F32) / quarter)
    position = coords.astype(F32)
    by_row = (lane < HD // 2)[None, None, :]
    position = jnp.where(by_row, position[:, 0, :, None], position[:, 1, :, None])
    angles = (position * frequency).reshape(windows * patch_len, LANES)
    used = (lane < HD)[None, :]
    return jnp.where(used, jnp.cos(angles), 0.0), jnp.where(used, jnp.sin(angles), 0.0)


def after(first, arrays):
    return lax.optimization_barrier((first, arrays))[1]


def per_device(patches, values, upstream, coords, counts, dest, weight):
    core, here = lax.axis_index("c"), lax.axis_index("x")
    nx, ny, nz = lax.axis_size("x"), lax.axis_size("y"), lax.axis_size("zh")
    slots = lax.axis_size(("zl", "x", "c"))
    window_count, patch_len, model_width = patches.shape
    value_width = values.shape[-1]
    row_total = window_count * patch_len
    depth = weight.shape[0]
    steps = [0, nx - 1, 1] + list(range(2, nx - 1))

    head = core * nx + here
    slice_q = lax.dynamic_slice_in_dim(weight, head * HD, HD, axis=1)
    slice_k = lax.dynamic_slice_in_dim(weight, value_width + head * HD, HD, axis=1)
    own_w = jnp.concatenate([slice_q, slice_k], axis=1)
    own_w = jnp.broadcast_to(own_w[None], (nz,) + own_w.shape)
    patches, values, upstream, coords, counts, dest = after(
        own_w, (patches, values, upstream, coords, counts, dest)
    )
    own_w = exchange(own_w, "zh")
    own_w = jnp.transpose(own_w, (1, 0, 2)).reshape(depth, nz * 2 * HD)
    own_w = spread(own_w, "y").reshape(ny * depth, nz * 2 * HD)

    patches = patches.reshape(row_total, model_width)
    values = values.reshape(row_total, value_width)
    upstream = upstream.reshape(row_total, value_width)
    other_patches = core_swap(patches)
    small = jnp.concatenate([coords.reshape(window_count, -1), counts[:, None], dest], axis=1)
    small = jnp.concatenate([small, core_swap(small)], axis=0)
    both_coords = small[:, : 2 * patch_len].reshape(2 * window_count, 2, patch_len)
    both_counts, both_dest = small[:, 2 * patch_len], small[:, 2 * patch_len + 1]
    tables = rotary_tables(both_coords)
    order = [lax.rem(here + step, nx) for step in steps]
    place = [jnp.int32(0)] * nx
    for at, head_at in enumerate(order):
        place = [jnp.where(head_at == h, at, place[h]) for h in range(nx)]
    place = jnp.stack(place + [core, 1 - core]).astype(jnp.int32)
    order = jnp.stack(order + [core]).astype(jnp.int32)
    turned, value_heads, upstream_heads = prepare(
        order,
        (patches, other_patches),
        (values, core_swap(values)),
        (upstream, core_swap(upstream)),
        nx,
    )

    own_w = after((turned, tables), own_w)
    weights = [own_w] + [ring_x(own_w, -step) for step in steps[1:]]
    contexts, grads = [], []
    for at, step in enumerate(steps):
        at_weight = weights[at]
        if at:
            at_weight = after((contexts[-1], grads[1 : at - 1]), at_weight)
        context, grad = one_head(
            at,
            both_counts,
            order,
            at_weight,
            patches,
            other_patches,
            turned,
            tables,
            (value_heads, upstream_heads),
            patch_len,
        )
        contexts.append(context)
        grads.append(ring_x(grad, step) if step else grad)

    stack = after(grads[:-1], jnp.stack(contexts))
    routed = route(both_dest, place, stack, slots, patch_len)
    arrived = exchange(routed, ("zl", "x", "c"))
    total = grads[0].astype(F32)
    for grad in grads[1:]:
        total = total + grad.astype(F32)
    total = after(arrived, total.astype(BF16))
    placed = settle(arrived)

    total = exchange(total.reshape(ny, depth, nz * 2 * HD), "y")
    total = jnp.sum(total.astype(F32), axis=0).astype(BF16)
    total = jnp.transpose(total.reshape(depth, nz, 2 * HD), (1, 0, 2))
    copies = lax.axis_size("zl")
    total = jnp.broadcast_to(total[None], (copies,) + total.shape)
    total = exchange(total.reshape(copies * nz, depth, 2 * HD), ("zl", "zh"))
    total = jnp.sum(total.astype(F32), axis=0).astype(BF16)
    total = spread(total, ("x", "c")).reshape(nx, 2, depth, 2, HD)
    grad_weight = jnp.transpose(total, (2, 3, 1, 0, 4)).reshape(depth, 2 * value_width)
    return (placed, grad_weight.astype(F32))


def solution(mesh):
    fine = Mesh(mesh.devices.reshape(SPLIT), AXES)
    return jax.shard_map(
        per_device,
        mesh=fine,
        in_specs=(
            P(AXES, None, None),
            P(AXES, None, None),
            P(AXES, None, None),
            P(AXES, None, None),
            P(AXES),
            P(AXES, None),
            P(("zh", "y"), None),
        ),
        out_specs=(P(AXES, None, None), P(("zh", "y"), None)),
        check_vma=False,
    )
```

```python
import functools
import math

import jax
import jax.numpy as jnp
from jax import lax
from jax.experimental import pallas as pl
from jax.experimental.pallas import tpu as pltpu
from jax.sharding import Mesh
from jax.sharding import PartitionSpec as P

HD = 80
LANES = 128
POSITIONS = 32
EXTRA = 16
SPLIT = (3, 4, 2, 4, 8)
AXES = ("zl", "x", "c", "zh", "y")
GROUP = ("x", "c")
PEERS = ("zl", "x", "c")
BF16 = jnp.bfloat16
F32 = jnp.float32
VMEM_BYTES = 60 * 1024 * 1024


def exchange(array, axes):
    return lax.all_to_all(array, axes, split_axis=0, concat_axis=0, tiled=True)


def spread(array, axes):
    count = lax.axis_size(axes)
    return exchange(jnp.broadcast_to(array[None], (count,) + array.shape), axes)


def after(first, arrays):
    return lax.optimization_barrier((first, arrays))[1]


def dot(a, b, dims):
    return lax.dot_general(a, b, (dims, ((), ())), preferred_element_type=F32)


def head_of(place, cores, heads):
    return place % cores * (heads // cores) + place // cores


def partner(array):
    quarter = HD // 4
    lane = lax.broadcasted_iota(jnp.int32, array.shape, 1)
    front = lax.rem(lane, 2 * quarter) < quarter
    ahead = pltpu.roll(array, LANES - quarter, 1)
    behind = pltpu.roll(array, quarter, 1)
    return jnp.where(front, -ahead, behind)


def pack_kernel(cores, values_ref, upstream_ref, notes_ref, packed_ref):
    heads, rows = packed_ref.shape[0], values_ref.shape[0]
    parts = packed_ref.shape[2] // (2 * HD)
    depth = rows // parts
    for place in range(heads):
        lanes = pl.ds(head_of(place, cores, heads) * HD, HD)
        for part in range(parts):
            span, at = pl.ds(part * depth, depth), part * 2 * HD
            packed_ref[place, :depth, pl.ds(at, HD)] = values_ref[span, lanes]
            packed_ref[place, :depth, pl.ds(at + HD, HD)] = upstream_ref[span, lanes]
        packed_ref[place, depth:, :] = notes_ref[...]


def pack(values, upstream, notes, heads, cores):
    rows, width = values.shape
    parts = width // (2 * HD)
    vmem = pl.BlockSpec(memory_space=pltpu.VMEM)
    return pl.pallas_call(
        functools.partial(pack_kernel, cores),
        in_specs=[vmem] * 3,
        out_specs=vmem,
        out_shape=jax.ShapeDtypeStruct((heads, rows // parts + EXTRA, width), BF16),
        compiler_params=pltpu.CompilerParams(vmem_limit_bytes=VMEM_BYTES),
        name="pack",
    )(values, upstream, notes)


def head_kernel(
    patch_len,
    group,
    weight_ref,
    table_ref,
    patches_ref,
    packed_ref,
    context_ref,
    grad_ref,
    full_ref,
    sum_ref,
    dproj_ref,
    values_ref,
    upstream_ref,
):
    step = pl.program_id(0)
    rows = patches_ref.shape[1]
    block = group * patch_len
    strip, strips = weight_ref.shape[0], weight_ref.shape[1] // (2 * HD)
    scale = 1.0 / math.sqrt(HD)

    @pl.when(step == 0)
    def _():
        full_ref[...] = jnp.zeros_like(full_ref)
        sum_ref[...] = jnp.zeros_like(sum_ref)
        values_ref[...] = jnp.zeros_like(values_ref)
        upstream_ref[...] = jnp.zeros_like(upstream_ref)
        for z in range(strips):
            span, at = pl.ds(z * strip, strip), z * 2 * HD
            full_ref[span, pl.ds(0, HD)] = weight_ref[:, pl.ds(at, HD)]
            full_ref[span, pl.ds(LANES, HD)] = weight_ref[:, pl.ds(at + HD, HD)]

    depth = packed_ref.shape[1] - EXTRA
    for part in range(rows // depth):
        span, at = pl.ds(part * depth, depth), part * 2 * HD
        values_ref[span, pl.ds(0, HD)] = packed_ref[0, :depth, pl.ds(at, HD)]
        upstream_ref[span, pl.ds(0, HD)] = packed_ref[0, :depth, pl.ds(at + HD, HD)]
    notes = packed_ref[0, depth:, :rows].astype(F32)
    live_keys = notes[2:3, :]
    kind = lax.broadcasted_iota(jnp.int32, (3 * POSITIONS, rows), 0)
    wanted = lax.rem(kind, POSITIONS).astype(F32)
    row_at, col_at = notes[0:1, :], notes[1:2, :]
    by_row = jnp.where(row_at == wanted, 1.0, 0.0)
    by_col = jnp.where(col_at == wanted, 1.0, 0.0)
    chosen = jnp.where(kind < POSITIONS, by_row, jnp.where(kind < 2 * POSITIONS, by_col, live_keys))
    chosen = chosen.astype(BF16)
    tables = dot(chosen, table_ref[0], ((0,), (0,)))
    tables += dot(chosen, table_ref[1], ((0,), (0,)))
    tables += dot(chosen, table_ref[2], ((0,), (0,)))

    proj = dot(patches_ref[0], full_ref[...], ((1,), (0,)))
    row_win = lax.broadcasted_iota(jnp.int32, (block, block), 0) // patch_len
    key_win = lax.broadcasted_iota(jnp.int32, (block, block), 1) // patch_len
    same = row_win == key_win
    starts = list(range(0, rows, block))
    each = range(len(starts))
    cosines = [tables[s : s + block, :LANES] for s in starts]
    sines = [tables[s : s + block, LANES:] for s in starts]
    masks = [same & (live_keys[:, s : s + block] > 0.5) for s in starts]
    lives = [cosine[:, HD : HD + 1] for cosine in cosines]
    q = [proj[s : s + block, :LANES] for s in starts]
    k = [proj[s : s + block, LANES:] for s in starts]
    q = [(q[i] * cosines[i] + partner(q[i]) * sines[i]).astype(BF16) for i in each]
    k = [(k[i] * cosines[i] + partner(k[i]) * sines[i]).astype(BF16) for i in each]
    scores = [dot(q[i], k[i], ((1,), (1,))) * scale for i in each]
    v = [values_ref[s : s + block, :] for s in starts]
    dprobs = [dot(upstream_ref[s : s + block, :], v[i], ((1,), (1,))) for i, s in enumerate(starts)]
    scores = [jnp.where(masks[i], scores[i], -1e30) for i in each]
    tops = [jnp.max(scores[i], axis=1, keepdims=True) for i in each]
    exps = [jnp.exp(scores[i] - tops[i]) for i in each]
    sums = [jnp.sum(exps[i], axis=1, keepdims=True) for i in each]
    probs = [exps[i] * (lives[i] / sums[i]) for i in each]
    context = [dot(probs[i].astype(BF16), v[i], ((1,), (0,))) for i in each]
    delta = [jnp.sum(probs[i] * dprobs[i], axis=1, keepdims=True) for i in each]
    dscores = [(probs[i] * (dprobs[i] - delta[i]) * scale).astype(BF16) for i in each]
    dquery = [dot(dscores[i], k[i], ((1,), (0,))) for i in each]
    dkey = [dot(dscores[i], q[i], ((0,), (0,))) for i in each]
    for i, s in enumerate(starts):
        span = pl.ds(s, block)
        context_ref[span, :] = context[i].astype(BF16)
        back = dquery[i] * cosines[i] - partner(dquery[i]) * sines[i]
        dproj_ref[span, pl.ds(0, LANES)] = back.astype(BF16)
        back = dkey[i] * cosines[i] - partner(dkey[i]) * sines[i]
        dproj_ref[span, pl.ds(LANES, LANES)] = back.astype(BF16)
    sum_ref[...] += dot(dproj_ref[...], patches_ref[0], ((0,), (0,)))

    @pl.when(step == pl.num_programs(0) - 1)
    def _():
        for z in range(strips):
            at = z * 2 * HD
            part = jnp.transpose(sum_ref[:, z * strip : (z + 1) * strip]).astype(BF16)
            grad_ref[:, pl.ds(at, HD)] = part[:, :HD]
            grad_ref[:, pl.ds(at + HD, HD)] = part[:, LANES : LANES + HD]


def one_head(weight, table, patches, packed, patch_len):
    sources, rows, model_width = patches.shape
    group = math.gcd(rows // patch_len, max(1, 128 // patch_len))
    return pl.pallas_call(
        functools.partial(head_kernel, patch_len, group),
        grid=(sources,),
        in_specs=[
            pl.BlockSpec(weight.shape, lambda s: (0, 0)),
            pl.BlockSpec(table.shape, lambda s: (0, 0, 0)),
            pl.BlockSpec((1, rows, model_width), lambda s: (s, 0, 0)),
            pl.BlockSpec((1,) + packed.shape[1:], lambda s: (s, 0, 0)),
        ],
        out_specs=[
            pl.BlockSpec((rows, LANES), lambda s: (s, 0)),
            pl.BlockSpec(weight.shape, lambda s: (0, 0)),
        ],
        out_shape=[
            jax.ShapeDtypeStruct((sources * rows, LANES), BF16),
            jax.ShapeDtypeStruct(weight.shape, BF16),
        ],
        scratch_shapes=[
            pltpu.VMEM((model_width, 2 * LANES), BF16),
            pltpu.VMEM((2 * LANES, model_width), F32),
            pltpu.VMEM((rows, 2 * LANES), BF16),
            pltpu.VMEM((rows, LANES), BF16),
            pltpu.VMEM((rows, LANES), BF16),
        ],
        compiler_params=pltpu.CompilerParams(vmem_limit_bytes=VMEM_BYTES),
        cost_estimate=pl.CostEstimate(
            flops=20_000_000_000, bytes_accessed=12_000_000, transcendentals=3_000_000
        ),
        name="one_head",
    )(weight, table, patches, packed)


def route_kernel(patch_len, dest, context_ref, routed_ref):
    routed_ref[...] = jnp.zeros_like(routed_ref)
    sources = routed_ref.shape[2] // HD
    windows = context_ref.shape[0] // patch_len // sources
    for source in range(sources):
        for window in range(windows):
            at = source * windows + window
            rows = context_ref[pl.ds(at * patch_len, patch_len), :]
            routed_ref[dest[at], :patch_len, pl.ds(source * HD, HD)] = rows[:, :HD]


def route(dest, context, slots, patch_len, chunk, sources):
    vmem = pl.BlockSpec(memory_space=pltpu.VMEM)
    return pl.pallas_call(
        functools.partial(route_kernel, patch_len),
        in_specs=[pl.BlockSpec(memory_space=pltpu.SMEM), vmem],
        out_specs=vmem,
        out_shape=jax.ShapeDtypeStruct((slots, patch_len + chunk, sources * HD), BF16),
        compiler_params=pltpu.CompilerParams(vmem_limit_bytes=VMEM_BYTES),
        name="route",
    )(dest, context)


def fold_kernel(parts_ref, folded_ref):
    total = parts_ref[0].astype(F32)
    for at in range(1, parts_ref.shape[0]):
        total += parts_ref[at].astype(F32)
    total = total.astype(BF16)
    depth, width = total.shape
    folded_ref[...] = jnp.zeros_like(folded_ref)
    chunk = folded_ref.shape[1]
    for at in range(0, depth, chunk):
        count = min(chunk, depth - at)
        lanes = pl.ds(at // chunk * width, width)
        folded_ref[:, :count, lanes] = jnp.broadcast_to(
            total[at : at + count][None], (folded_ref.shape[0], count, width)
        )


def fold(parts, slots, chunk, width):
    vmem = pl.BlockSpec(memory_space=pltpu.VMEM)
    return pl.pallas_call(
        fold_kernel,
        in_specs=[vmem],
        out_specs=vmem,
        out_shape=jax.ShapeDtypeStruct((slots, chunk, width), BF16),
        compiler_params=pltpu.CompilerParams(vmem_limit_bytes=VMEM_BYTES),
        name="fold",
    )(parts)


def settle_kernel(cores, patch_len, arrived_ref, placed_ref, grad_ref):
    heads = arrived_ref.shape[2] // HD
    copies = arrived_ref.shape[0] // heads
    depth, chunk = grad_ref.shape[0], arrived_ref.shape[1] - patch_len
    for place in range(heads):
        head = head_of(place, cores, heads)
        out = pl.ds(head * HD, HD)
        for copy in range(copies):
            for source in range(heads):
                rows = arrived_ref[copy * heads + place, :patch_len, pl.ds(source * HD, HD)]
                placed_ref[copy * heads + source, :, out] = rows
        total = arrived_ref[place, patch_len:, :].astype(F32)
        for copy in range(1, copies):
            total += arrived_ref[copy * heads + place, patch_len:, :].astype(F32)
        for at in range(0, depth, chunk):
            count = min(chunk, depth - at)
            lanes = at // chunk * 2 * HD
            span = pl.ds(at, count)
            grad_ref[span, out] = total[:count, lanes : lanes + HD]
            other = pl.ds((heads + head) * HD, HD)
            grad_ref[span, other] = total[:count, lanes + HD : lanes + 2 * HD]


def settle(arrived, patch_len, depth, cores):
    slots, _, width = arrived.shape
    vmem = pl.BlockSpec(memory_space=pltpu.VMEM)
    return pl.pallas_call(
        functools.partial(settle_kernel, cores, patch_len),
        in_specs=[vmem],
        out_specs=[vmem, vmem],
        out_shape=[
            jax.ShapeDtypeStruct((slots, patch_len, width), BF16),
            jax.ShapeDtypeStruct((depth, 2 * width), F32),
        ],
        compiler_params=pltpu.CompilerParams(vmem_limit_bytes=VMEM_BYTES),
        name="settle",
    )(arrived)


def rotary_table():
    quarter = HD // 4
    lane = jnp.arange(LANES, dtype=jnp.int32)[None, :]
    kind = jnp.arange(3 * POSITIONS, dtype=jnp.int32)[:, None]
    frequency = 10000.0 ** (-(lane % quarter).astype(F32) / quarter)
    angles = (kind % POSITIONS).astype(F32) * frequency
    by_row = (kind < POSITIONS) & (lane < HD // 2)
    by_col = (kind >= POSITIONS) & (kind < 2 * POSITIONS) & (lane >= HD // 2) & (lane < HD)
    used = by_row | by_col
    flag = (kind == 2 * POSITIONS) & (lane == HD)
    cosine = jnp.where(used, jnp.cos(angles), jnp.where(flag, 1.0, 0.0))
    left = jnp.concatenate([cosine, jnp.where(used, jnp.sin(angles), 0.0)], axis=1)
    terms = []
    for _ in range(3):
        term = lax.reduce_precision(left, 8, 7)
        terms.append(term.astype(BF16))
        left = left - term
    return jnp.stack(terms)


def per_device(patches, values, upstream, coords, counts, dest, weight):
    core, here = lax.axis_index("c"), lax.axis_index("x")
    nx, nc = lax.axis_size("x"), lax.axis_size("c")
    ny, nz = lax.axis_size("y"), lax.axis_size("zh")
    heads = nx * nc
    slots = lax.axis_size(PEERS)
    window_count, patch_len, model_width = patches.shape
    value_width = values.shape[-1]
    row_total = window_count * patch_len
    depth = weight.shape[0]
    chunk = -(-depth * 2 * HD // value_width)
    chunk = -(-chunk // EXTRA) * EXTRA

    gathered = lax.all_gather(patches.reshape(row_total, model_width), GROUP, axis=0)
    head = core * nx + here
    slice_q = lax.dynamic_slice_in_dim(weight, head * HD, HD, axis=1)
    slice_k = lax.dynamic_slice_in_dim(weight, value_width + head * HD, HD, axis=1)
    own_w = jnp.concatenate([slice_q, slice_k], axis=1)
    own_w = jnp.broadcast_to(own_w[None], (nz,) + own_w.shape)
    values, upstream, coords, counts, dest = after(
        own_w, (values, upstream, coords, counts, dest)
    )
    own_w = exchange(own_w, "zh")
    own_w = jnp.transpose(own_w, (1, 0, 2)).reshape(depth, nz * 2 * HD)
    own_w = spread(own_w, "y").reshape(ny * depth, nz * 2 * HD)

    live = jnp.arange(patch_len, dtype=jnp.int32)[None, :] < counts[:, None]
    notes = jnp.stack(
        [
            coords[:, 0, :].reshape(row_total),
            coords[:, 1, :].reshape(row_total),
            live.astype(jnp.int32).reshape(row_total),
            jnp.pad(dest[:, 0], (0, row_total - window_count)),
        ]
    )
    notes = jnp.pad(notes, ((0, EXTRA - 4), (0, value_width - row_total))).astype(BF16)
    values = values.reshape(row_total, value_width)
    upstream = upstream.reshape(row_total, value_width)
    packed = exchange(pack(values, upstream, notes, heads, nc), GROUP)
    all_dest = packed[:, packed.shape[1] - EXTRA + 3, :window_count]
    all_dest = all_dest.astype(jnp.int32).reshape(heads * window_count)

    context, grad = one_head(own_w, rotary_table(), gathered, packed, patch_len)
    routed = route(all_dest, context, slots, patch_len, chunk, heads)

    grad = exchange(grad.reshape(ny, depth, nz * 2 * HD), "y")
    grad = jnp.sum(grad.astype(F32), axis=0).astype(BF16)
    grad = jnp.transpose(grad.reshape(depth, nz, 2 * HD), (1, 0, 2))
    folded = fold(exchange(grad, "zh"), slots, chunk, value_width)
    routed = lax.dynamic_update_slice(routed, folded, (0, patch_len, 0))
    arrived = exchange(routed, PEERS)
    return tuple(settle(arrived, patch_len, depth, nc))


def solution(mesh):
    fine = Mesh(mesh.devices.reshape(SPLIT), AXES)
    return jax.shard_map(
        per_device,
        mesh=fine,
        in_specs=(
            P(AXES, None, None),
            P(AXES, None, None),
            P(AXES, None, None),
            P(AXES, None, None),
            P(AXES),
            P(AXES, None),
            P(("zh", "y"), None),
        ),
        out_specs=(P(AXES, None, None), P(("zh", "y"), None)),
        check_vma=False,
    )
```

```python
import functools
import math

import jax
import jax.numpy as jnp
from jax import lax
from jax.experimental import pallas as pl
from jax.experimental.pallas import tpu as pltpu
from jax.sharding import Mesh
from jax.sharding import PartitionSpec as P

HD = 80
LANES = 128
POSITIONS = 32
EXTRA = 16
SPLIT = (3, 4, 2, 4, 8)
AXES = ("zl", "x", "c", "zh", "y")
PEERS = ("zl", "x", "c")
BF16 = jnp.bfloat16
F32 = jnp.float32
VMEM_BYTES = 60 * 1024 * 1024


def core_swap(array):
    return lax.ppermute(array, "c", [(0, 1), (1, 0)])


def ring_x(array, step):
    count = lax.axis_size("x")
    if step == 0:
        return array
    return lax.ppermute(array, "x", [(i, (i + step) % count) for i in range(count)])


def exchange(array, axes):
    return lax.all_to_all(array, axes, split_axis=0, concat_axis=0, tiled=True)


def spread(array, axes):
    count = lax.axis_size(axes)
    return exchange(jnp.broadcast_to(array[None], (count,) + array.shape), axes)


def after(first, arrays):
    return lax.optimization_barrier((first, arrays))[1]


def dot(a, b, dims):
    return lax.dot_general(a, b, (dims, ((), ())), preferred_element_type=F32)


def head_of(place, cores, heads):
    return place % cores * (heads // cores) + place // cores


def partner(array):
    quarter = HD // 4
    lane = lax.broadcasted_iota(jnp.int32, array.shape, 1)
    front = lax.rem(lane, 2 * quarter) < quarter
    ahead = pltpu.roll(array, LANES - quarter, 1)
    behind = pltpu.roll(array, quarter, 1)
    return jnp.where(front, -ahead, behind)


def ring_steps(count):
    return [0, count - 1, 1] + list(range(2, count - 1))


def pack_kernel(where, values_ref, upstream_ref, notes_ref, *packed_refs):
    count = len(packed_refs)
    steps = ring_steps(count)
    rows, width = values_ref.shape
    parts = width // (2 * HD)
    depth = rows // parts
    kinds = width // HD // count
    for here in range(count):

        @pl.when(where[0] == here)
        def _():
            for packed_ref, step in zip(packed_refs, steps):
                for kind in range(kinds):
                    head = kind * count + (here + step) % count
                    lanes = pl.ds(head * HD, HD)
                    for part in range(parts):
                        span, at = pl.ds(part * depth, depth), part * 2 * HD
                        out = pl.ds(kind * depth, depth)
                        packed_ref[out, pl.ds(at, HD)] = values_ref[span, lanes]
                        packed_ref[out, pl.ds(at + HD, HD)] = upstream_ref[span, lanes]

    for packed_ref in packed_refs:
        packed_ref[kinds * depth :, :] = notes_ref[...]


def pack(where, values, upstream, notes, count):
    rows, width = values.shape
    parts = width // (2 * HD)
    kinds = width // HD // count
    vmem = pl.BlockSpec(memory_space=pltpu.VMEM)
    piece = jax.ShapeDtypeStruct((kinds * rows // parts + EXTRA, width), BF16)
    return pl.pallas_call(
        pack_kernel,
        in_specs=[pl.BlockSpec(memory_space=pltpu.SMEM)] + [vmem] * 3,
        out_specs=[vmem] * count,
        out_shape=[piece] * count,
        compiler_params=pltpu.CompilerParams(vmem_limit_bytes=VMEM_BYTES),
        name="pack",
    )(where, values, upstream, notes)


def heads_kernel(patch_len, group, sources, first, last, where, own_hbm, other_hbm, *refs):
    refs = list(refs)
    take = lambda count: [refs.pop(0) for _ in range(count)]
    table_hbm = take(1)[0]
    patches_hbm, packed_hbm = take(sources), take(sources)
    total_hbm = [] if first else take(1)
    context_refs = take(sources)
    results = take(2 if last else 1)
    own_ref, other_ref, table_ref = take(3)
    patches_refs, packed_refs = take(sources), take(sources)
    full_ref, sum_ref, dproj_ref, values_ref, upstream_ref, arrivals = take(6)
    moves = [(own_hbm, own_ref), (other_hbm, other_ref), (table_hbm, table_ref)]
    for at in range(sources):
        moves.append((patches_hbm[at], patches_refs[at]))
        moves.append((packed_hbm[at], packed_refs[at]))
    if not first:
        moves.append((total_hbm[0], sum_ref))
    copies = [
        pltpu.make_async_copy(source, target, arrivals.at[at])
        for at, (source, target) in enumerate(moves)
    ]
    for copy in copies:
        copy.start()
    strip, strips = own_ref.shape[0], own_ref.shape[1] // (2 * HD)
    rows = patches_refs[0].shape[0]
    block = group * patch_len
    scale = 1.0 / math.sqrt(HD)
    full_ref[...] = jnp.zeros_like(full_ref)
    values_ref[...] = jnp.zeros_like(values_ref)
    upstream_ref[...] = jnp.zeros_like(upstream_ref)
    is_first = where[1] == 0
    copies[0].wait()
    copies[1].wait()
    for z in range(strips):
        span = pl.ds(z * strip, strip)
        for part in range(2):
            lanes = pl.ds((2 * z + part) * HD, HD)
            own, other = own_ref[:, lanes], other_ref[:, lanes]
            full_ref[span, pl.ds(part * LANES, HD)] = jnp.where(is_first, own, other)
            full_ref[span, pl.ds((2 + part) * LANES, HD)] = jnp.where(is_first, other, own)
    copies[2].wait()
    row_win = lax.broadcasted_iota(jnp.int32, (block, block), 0) // patch_len
    key_win = lax.broadcasted_iota(jnp.int32, (block, block), 1) // patch_len
    same = row_win == key_win
    kind = lax.broadcasted_iota(jnp.int32, (3 * POSITIONS, rows), 0)
    wanted = lax.rem(kind, POSITIONS).astype(F32)
    starts = [at for at in range(0, rows, block)]
    chains = [(head, at) for head in range(2) for at in range(len(starts))]
    each = range(len(chains))
    for source in range(sources):
        patches_ref, packed_ref = patches_refs[source], packed_refs[source]
        copies[3 + 2 * source].wait()
        proj = dot(patches_ref[...], full_ref[...], ((1,), (0,)))
        copies[4 + 2 * source].wait()
        depth = (packed_ref.shape[0] - EXTRA) // 2
        notes = packed_ref[2 * depth :, :rows].astype(F32)
        live_keys = notes[2:3, :]
        by_row = jnp.where(notes[0:1, :] == wanted, 1.0, 0.0)
        by_col = jnp.where(notes[1:2, :] == wanted, 1.0, 0.0)
        chosen = jnp.where(kind < 2 * POSITIONS, by_col, live_keys)
        chosen = jnp.where(kind < POSITIONS, by_row, chosen).astype(BF16)
        tables = dot(chosen, table_ref[0], ((0,), (0,)))
        tables += dot(chosen, table_ref[1], ((0,), (0,)))
        tables += dot(chosen, table_ref[2], ((0,), (0,)))
        for head in range(2):
            out, come = pl.ds(head * LANES, HD), pl.ds(head * depth, depth)
            for part in range(rows // depth):
                span, at = pl.ds(part * depth, depth), part * 2 * HD
                values_ref[span, out] = packed_ref[come, pl.ds(at, HD)]
                upstream_ref[span, out] = packed_ref[come, pl.ds(at + HD, HD)]
        cosines = [tables[s : s + block, :LANES] for s in starts]
        sines = [tables[s : s + block, LANES:] for s in starts]
        masks = [same & (live_keys[:, s : s + block] > 0.5) for s in starts]
        lives = [cosine[:, HD : HD + 1] for cosine in cosines]
        spans = [pl.ds(starts[at], block) for _, at in chains]
        lanes = [pl.ds(head * LANES, LANES) for head, _ in chains]
        blocks = [at for _, at in chains]
        q = [proj[starts[at] : starts[at] + block, 2 * h * LANES :][:, :LANES] for h, at in chains]
        k = [
            proj[starts[at] : starts[at] + block, (2 * h + 1) * LANES :][:, :LANES]
            for h, at in chains
        ]
        turn = lambda x, at: x * cosines[at] + partner(x) * sines[at]
        q = [turn(q[i], blocks[i]).astype(BF16) for i in each]
        k = [turn(k[i], blocks[i]).astype(BF16) for i in each]
        scores = [dot(q[i], k[i], ((1,), (1,))) * scale for i in each]
        v = [values_ref[spans[i], lanes[i]] for i in each]
        dprobs = [dot(upstream_ref[spans[i], lanes[i]], v[i], ((1,), (1,))) for i in each]
        scores = [jnp.where(masks[blocks[i]], scores[i], -1e30) for i in each]
        tops = [jnp.max(scores[i], axis=1, keepdims=True) for i in each]
        exps = [jnp.exp(scores[i] - tops[i]) for i in each]
        sums = [jnp.sum(exps[i], axis=1, keepdims=True) for i in each]
        probs = [exps[i] * (lives[blocks[i]] / sums[i]) for i in each]
        context = [dot(probs[i].astype(BF16), v[i], ((1,), (0,))) for i in each]
        delta = [jnp.sum(probs[i] * dprobs[i], axis=1, keepdims=True) for i in each]
        dscores = [(probs[i] * (dprobs[i] - delta[i]) * scale).astype(BF16) for i in each]
        dquery = [dot(dscores[i], k[i], ((1,), (0,))) for i in each]
        dkey = [dot(dscores[i], q[i], ((0,), (0,))) for i in each]
        back = lambda x, at: (x * cosines[at] - partner(x) * sines[at]).astype(BF16)
        for i in each:
            context_refs[source][spans[i], lanes[i]] = context[i].astype(BF16)
            at = 2 * chains[i][0] * LANES
            dproj_ref[spans[i], pl.ds(at, LANES)] = back(dquery[i], blocks[i])
            dproj_ref[spans[i], pl.ds(at + LANES, LANES)] = back(dkey[i], blocks[i])
        grown = dot(dproj_ref[...], patches_ref[...], ((0,), (0,)))
        if first and source == 0:
            sum_ref[...] = grown
        else:
            if source == 0:
                copies[-1].wait()
            sum_ref[...] += grown
    if not last:
        results[0][...] = sum_ref[...]
        return
    for z in range(strips):
        part = jnp.transpose(sum_ref[:, z * strip : (z + 1) * strip]).astype(BF16)
        for at in range(2):
            low = part[:, at * LANES : at * LANES + HD]
            high = part[:, (2 + at) * LANES : (2 + at) * LANES + HD]
            lanes = pl.ds((2 * z + at) * HD, HD)
            results[0][:, lanes] = jnp.where(is_first, low, high)
            results[1][:, lanes] = jnp.where(is_first, high, low)


def some_heads(where, weights, table, patches, packed, total, last, patch_len):
    sources = len(patches)
    rows, model_width = patches[0].shape
    group = math.gcd(rows // patch_len, max(1, 128 // patch_len))
    vmem = pl.BlockSpec(memory_space=pltpu.VMEM)
    hbm = pl.BlockSpec(memory_space=pltpu.HBM)
    carried = [] if total is None else [total]
    sum_shape = jax.ShapeDtypeStruct((4 * LANES, model_width), F32)
    grad_shape = jax.ShapeDtypeStruct(weights[0].shape, BF16)
    results = [grad_shape] * 2 if last else [sum_shape]
    moves = 3 + 2 * sources + len(carried)
    return pl.pallas_call(
        functools.partial(heads_kernel, patch_len, group, sources, total is None, last),
        in_specs=[pl.BlockSpec(memory_space=pltpu.SMEM)] + [hbm] * moves,
        out_specs=[vmem] * (sources + len(results)),
        out_shape=[jax.ShapeDtypeStruct((rows, 2 * LANES), BF16)] * sources + results,
        scratch_shapes=[pltpu.VMEM(weights[0].shape, BF16)] * 2
        + [pltpu.VMEM(table.shape, BF16)]
        + [pltpu.VMEM(patches[0].shape, BF16)] * sources
        + [pltpu.VMEM(packed[0].shape, BF16)] * sources
        + [
            pltpu.VMEM((model_width, 4 * LANES), BF16),
            pltpu.VMEM(sum_shape.shape, F32),
            pltpu.VMEM((rows, 4 * LANES), BF16),
            pltpu.VMEM((rows, 2 * LANES), BF16),
            pltpu.VMEM((rows, 2 * LANES), BF16),
            pltpu.SemaphoreType.DMA((moves,)),
        ],
        compiler_params=pltpu.CompilerParams(vmem_limit_bytes=VMEM_BYTES),
        cost_estimate=pl.CostEstimate(
            flops=5_000_000_000 * sources,
            bytes_accessed=3_000_000 * sources,
            transcendentals=800_000 * sources,
        ),
        name="heads",
    )(where, *weights, table, *patches, *packed, *carried)


def route_kernel(patch_len, dest, *refs):
    context_refs, routed_ref = refs[:-1], refs[-1]
    routed_ref[...] = jnp.zeros_like(routed_ref)
    windows = context_refs[0].shape[0] // patch_len
    for source, context_ref in enumerate(context_refs):
        for window in range(windows):
            slot = dest[source * windows + window]
            rows = context_ref[pl.ds(window * patch_len, patch_len), :]
            for head in range(2):
                lanes = pl.ds((2 * source + head) * HD, HD)
                routed_ref[slot, :patch_len, lanes] = rows[:, head * LANES : head * LANES + HD]


def route(dest, contexts, slots, patch_len, chunk):
    vmem = pl.BlockSpec(memory_space=pltpu.VMEM)
    width = 2 * HD * len(contexts)
    return pl.pallas_call(
        functools.partial(route_kernel, patch_len),
        in_specs=[pl.BlockSpec(memory_space=pltpu.SMEM)] + [vmem] * len(contexts),
        out_specs=vmem,
        out_shape=jax.ShapeDtypeStruct((slots, patch_len + chunk, width), BF16),
        compiler_params=pltpu.CompilerParams(vmem_limit_bytes=VMEM_BYTES),
        name="route",
    )(dest, *contexts)


def fold_kernel(parts_ref, folded_ref):
    total = parts_ref[0].astype(F32)
    for at in range(1, parts_ref.shape[0]):
        total += parts_ref[at].astype(F32)
    total = total.astype(BF16)
    depth, width = total.shape
    folded_ref[...] = jnp.zeros_like(folded_ref)
    chunk = folded_ref.shape[1]
    for at in range(0, depth, chunk):
        count = min(chunk, depth - at)
        lanes = pl.ds(at // chunk * width, width)
        folded_ref[:, :count, lanes] = jnp.broadcast_to(
            total[at : at + count][None], (folded_ref.shape[0], count, width)
        )


def fold(parts, slots, chunk, width):
    vmem = pl.BlockSpec(memory_space=pltpu.VMEM)
    return pl.pallas_call(
        fold_kernel,
        in_specs=[vmem],
        out_specs=vmem,
        out_shape=jax.ShapeDtypeStruct((slots, chunk, width), BF16),
        compiler_params=pltpu.CompilerParams(vmem_limit_bytes=VMEM_BYTES),
        name="fold",
    )(parts)


def settle_kernel(cores, patch_len, arrived_ref, placed_ref, grad_ref):
    heads = arrived_ref.shape[2] // HD
    copies = arrived_ref.shape[0] // heads
    depth, chunk = grad_ref.shape[0], arrived_ref.shape[1] - patch_len
    for place in range(heads):
        head = head_of(place, cores, heads)
        out = pl.ds(head * HD, HD)
        count = heads // cores
        here, core = place // cores, place % cores
        for copy in range(copies):
            for at, step in enumerate(ring_steps(count)):
                source = copy * heads + (here - step) % count * cores + core
                for kind in range(cores):
                    lanes = pl.ds((cores * at + kind) * HD, HD)
                    rows = arrived_ref[copy * heads + place, :patch_len, lanes]
                    placed_ref[source, :, pl.ds((kind * count + here) * HD, HD)] = rows
        total = arrived_ref[place, patch_len:, :].astype(F32)
        for copy in range(1, copies):
            total += arrived_ref[copy * heads + place, patch_len:, :].astype(F32)
        for at in range(0, depth, chunk):
            count = min(chunk, depth - at)
            lanes = at // chunk * 2 * HD
            span = pl.ds(at, count)
            grad_ref[span, out] = total[:count, lanes : lanes + HD]
            other = pl.ds((heads + head) * HD, HD)
            grad_ref[span, other] = total[:count, lanes + HD : lanes + 2 * HD]


def settle(arrived, patch_len, depth, cores):
    slots, _, width = arrived.shape
    vmem = pl.BlockSpec(memory_space=pltpu.VMEM)
    return pl.pallas_call(
        functools.partial(settle_kernel, cores, patch_len),
        in_specs=[vmem],
        out_specs=[vmem, vmem],
        out_shape=[
            jax.ShapeDtypeStruct((slots, patch_len, width), BF16),
            jax.ShapeDtypeStruct((depth, 2 * width), F32),
        ],
        compiler_params=pltpu.CompilerParams(vmem_limit_bytes=VMEM_BYTES),
        name="settle",
    )(arrived)


def rotary_table():
    quarter = HD // 4
    lane = jnp.arange(LANES, dtype=jnp.int32)[None, :]
    kind = jnp.arange(3 * POSITIONS, dtype=jnp.int32)[:, None]
    frequency = 10000.0 ** (-(lane % quarter).astype(F32) / quarter)
    angles = (kind % POSITIONS).astype(F32) * frequency
    by_row = (kind < POSITIONS) & (lane < HD // 2)
    by_col = (kind >= POSITIONS) & (kind < 2 * POSITIONS) & (lane >= HD // 2) & (lane < HD)
    used = by_row | by_col
    flag = (kind == 2 * POSITIONS) & (lane == HD)
    cosine = jnp.where(used, jnp.cos(angles), jnp.where(flag, 1.0, 0.0))
    left = jnp.concatenate([cosine, jnp.where(used, jnp.sin(angles), 0.0)], axis=1)
    terms = []
    for _ in range(3):
        term = lax.reduce_precision(left, 8, 7)
        terms.append(term.astype(BF16))
        left = left - term
    return jnp.stack(terms)


def per_device(patches, values, upstream, coords, counts, dest, weight):
    core, here = lax.axis_index("c"), lax.axis_index("x")
    nx, nc = lax.axis_size("x"), lax.axis_size("c")
    ny, nz = lax.axis_size("y"), lax.axis_size("zh")
    heads = nx * nc
    slots = lax.axis_size(PEERS)
    window_count, patch_len, model_width = patches.shape
    value_width = values.shape[-1]
    row_total = window_count * patch_len
    depth = weight.shape[0]
    chunk = -(-depth * 2 * HD // value_width)
    chunk = -(-chunk // EXTRA) * EXTRA

    head = core * nx + here
    slice_q = lax.dynamic_slice_in_dim(weight, head * HD, HD, axis=1)
    slice_k = lax.dynamic_slice_in_dim(weight, value_width + head * HD, HD, axis=1)
    own_w = jnp.concatenate([slice_q, slice_k], axis=1)
    own_w = jnp.broadcast_to(own_w[None], (nz,) + own_w.shape)
    patches, values, upstream, coords, counts, dest = after(
        own_w, (patches, values, upstream, coords, counts, dest)
    )
    own_w = exchange(own_w, "zh")
    own_w = jnp.transpose(own_w, (1, 0, 2)).reshape(depth, nz * 2 * HD)
    own_w = spread(own_w, "y").reshape(ny * depth, nz * 2 * HD)

    live = jnp.arange(patch_len, dtype=jnp.int32)[None, :] < counts[:, None]
    notes = jnp.stack(
        [
            coords[:, 0, :].reshape(row_total),
            coords[:, 1, :].reshape(row_total),
            live.astype(jnp.int32).reshape(row_total),
            jnp.pad(dest[:, 0], (0, row_total - window_count)),
        ]
    )
    notes = jnp.pad(notes, ((0, EXTRA - 4), (0, value_width - row_total))).astype(BF16)
    values = values.reshape(row_total, value_width)
    upstream = upstream.reshape(row_total, value_width)
    steps = ring_steps(nx)
    where = jnp.stack([here, core]).astype(jnp.int32)
    patches = patches.reshape(row_total, model_width)
    all_patches = [ring_x(patches, step) for step in steps]
    packed = pack(where, values, upstream, notes, nx)
    packed = [ring_x(piece, step) for piece, step in zip(packed, steps)]
    note_at = packed[0].shape[0] - EXTRA + 3
    all_dest = jnp.concatenate([piece[note_at, :window_count] for piece in packed])
    all_dest = all_dest.astype(jnp.int32)

    weights = (own_w, core_swap(own_w))
    table = rotary_table()
    early = len(steps) - 1
    *contexts, total = some_heads(
        where, weights, table, all_patches[:early], packed[:early], None, False, patch_len
    )
    context, grad, sent = some_heads(
        where, weights, table, all_patches[early:], packed[early:], total, True, patch_len
    )
    routed = route(all_dest, contexts + [context], slots, patch_len, chunk)

    grad = (grad.astype(F32) + core_swap(sent).astype(F32)).astype(BF16)
    grad = exchange(grad.reshape(ny, depth, nz * 2 * HD), "y")
    grad = jnp.sum(grad.astype(F32), axis=0).astype(BF16)
    grad = jnp.transpose(grad.reshape(depth, nz, 2 * HD), (1, 0, 2))
    folded = fold(exchange(grad, "zh"), slots, chunk, value_width)
    routed = lax.dynamic_update_slice(routed, folded, (0, patch_len, 0))
    arrived = exchange(routed, PEERS)
    return tuple(settle(arrived, patch_len, depth, nc))


def solution(mesh):
    fine = Mesh(mesh.devices.reshape(SPLIT), AXES)
    return jax.shard_map(
        per_device,
        mesh=fine,
        in_specs=(
            P(AXES, None, None),
            P(AXES, None, None),
            P(AXES, None, None),
            P(AXES, None, None),
            P(AXES),
            P(AXES, None),
            P(("zh", "y"), None),
        ),
        out_specs=(P(AXES, None, None), P(("zh", "y"), None)),
        check_vma=False,
    )
```

```python
import functools
import math

import jax
import jax.numpy as jnp
from jax import lax
from jax.experimental import pallas as pl
from jax.experimental.pallas import tpu as pltpu
from jax.sharding import Mesh
from jax.sharding import PartitionSpec as P

HD = 80
LANES = 128
POSITIONS = 32
EXTRA = 16
SPLIT = (3, 4, 2, 4, 8)
AXES = ("zl", "x", "c", "zh", "y")
PEERS = ("zl", "x", "c")
BF16 = jnp.bfloat16
F32 = jnp.float32
VMEM_BYTES = 60 * 1024 * 1024


def core_swap(array):
    return lax.ppermute(array, "c", [(0, 1), (1, 0)])


def ring(array, axis, step):
    count = lax.axis_size(axis)
    if step == 0:
        return array
    return lax.ppermute(array, axis, [(i, (i + step) % count) for i in range(count)])


def exchange(array, axes):
    return lax.all_to_all(array, axes, split_axis=0, concat_axis=0, tiled=True)


def spread(array, axes):
    count = lax.axis_size(axes)
    return exchange(jnp.broadcast_to(array[None], (count,) + array.shape), axes)


def after(first, arrays):
    return lax.optimization_barrier((first, arrays))[1]


def dot(a, b, dims):
    return lax.dot_general(a, b, (dims, ((), ())), preferred_element_type=F32)


def head_of(place, cores, heads):
    return place % cores * (heads // cores) + place // cores


def partner(array):
    quarter = HD // 4
    lane = lax.broadcasted_iota(jnp.int32, array.shape, 1)
    front = lax.rem(lane, 2 * quarter) < quarter
    ahead = pltpu.roll(array, LANES - quarter, 1)
    behind = pltpu.roll(array, quarter, 1)
    return jnp.where(front, -ahead, behind)


def ring_steps(count):
    return [0, count - 1, 1] + list(range(2, count - 1))


def pack_kernel(where, values_ref, upstream_ref, notes_ref, *packed_refs):
    count = len(packed_refs)
    steps = ring_steps(count)
    rows, width = values_ref.shape
    parts = width // (2 * HD)
    depth = rows // parts
    kinds = width // HD // count
    for here in range(count):

        @pl.when(where[0] == here)
        def _():
            for packed_ref, step in zip(packed_refs, steps):
                for kind in range(kinds):
                    head = kind * count + (here + step) % count
                    lanes = pl.ds(head * HD, HD)
                    for part in range(parts):
                        span, at = pl.ds(part * depth, depth), part * 2 * HD
                        out = pl.ds(kind * depth, depth)
                        packed_ref[out, pl.ds(at, HD)] = values_ref[span, lanes]
                        packed_ref[out, pl.ds(at + HD, HD)] = upstream_ref[span, lanes]

    for packed_ref in packed_refs:
        packed_ref[kinds * depth :, :] = notes_ref[...]


def pack(where, values, upstream, notes, count):
    rows, width = values.shape
    parts = width // (2 * HD)
    kinds = width // HD // count
    vmem = pl.BlockSpec(memory_space=pltpu.VMEM)
    piece = jax.ShapeDtypeStruct((kinds * rows // parts + EXTRA, width), BF16)
    return pl.pallas_call(
        pack_kernel,
        in_specs=[pl.BlockSpec(memory_space=pltpu.SMEM)] + [vmem] * 3,
        out_specs=[vmem] * count,
        out_shape=[piece] * count,
        compiler_params=pltpu.CompilerParams(vmem_limit_bytes=VMEM_BYTES),
        name="pack",
    )(where, values, upstream, notes)


def heads_kernel(patch_len, group, sources, first, last, where, own_hbm, other_hbm, *refs):
    refs = list(refs)
    take = lambda count: [refs.pop(0) for _ in range(count)]
    table_hbm = take(1)[0]
    patches_hbm, packed_hbm = take(sources), take(sources)
    total_hbm = [] if first else take(1)
    context_refs = take(sources)
    results = take(2 if last else 1)
    own_ref, other_ref, table_ref = take(3)
    whole_ref, packed_refs = take(1)[0], take(sources)
    rows = whole_ref.shape[0] // sources
    patches_refs = [whole_ref.at[pl.ds(at * rows, rows), :] for at in range(sources)]
    full_ref, sum_ref, dproj_ref, values_ref, upstream_ref, arrivals = take(6)
    moves = [(own_hbm, own_ref), (other_hbm, other_ref), (table_hbm, table_ref)]
    for at in range(sources):
        moves.append((patches_hbm[at], patches_refs[at]))
        moves.append((packed_hbm[at], packed_refs[at]))
    if not first:
        moves.append((total_hbm[0], sum_ref))
    copies = [
        pltpu.make_async_copy(source, target, arrivals.at[at])
        for at, (source, target) in enumerate(moves)
    ]
    for copy in copies:
        copy.start()
    strip, strips = own_ref.shape[0], own_ref.shape[1] // (2 * HD)
    block = group * patch_len
    scale = 1.0 / math.sqrt(HD)
    full_ref[...] = jnp.zeros_like(full_ref)
    values_ref[...] = jnp.zeros_like(values_ref)
    upstream_ref[...] = jnp.zeros_like(upstream_ref)
    is_first = where[1] == 0
    copies[0].wait()
    copies[1].wait()
    for z in range(strips):
        span = pl.ds(z * strip, strip)
        for part in range(2):
            lanes = pl.ds((2 * z + part) * HD, HD)
            own, other = own_ref[:, lanes], other_ref[:, lanes]
            full_ref[span, pl.ds(part * LANES, HD)] = jnp.where(is_first, own, other)
            full_ref[span, pl.ds((2 + part) * LANES, HD)] = jnp.where(is_first, other, own)
    copies[2].wait()
    row_win = lax.broadcasted_iota(jnp.int32, (block, block), 0) // patch_len
    key_win = lax.broadcasted_iota(jnp.int32, (block, block), 1) // patch_len
    same = row_win == key_win
    kind = lax.broadcasted_iota(jnp.int32, (3 * POSITIONS, rows), 0)
    wanted = lax.rem(kind, POSITIONS).astype(F32)
    starts = [at for at in range(0, rows, block)]
    chains = [(head, at) for head in range(2) for at in range(len(starts))]
    each = range(len(chains))
    for source in range(sources):
        patches_ref, packed_ref = patches_refs[source], packed_refs[source]
        copies[3 + 2 * source].wait()
        proj = dot(patches_ref[...], full_ref[...], ((1,), (0,)))
        copies[4 + 2 * source].wait()
        depth = (packed_ref.shape[0] - EXTRA) // 2
        notes = packed_ref[2 * depth :, :rows].astype(F32)
        live_keys = notes[2:3, :]
        by_row = jnp.where(notes[0:1, :] == wanted, 1.0, 0.0)
        by_col = jnp.where(notes[1:2, :] == wanted, 1.0, 0.0)
        chosen = jnp.where(kind < 2 * POSITIONS, by_col, live_keys)
        chosen = jnp.where(kind < POSITIONS, by_row, chosen).astype(BF16)
        tables = dot(chosen, table_ref[0], ((0,), (0,)))
        tables += dot(chosen, table_ref[1], ((0,), (0,)))
        tables += dot(chosen, table_ref[2], ((0,), (0,)))
        for head in range(2):
            out, come = pl.ds(head * LANES, HD), pl.ds(head * depth, depth)
            for part in range(rows // depth):
                span, at = pl.ds(part * depth, depth), part * 2 * HD
                values_ref[span, out] = packed_ref[come, pl.ds(at, HD)]
                upstream_ref[span, out] = packed_ref[come, pl.ds(at + HD, HD)]
        cosines = [tables[s : s + block, :LANES] for s in starts]
        sines = [tables[s : s + block, LANES:] for s in starts]
        masks = [same & (live_keys[:, s : s + block] > 0.5) for s in starts]
        lives = [cosine[:, HD : HD + 1] for cosine in cosines]
        spans = [pl.ds(starts[at], block) for _, at in chains]
        lanes = [pl.ds(head * LANES, LANES) for head, _ in chains]
        blocks = [at for _, at in chains]
        q = [proj[starts[at] : starts[at] + block, 2 * h * LANES :][:, :LANES] for h, at in chains]
        k = [
            proj[starts[at] : starts[at] + block, (2 * h + 1) * LANES :][:, :LANES]
            for h, at in chains
        ]
        turn = lambda x, at: x * cosines[at] + partner(x) * sines[at]
        q = [turn(q[i], blocks[i]).astype(BF16) for i in each]
        k = [turn(k[i], blocks[i]).astype(BF16) for i in each]
        scores = [dot(q[i], k[i], ((1,), (1,))) * scale for i in each]
        v = [values_ref[spans[i], lanes[i]] for i in each]
        dprobs = [dot(upstream_ref[spans[i], lanes[i]], v[i], ((1,), (1,))) for i in each]
        scores = [jnp.where(masks[blocks[i]], scores[i], -1e30) for i in each]
        tops = [jnp.max(scores[i], axis=1, keepdims=True) for i in each]
        exps = [jnp.exp(scores[i] - tops[i]) for i in each]
        sums = [jnp.sum(exps[i], axis=1, keepdims=True) for i in each]
        probs = [exps[i] * (lives[blocks[i]] / sums[i]) for i in each]
        context = [dot(probs[i].astype(BF16), v[i], ((1,), (0,))) for i in each]
        delta = [jnp.sum(probs[i] * dprobs[i], axis=1, keepdims=True) for i in each]
        dscores = [(probs[i] * (dprobs[i] - delta[i]) * scale).astype(BF16) for i in each]
        dquery = [dot(dscores[i], k[i], ((1,), (0,))) for i in each]
        dkey = [dot(dscores[i], q[i], ((0,), (0,))) for i in each]
        back = lambda x, at: (x * cosines[at] - partner(x) * sines[at]).astype(BF16)
        for i in each:
            context_refs[source][spans[i], lanes[i]] = context[i].astype(BF16)
            at = 2 * chains[i][0] * LANES
            here = pl.ds(source * rows + starts[blocks[i]], block)
            dproj_ref[here, pl.ds(at, LANES)] = back(dquery[i], blocks[i])
            dproj_ref[here, pl.ds(at + LANES, LANES)] = back(dkey[i], blocks[i])
    sum_ref[...] = dot(dproj_ref[...], whole_ref[...], ((0,), (0,)))
    if not first:
        copies[-1].wait()
    if not last:
        results[0][...] = sum_ref[...]
        return
    for z in range(strips):
        part = jnp.transpose(sum_ref[:, z * strip : (z + 1) * strip]).astype(BF16)
        for at in range(2):
            low = part[:, at * LANES : at * LANES + HD]
            high = part[:, (2 + at) * LANES : (2 + at) * LANES + HD]
            lanes = pl.ds((2 * z + at) * HD, HD)
            results[0][:, lanes] = jnp.where(is_first, low, high)
            results[1][:, lanes] = jnp.where(is_first, high, low)


def some_heads(where, weights, table, patches, packed, total, last, patch_len):
    sources = len(patches)
    rows, model_width = patches[0].shape
    group = math.gcd(rows // patch_len, max(1, 128 // patch_len))
    vmem = pl.BlockSpec(memory_space=pltpu.VMEM)
    hbm = pl.BlockSpec(memory_space=pltpu.HBM)
    carried = [] if total is None else [total]
    sum_shape = jax.ShapeDtypeStruct((4 * LANES, model_width), F32)
    grad_shape = jax.ShapeDtypeStruct(weights[0].shape, BF16)
    results = [grad_shape] * 2 if last else [sum_shape]
    moves = 3 + 2 * sources + len(carried)
    return pl.pallas_call(
        functools.partial(heads_kernel, patch_len, group, sources, total is None, last),
        in_specs=[pl.BlockSpec(memory_space=pltpu.SMEM)] + [hbm] * moves,
        out_specs=[vmem] * (sources + len(results)),
        out_shape=[jax.ShapeDtypeStruct((rows, 2 * LANES), BF16)] * sources + results,
        scratch_shapes=[pltpu.VMEM(weights[0].shape, BF16)] * 2
        + [pltpu.VMEM(table.shape, BF16)]
        + [pltpu.VMEM((sources * rows, model_width), BF16)]
        + [pltpu.VMEM(packed[0].shape, BF16)] * sources
        + [
            pltpu.VMEM((model_width, 4 * LANES), BF16),
            pltpu.VMEM(sum_shape.shape, F32),
            pltpu.VMEM((sources * rows, 4 * LANES), BF16),
            pltpu.VMEM((rows, 2 * LANES), BF16),
            pltpu.VMEM((rows, 2 * LANES), BF16),
            pltpu.SemaphoreType.DMA((moves,)),
        ],
        compiler_params=pltpu.CompilerParams(vmem_limit_bytes=VMEM_BYTES),
        cost_estimate=pl.CostEstimate(
            flops=5_000_000_000 * sources,
            bytes_accessed=3_000_000 * sources,
            transcendentals=800_000 * sources,
        ),
        name="heads",
    )(where, *weights, table, *patches, *packed, *carried)


def route_kernel(patch_len, slot_of, *refs):
    context_refs, routed_ref = refs[:-1], refs[-1]
    routed_ref[...] = jnp.zeros_like(routed_ref)
    windows = context_refs[0].shape[0] // patch_len
    for source, context_ref in enumerate(context_refs):
        for window in range(windows):
            slot = slot_of[source * windows + window]
            rows = context_ref[pl.ds(window * patch_len, patch_len), :]
            for head in range(2):
                lanes = pl.ds((2 * source + head) * HD, HD)
                routed_ref[slot, :, lanes] = rows[:, head * LANES : head * LANES + HD]


def route(slot_of, contexts, slots, patch_len):
    vmem = pl.BlockSpec(memory_space=pltpu.VMEM)
    width = 2 * HD * len(contexts)
    return pl.pallas_call(
        functools.partial(route_kernel, patch_len),
        in_specs=[pl.BlockSpec(memory_space=pltpu.SMEM)] + [vmem] * len(contexts),
        out_specs=vmem,
        out_shape=jax.ShapeDtypeStruct((slots, patch_len, width), BF16),
        compiler_params=pltpu.CompilerParams(vmem_limit_bytes=VMEM_BYTES),
        name="route",
    )(slot_of, *contexts)


def join_kernel(kept_ref, got_ref, *out_refs):
    count = out_refs[0].shape[1]
    for at, out_ref in enumerate(out_refs):
        out_ref[0] = kept_ref[pl.ds(at * count, count)]
        out_ref[1] = got_ref[pl.ds(at * count, count)]


def join(kept, got, nx):
    slots, patch_len, width = kept.shape
    vmem = pl.BlockSpec(memory_space=pltpu.VMEM)
    piece = jax.ShapeDtypeStruct((2, slots // nx, patch_len, width), BF16)
    return pl.pallas_call(
        join_kernel,
        in_specs=[vmem] * 2,
        out_specs=[vmem] * nx,
        out_shape=[piece] * nx,
        compiler_params=pltpu.CompilerParams(vmem_limit_bytes=VMEM_BYTES),
        name="join",
    )(kept, got)


def regroup_kernel(where, *refs):
    inputs = [ref for ref in refs if ref.shape[0] == 2]
    outputs = refs[len(inputs) :]
    copies = len(outputs)
    for step, out_ref in enumerate(outputs):
        target = lax.rem(where[2] + step, copies)
        for at, ref in enumerate(inputs):
            for kind in range(2):
                out_ref[at, kind] = ref[kind, target]


def regroup(where, pieces):
    _, copies, patch_len, width = pieces[0].shape
    vmem = pl.BlockSpec(memory_space=pltpu.VMEM)
    piece = jax.ShapeDtypeStruct((len(pieces), 2, patch_len, width), BF16)
    return pl.pallas_call(
        regroup_kernel,
        in_specs=[pl.BlockSpec(memory_space=pltpu.SMEM)] + [vmem] * len(pieces),
        out_specs=[vmem] * copies,
        out_shape=[piece] * copies,
        compiler_params=pltpu.CompilerParams(vmem_limit_bytes=VMEM_BYTES),
        name="regroup",
    )(where, *pieces)


def settle_kernel(where, places, *refs):
    arrived_refs, placed_ref = refs[:-1], refs[-1]
    copies, nx = len(arrived_refs), arrived_refs[0].shape[0]
    steps = ring_steps(nx)
    for step, arrived_ref in enumerate(arrived_refs):
        copy = lax.rem(where[2] + copies - step, copies)
        for swap in range(2):
            core = where[1] if swap == 0 else 1 - where[1]
            for sender in range(nx):
                at = places[sender]
                for source in range(nx):
                    lane = 2 * steps.index((sender - source) % nx)
                    slot = (copy * nx + source) * 2 + core
                    for kind in range(2):
                        rows = arrived_ref[at, swap, :, pl.ds((lane + kind) * HD, HD)]
                        placed_ref[slot, :, pl.ds((kind * nx + sender) * HD, HD)] = rows


def settle(where, places, arrived):
    nx, _, patch_len, width = arrived[0].shape
    vmem = pl.BlockSpec(memory_space=pltpu.VMEM)
    smem = pl.BlockSpec(memory_space=pltpu.SMEM)
    return pl.pallas_call(
        settle_kernel,
        in_specs=[smem, smem] + [vmem] * len(arrived),
        out_specs=vmem,
        out_shape=jax.ShapeDtypeStruct((len(arrived) * nx * 2, patch_len, width), BF16),
        compiler_params=pltpu.CompilerParams(vmem_limit_bytes=VMEM_BYTES),
        name="settle",
    )(where, places, *arrived)


def finish_kernel(cores, arrived_ref, grad_ref):
    heads = arrived_ref.shape[0]
    for place in range(heads):
        head = head_of(place, cores, heads)
        part = arrived_ref[place].astype(F32)
        grad_ref[:, pl.ds(head * HD, HD)] = part[:, :HD]
        grad_ref[:, pl.ds((heads + head) * HD, HD)] = part[:, HD:]


def finish(arrived, cores):
    heads, depth, width = arrived.shape
    vmem = pl.BlockSpec(memory_space=pltpu.VMEM)
    return pl.pallas_call(
        functools.partial(finish_kernel, cores),
        in_specs=[vmem],
        out_specs=vmem,
        out_shape=jax.ShapeDtypeStruct((depth, heads * width), F32),
        compiler_params=pltpu.CompilerParams(vmem_limit_bytes=VMEM_BYTES),
        name="finish",
    )(arrived)


def rotary_table():
    quarter = HD // 4
    lane = jnp.arange(LANES, dtype=jnp.int32)[None, :]
    kind = jnp.arange(3 * POSITIONS, dtype=jnp.int32)[:, None]
    frequency = 10000.0 ** (-(lane % quarter).astype(F32) / quarter)
    angles = (kind % POSITIONS).astype(F32) * frequency
    by_row = (kind < POSITIONS) & (lane < HD // 2)
    by_col = (kind >= POSITIONS) & (kind < 2 * POSITIONS) & (lane >= HD // 2) & (lane < HD)
    used = by_row | by_col
    flag = (kind == 2 * POSITIONS) & (lane == HD)
    cosine = jnp.where(used, jnp.cos(angles), jnp.where(flag, 1.0, 0.0))
    left = jnp.concatenate([cosine, jnp.where(used, jnp.sin(angles), 0.0)], axis=1)
    terms = []
    for _ in range(3):
        term = lax.reduce_precision(left, 8, 7)
        terms.append(term.astype(BF16))
        left = left - term
    return jnp.stack(terms)


def per_device(patches, values, upstream, coords, counts, dest, weight):
    core, here, copy = lax.axis_index("c"), lax.axis_index("x"), lax.axis_index("zl")
    nx, nc, copies = lax.axis_size("x"), lax.axis_size("c"), lax.axis_size("zl")
    ny, nz = lax.axis_size("y"), lax.axis_size("zh")
    heads = nx * nc
    slots = lax.axis_size(PEERS)
    window_count, patch_len, model_width = patches.shape
    value_width = values.shape[-1]
    row_total = window_count * patch_len
    depth = weight.shape[0]

    head = core * nx + here
    slice_q = lax.dynamic_slice_in_dim(weight, head * HD, HD, axis=1)
    slice_k = lax.dynamic_slice_in_dim(weight, value_width + head * HD, HD, axis=1)
    own_w = jnp.concatenate([slice_q, slice_k], axis=1)
    own_w = jnp.broadcast_to(own_w[None], (nz,) + own_w.shape)
    patches, values, upstream, coords, counts, dest = after(
        own_w, (patches, values, upstream, coords, counts, dest)
    )
    own_w = exchange(own_w, "zh")
    own_w = jnp.transpose(own_w, (1, 0, 2)).reshape(depth, nz * 2 * HD)
    own_w = spread(own_w, "y").reshape(ny * depth, nz * 2 * HD)

    live = jnp.arange(patch_len, dtype=jnp.int32)[None, :] < counts[:, None]
    notes = jnp.stack(
        [
            coords[:, 0, :].reshape(row_total),
            coords[:, 1, :].reshape(row_total),
            live.astype(jnp.int32).reshape(row_total),
            jnp.pad(dest[:, 0], (0, row_total - window_count)),
        ]
    )
    notes = jnp.pad(notes, ((0, EXTRA - 4), (0, value_width - row_total))).astype(BF16)
    values = values.reshape(row_total, value_width)
    upstream = upstream.reshape(row_total, value_width)
    steps = ring_steps(nx)
    where = jnp.stack([here, core, copy]).astype(jnp.int32)
    patches = patches.reshape(row_total, model_width)
    all_patches = [ring(patches, "x", step) for step in steps]
    packed = pack(where, values, upstream, notes, nx)
    packed = [ring(piece, "x", step) for piece, step in zip(packed, steps)]
    note_at = packed[0].shape[0] - EXTRA + 3
    all_dest = jnp.concatenate([piece[note_at, :window_count] for piece in packed])
    all_dest = all_dest.astype(jnp.int32)

    weights = (own_w, core_swap(own_w))
    table = rotary_table()
    *contexts, grad, sent = some_heads(
        where, weights, table, all_patches, packed, None, True, patch_len
    )
    step_of = lax.rem(all_dest // nc + nx - here, nx)
    slot_of = jnp.zeros_like(step_of)
    for at, step in enumerate(steps):
        slot_of = jnp.where(step_of == step, at, slot_of)
    away = jnp.where(lax.rem(all_dest, nc) == core, 0, nx)
    slot_of = (away + slot_of) * copies + all_dest // (nc * nx)
    routed = route(slot_of, contexts, slots, patch_len)
    half = slots // 2
    pieces = join(routed[:half], core_swap(routed[half:]), nx)
    pieces = [ring(piece, "x", step) for piece, step in zip(pieces, steps)]
    pieces = regroup(where, pieces)
    pieces = [ring(piece, "zl", step) for step, piece in enumerate(pieces)]
    places = [lax.rem(here - sender + nx, nx) for sender in range(nx)]
    places = [sum(jnp.where(at == steps[k], k, 0) for k in range(nx)) for at in places]
    places = jnp.stack(places).astype(jnp.int32)
    placed = settle(where, places, pieces)

    grad = (grad.astype(F32) + core_swap(sent).astype(F32)).astype(BF16)
    grad = exchange(grad.reshape(ny, depth, nz * 2 * HD), "y")
    grad = jnp.sum(grad.astype(F32), axis=0).astype(BF16)
    grad = jnp.transpose(grad.reshape(depth, nz, 2 * HD), (1, 0, 2))
    grad = jnp.broadcast_to(grad[None], (copies,) + grad.shape)
    grad = exchange(grad.reshape(copies * nz, depth, 2 * HD), ("zl", "zh"))
    grad = jnp.sum(grad.astype(F32), axis=0).astype(BF16)
    return (placed, finish(spread(grad, ("x", "c")), nc))


def solution(mesh):
    fine = Mesh(mesh.devices.reshape(SPLIT), AXES)
    return jax.shard_map(
        per_device,
        mesh=fine,
        in_specs=(
            P(AXES, None, None),
            P(AXES, None, None),
            P(AXES, None, None),
            P(AXES, None, None),
            P(AXES),
            P(AXES, None),
            P(("zh", "y"), None),
        ),
        out_specs=(P(AXES, None, None), P(("zh", "y"), None)),
        check_vma=False,
    )
```

```python
import functools
import math

import jax
import jax.numpy as jnp
from jax import lax
from jax.experimental import pallas as pl
from jax.experimental.pallas import tpu as pltpu
from jax.sharding import Mesh
from jax.sharding import PartitionSpec as P

HD = 80
LANES = 128
POSITIONS = 32
EXTRA = 16
SPLIT = (3, 4, 2, 4, 8)
AXES = ("zl", "x", "c", "zh", "y")
PEERS = ("zl", "x", "c")
BF16 = jnp.bfloat16
F32 = jnp.float32
VMEM_BYTES = 60 * 1024 * 1024


def core_swap(array):
    return lax.ppermute(array, "c", [(0, 1), (1, 0)])


def ring(array, axis, step):
    count = lax.axis_size(axis)
    if step == 0:
        return array
    return lax.ppermute(array, axis, [(i, (i + step) % count) for i in range(count)])


def exchange(array, axes):
    return lax.all_to_all(array, axes, split_axis=0, concat_axis=0, tiled=True)


def spread(array, axes):
    count = lax.axis_size(axes)
    return exchange(jnp.broadcast_to(array[None], (count,) + array.shape), axes)


def after(first, arrays):
    return lax.optimization_barrier((first, arrays))[1]


def dot(a, b, dims):
    return lax.dot_general(a, b, (dims, ((), ())), preferred_element_type=F32)


def head_of(place, cores, heads):
    return place % cores * (heads // cores) + place // cores


def partner(array):
    quarter = HD // 4
    lane = lax.broadcasted_iota(jnp.int32, array.shape, 1)
    front = lax.rem(lane, 2 * quarter) < quarter
    ahead = pltpu.roll(array, LANES - quarter, 1)
    behind = pltpu.roll(array, quarter, 1)
    return jnp.where(front, -ahead, behind)


def ring_steps(count):
    return [0, count - 1, 1] + list(range(2, count - 1))


def pack_kernel(
    where,
    counts,
    dest,
    coords_ref,
    patches_ref,
    values_ref,
    upstream_ref,
    own_ref,
    left_ref,
    right_ref,
    far_ref,
    notes_ref,
):
    packed_refs = (own_ref, left_ref, right_ref, far_ref)
    count = len(packed_refs)
    steps = ring_steps(count)
    rows, width = values_ref.shape
    windows, _, patch_len = coords_ref.shape
    lane = lax.broadcasted_iota(jnp.int32, (1, width), 1)
    live = jnp.zeros((1, width), jnp.int32)
    slot = jnp.zeros((1, width), jnp.int32)
    notes_ref[...] = jnp.zeros_like(notes_ref)
    for window in range(windows):
        at = window * patch_len
        for axis in range(2):
            coord = coords_ref[window, axis : axis + 1, :].astype(F32)
            notes_ref[axis : axis + 1, at : at + patch_len] = coord
        live = jnp.where((lane >= at) & (lane < at + counts[window]), 1, live)
        slot = jnp.where(lane == window, dest[window, 0], slot)
    notes_ref[2:3, :] = live.astype(F32)
    notes_ref[3:4, :] = slot.astype(F32)
    for packed_ref in (left_ref, right_ref):
        packed_ref[:rows, :] = patches_ref[:, :width]
        packed_ref[rows : 2 * rows, :] = patches_ref[:, width:]
    parts = width // (2 * HD)
    depth = rows // parts
    kinds = width // HD // count
    tops = [ref.shape[0] - EXTRA - kinds * depth for ref in packed_refs]
    for here in range(count):

        @pl.when(where[0] == here)
        def _():
            for packed_ref, step, top in zip(packed_refs, steps, tops):
                for kind in range(kinds):
                    head = kind * count + (here + step) % count
                    lanes = pl.ds(head * HD, HD)
                    for part in range(parts):
                        span, at = pl.ds(part * depth, depth), part * 2 * HD
                        out = pl.ds(top + kind * depth, depth)
                        packed_ref[out, pl.ds(at, HD)] = values_ref[span, lanes]
                        packed_ref[out, pl.ds(at + HD, HD)] = upstream_ref[span, lanes]

    notes = notes_ref[...].astype(BF16)
    for packed_ref in packed_refs:
        packed_ref[packed_ref.shape[0] - EXTRA :, :] = notes


def pack(where, counts, dest, coords, patches, values, upstream, count):
    rows, width = values.shape
    depth = width // HD // count * rows // (width // (2 * HD)) + EXTRA
    vmem = pl.BlockSpec(memory_space=pltpu.VMEM)
    smem = pl.BlockSpec(memory_space=pltpu.SMEM)
    small = jax.ShapeDtypeStruct((depth, width), BF16)
    large = jax.ShapeDtypeStruct((2 * rows + depth, width), BF16)
    return pl.pallas_call(
        pack_kernel,
        in_specs=[smem] * 3 + [vmem] * 4,
        out_specs=[vmem] * 4,
        out_shape=[small, large, large, small],
        scratch_shapes=[pltpu.VMEM((EXTRA, width), F32)],
        compiler_params=pltpu.CompilerParams(vmem_limit_bytes=VMEM_BYTES),
        name="pack",
    )(where, counts, dest, coords, patches, values, upstream)


def heads_kernel(patch_len, group, where, *refs):
    refs = list(refs)
    take = lambda count: [refs.pop(0) for _ in range(count)]
    own_hbm, other_hbm, table_hbm, patches_hbm, packed_hbm = take(5)
    left_hbm, right_hbm, low_hbm, high_hbm, far_hbm = take(5)
    context_refs = take(4)
    results = take(2)
    own_ref, other_ref, table_ref, whole_ref = take(4)
    packed_refs = take(4)
    full_ref, sum_ref, dproj_ref, values_ref, upstream_ref, arrivals = take(6)
    sources = len(packed_refs)
    rows, width = patches_hbm.shape[0], packed_hbm.shape[1]
    depth = packed_hbm.shape[0]
    patches_refs = [whole_ref.at[pl.ds(at * rows, rows), :] for at in range(sources)]
    halves = [[ref.at[:, pl.ds(at * width, width)] for at in range(2)] for ref in patches_refs]
    moves = [(own_hbm, own_ref), (other_hbm, other_ref), (table_hbm, table_ref)]
    waits = [[(patches_hbm, patches_refs[0])], [(packed_hbm, packed_refs[0])]]
    for at, source_hbm in ((1, left_hbm), (2, right_hbm)):
        cut = [source_hbm.at[pl.ds(half * rows, rows), :] for half in range(2)]
        waits.append(list(zip(cut, halves[at])))
        waits.append([(source_hbm.at[pl.ds(2 * rows, depth), :], packed_refs[at])])
    waits.append([(low_hbm, halves[3][0]), (high_hbm, halves[3][1])])
    waits.append([(far_hbm, packed_refs[3])])
    waits = [[move] for move in moves] + waits
    number = 0
    copies = []
    for moves in waits:
        copies.append([])
        for source, target in moves:
            copy = pltpu.make_async_copy(source, target, arrivals.at[number])
            copy.start()
            copies[-1].append(copy)
            number += 1

    def arrive(at):
        for copy in copies[at]:
            copy.wait()

    strip, strips = own_ref.shape[0], own_ref.shape[1] // (2 * HD)
    block = group * patch_len
    scale = 1.0 / math.sqrt(HD)
    full_ref[...] = jnp.zeros_like(full_ref)
    values_ref[...] = jnp.zeros_like(values_ref)
    upstream_ref[...] = jnp.zeros_like(upstream_ref)
    is_first = where[1] == 0
    arrive(0)
    arrive(1)
    for z in range(strips):
        span = pl.ds(z * strip, strip)
        for part in range(2):
            lanes = pl.ds((2 * z + part) * HD, HD)
            own, other = own_ref[:, lanes], other_ref[:, lanes]
            full_ref[span, pl.ds(part * LANES, HD)] = jnp.where(is_first, own, other)
            full_ref[span, pl.ds((2 + part) * LANES, HD)] = jnp.where(is_first, other, own)
    arrive(2)
    row_win = lax.broadcasted_iota(jnp.int32, (block, block), 0) // patch_len
    key_win = lax.broadcasted_iota(jnp.int32, (block, block), 1) // patch_len
    same = row_win == key_win
    kind = lax.broadcasted_iota(jnp.int32, (3 * POSITIONS, rows), 0)
    wanted = lax.rem(kind, POSITIONS).astype(F32)
    starts = [at for at in range(0, rows, block)]
    chains = [(head, at) for head in range(2) for at in range(len(starts))]
    each = range(len(chains))
    for source in range(sources):
        patches_ref, packed_ref = patches_refs[source], packed_refs[source]
        arrive(3 + 2 * source)
        proj = dot(patches_ref[...], full_ref[...], ((1,), (0,)))
        arrive(4 + 2 * source)
        depth = (packed_ref.shape[0] - EXTRA) // 2
        notes = packed_ref[2 * depth :, :rows].astype(F32)
        live_keys = notes[2:3, :]
        by_row = jnp.where(notes[0:1, :] == wanted, 1.0, 0.0)
        by_col = jnp.where(notes[1:2, :] == wanted, 1.0, 0.0)
        chosen = jnp.where(kind < 2 * POSITIONS, by_col, live_keys)
        chosen = jnp.where(kind < POSITIONS, by_row, chosen).astype(BF16)
        tables = dot(chosen, table_ref[0], ((0,), (0,)))
        tables += dot(chosen, table_ref[1], ((0,), (0,)))
        tables += dot(chosen, table_ref[2], ((0,), (0,)))
        for head in range(2):
            out, come = pl.ds(head * LANES, HD), pl.ds(head * depth, depth)
            for part in range(rows // depth):
                span, at = pl.ds(part * depth, depth), part * 2 * HD
                values_ref[span, out] = packed_ref[come, pl.ds(at, HD)]
                upstream_ref[span, out] = packed_ref[come, pl.ds(at + HD, HD)]
        cosines = [tables[s : s + block, :LANES] for s in starts]
        sines = [tables[s : s + block, LANES:] for s in starts]
        masks = [same & (live_keys[:, s : s + block] > 0.5) for s in starts]
        lives = [cosine[:, HD : HD + 1] for cosine in cosines]
        spans = [pl.ds(starts[at], block) for _, at in chains]
        lanes = [pl.ds(head * LANES, LANES) for head, _ in chains]
        blocks = [at for _, at in chains]
        q = [proj[starts[at] : starts[at] + block, 2 * h * LANES :][:, :LANES] for h, at in chains]
        k = [
            proj[starts[at] : starts[at] + block, (2 * h + 1) * LANES :][:, :LANES]
            for h, at in chains
        ]
        turn = lambda x, at: x * cosines[at] + partner(x) * sines[at]
        q = [turn(q[i], blocks[i]).astype(BF16) for i in each]
        k = [turn(k[i], blocks[i]).astype(BF16) for i in each]
        scores = [dot(q[i], k[i], ((1,), (1,))) * scale for i in each]
        v = [values_ref[spans[i], lanes[i]] for i in each]
        dprobs = [dot(upstream_ref[spans[i], lanes[i]], v[i], ((1,), (1,))) for i in each]
        scores = [jnp.where(masks[blocks[i]], scores[i], -1e30) for i in each]
        tops = [jnp.max(scores[i], axis=1, keepdims=True) for i in each]
        exps = [jnp.exp(scores[i] - tops[i]) for i in each]
        sums = [jnp.sum(exps[i], axis=1, keepdims=True) for i in each]
        probs = [exps[i] * (lives[blocks[i]] / sums[i]) for i in each]
        context = [dot(probs[i].astype(BF16), v[i], ((1,), (0,))) for i in each]
        delta = [jnp.sum(probs[i] * dprobs[i], axis=1, keepdims=True) for i in each]
        dscores = [(probs[i] * (dprobs[i] - delta[i]) * scale).astype(BF16) for i in each]
        dquery = [dot(dscores[i], k[i], ((1,), (0,))) for i in each]
        dkey = [dot(dscores[i], q[i], ((0,), (0,))) for i in each]
        back = lambda x, at: (x * cosines[at] - partner(x) * sines[at]).astype(BF16)
        for i in each:
            context_refs[source][spans[i], lanes[i]] = context[i].astype(BF16)
            at = 2 * chains[i][0] * LANES
            here = pl.ds(source * rows + starts[blocks[i]], block)
            dproj_ref[here, pl.ds(at, LANES)] = back(dquery[i], blocks[i])
            dproj_ref[here, pl.ds(at + LANES, LANES)] = back(dkey[i], blocks[i])
    sum_ref[...] = dot(dproj_ref[...], whole_ref[...], ((0,), (0,)))
    for z in range(strips):
        part = jnp.transpose(sum_ref[:, z * strip : (z + 1) * strip]).astype(BF16)
        for at in range(2):
            low = part[:, at * LANES : at * LANES + HD]
            high = part[:, (2 + at) * LANES : (2 + at) * LANES + HD]
            lanes = pl.ds((2 * z + at) * HD, HD)
            results[0][:, lanes] = jnp.where(is_first, low, high)
            results[1][:, lanes] = jnp.where(is_first, high, low)


def some_heads(where, weights, table, arrays, patch_len):
    rows, model_width = arrays[0].shape
    piece = arrays[1].shape
    group = math.gcd(rows // patch_len, max(1, 128 // patch_len))
    vmem = pl.BlockSpec(memory_space=pltpu.VMEM)
    hbm = pl.BlockSpec(memory_space=pltpu.HBM)
    grad_shape = jax.ShapeDtypeStruct(weights[0].shape, BF16)
    return pl.pallas_call(
        functools.partial(heads_kernel, patch_len, group),
        in_specs=[pl.BlockSpec(memory_space=pltpu.SMEM)] + [hbm] * (3 + len(arrays)),
        out_specs=[vmem] * 6,
        out_shape=[jax.ShapeDtypeStruct((rows, 2 * LANES), BF16)] * 4 + [grad_shape] * 2,
        scratch_shapes=[pltpu.VMEM(weights[0].shape, BF16)] * 2
        + [pltpu.VMEM(table.shape, BF16), pltpu.VMEM((4 * rows, model_width), BF16)]
        + [pltpu.VMEM(piece, BF16)] * 4
        + [
            pltpu.VMEM((model_width, 4 * LANES), BF16),
            pltpu.VMEM((4 * LANES, model_width), F32),
            pltpu.VMEM((4 * rows, 4 * LANES), BF16),
            pltpu.VMEM((rows, 2 * LANES), BF16),
            pltpu.VMEM((rows, 2 * LANES), BF16),
            pltpu.SemaphoreType.DMA((14,)),
        ],
        compiler_params=pltpu.CompilerParams(vmem_limit_bytes=VMEM_BYTES),
        cost_estimate=pl.CostEstimate(
            flops=20_000_000_000, bytes_accessed=12_000_000, transcendentals=3_000_000
        ),
        name="heads",
    )(where, *weights, table, *arrays)


def route_kernel(patch_len, slot_of, *refs):
    context_refs, routed_refs = refs[:-2], refs[-2:]
    half = routed_refs[0].shape[0]
    for routed_ref in routed_refs:
        routed_ref[...] = jnp.zeros_like(routed_ref)
    windows = context_refs[0].shape[0] // patch_len
    for source, context_ref in enumerate(context_refs):
        for window in range(windows):
            slot = slot_of[source * windows + window]
            rows = context_ref[pl.ds(window * patch_len, patch_len), :]
            for away, routed_ref in enumerate(routed_refs):

                @pl.when((slot >= half) == (away == 1))
                def _():
                    for head in range(2):
                        lanes = pl.ds((2 * source + head) * HD, HD)
                        here = rows[:, head * LANES : head * LANES + HD]
                        routed_ref[slot - away * half, :, lanes] = here


def route(slot_of, contexts, slots, patch_len):
    vmem = pl.BlockSpec(memory_space=pltpu.VMEM)
    piece = jax.ShapeDtypeStruct((slots // 2, patch_len, 2 * HD * len(contexts)), BF16)
    return pl.pallas_call(
        functools.partial(route_kernel, patch_len),
        in_specs=[pl.BlockSpec(memory_space=pltpu.SMEM)] + [vmem] * len(contexts),
        out_specs=[vmem] * 2,
        out_shape=[piece] * 2,
        compiler_params=pltpu.CompilerParams(vmem_limit_bytes=VMEM_BYTES),
        name="route",
    )(slot_of, *contexts)


def join_kernel(kept_ref, got_ref, *out_refs):
    count = out_refs[0].shape[1]
    for at, out_ref in enumerate(out_refs):
        out_ref[0] = kept_ref[pl.ds(at * count, count)]
        out_ref[1] = got_ref[pl.ds(at * count, count)]


def join(kept, got, nx):
    slots, patch_len, width = kept.shape
    vmem = pl.BlockSpec(memory_space=pltpu.VMEM)
    piece = jax.ShapeDtypeStruct((2, slots // nx, patch_len, width), BF16)
    return pl.pallas_call(
        join_kernel,
        in_specs=[vmem] * 2,
        out_specs=[vmem] * nx,
        out_shape=[piece] * nx,
        compiler_params=pltpu.CompilerParams(vmem_limit_bytes=VMEM_BYTES),
        name="join",
    )(kept, got)


def regroup_kernel(where, *refs):
    inputs = [ref for ref in refs if ref.shape[0] == 2]
    outputs = refs[len(inputs) :]
    copies = len(outputs)
    for step, out_ref in enumerate(outputs):
        target = lax.rem(where[2] + step, copies)
        for at, ref in enumerate(inputs):
            for kind in range(2):
                out_ref[at, kind] = ref[kind, target]


def regroup(where, pieces):
    _, copies, patch_len, width = pieces[0].shape
    vmem = pl.BlockSpec(memory_space=pltpu.VMEM)
    piece = jax.ShapeDtypeStruct((len(pieces), 2, patch_len, width), BF16)
    return pl.pallas_call(
        regroup_kernel,
        in_specs=[pl.BlockSpec(memory_space=pltpu.SMEM)] + [vmem] * len(pieces),
        out_specs=[vmem] * copies,
        out_shape=[piece] * copies,
        compiler_params=pltpu.CompilerParams(vmem_limit_bytes=VMEM_BYTES),
        name="regroup",
    )(where, *pieces)


def settle_kernel(where, places, *refs):
    arrived_refs, placed_ref = refs[:-1], refs[-1]
    copies, nx = len(arrived_refs), arrived_refs[0].shape[0]
    steps = ring_steps(nx)
    for step, arrived_ref in enumerate(arrived_refs):
        copy = lax.rem(where[2] + copies - step, copies)
        for swap in range(2):
            core = where[1] if swap == 0 else 1 - where[1]
            for sender in range(nx):
                at = places[sender]
                for source in range(nx):
                    lane = 2 * steps.index((sender - source) % nx)
                    slot = (copy * nx + source) * 2 + core
                    for kind in range(2):
                        rows = arrived_ref[at, swap, :, pl.ds((lane + kind) * HD, HD)]
                        placed_ref[slot, :, pl.ds((kind * nx + sender) * HD, HD)] = rows


def settle(where, places, arrived):
    nx, _, patch_len, width = arrived[0].shape
    vmem = pl.BlockSpec(memory_space=pltpu.VMEM)
    smem = pl.BlockSpec(memory_space=pltpu.SMEM)
    return pl.pallas_call(
        settle_kernel,
        in_specs=[smem, smem] + [vmem] * len(arrived),
        out_specs=vmem,
        out_shape=jax.ShapeDtypeStruct((len(arrived) * nx * 2, patch_len, width), BF16),
        compiler_params=pltpu.CompilerParams(vmem_limit_bytes=VMEM_BYTES),
        name="settle",
    )(where, places, *arrived)


def finish_kernel(cores, arrived_ref, grad_ref):
    heads = arrived_ref.shape[0]
    for place in range(heads):
        head = head_of(place, cores, heads)
        part = arrived_ref[place].astype(F32)
        grad_ref[:, pl.ds(head * HD, HD)] = part[:, :HD]
        grad_ref[:, pl.ds((heads + head) * HD, HD)] = part[:, HD:]


def finish(arrived, cores):
    heads, depth, width = arrived.shape
    vmem = pl.BlockSpec(memory_space=pltpu.VMEM)
    return pl.pallas_call(
        functools.partial(finish_kernel, cores),
        in_specs=[vmem],
        out_specs=vmem,
        out_shape=jax.ShapeDtypeStruct((depth, heads * width), F32),
        compiler_params=pltpu.CompilerParams(vmem_limit_bytes=VMEM_BYTES),
        name="finish",
    )(arrived)


def rotary_table():
    quarter = HD // 4
    lane = jnp.arange(LANES, dtype=jnp.int32)[None, :]
    kind = jnp.arange(3 * POSITIONS, dtype=jnp.int32)[:, None]
    frequency = 10000.0 ** (-(lane % quarter).astype(F32) / quarter)
    angles = (kind % POSITIONS).astype(F32) * frequency
    by_row = (kind < POSITIONS) & (lane < HD // 2)
    by_col = (kind >= POSITIONS) & (kind < 2 * POSITIONS) & (lane >= HD // 2) & (lane < HD)
    used = by_row | by_col
    flag = (kind == 2 * POSITIONS) & (lane == HD)
    cosine = jnp.where(used, jnp.cos(angles), jnp.where(flag, 1.0, 0.0))
    left = jnp.concatenate([cosine, jnp.where(used, jnp.sin(angles), 0.0)], axis=1)
    terms = []
    for _ in range(3):
        term = lax.reduce_precision(left, 8, 7)
        terms.append(term.astype(BF16))
        left = left - term
    return jnp.stack(terms)


def per_device(patches, values, upstream, coords, counts, dest, weight):
    core, here, copy = lax.axis_index("c"), lax.axis_index("x"), lax.axis_index("zl")
    nx, nc, copies = lax.axis_size("x"), lax.axis_size("c"), lax.axis_size("zl")
    ny, nz = lax.axis_size("y"), lax.axis_size("zh")
    heads = nx * nc
    slots = lax.axis_size(PEERS)
    window_count, patch_len, model_width = patches.shape
    value_width = values.shape[-1]
    row_total = window_count * patch_len
    depth = weight.shape[0]

    where = jnp.stack([here, core, copy]).astype(jnp.int32)
    steps = ring_steps(nx)
    patches = patches.reshape(row_total, model_width)
    values = values.reshape(row_total, value_width)
    upstream = upstream.reshape(row_total, value_width)
    own, left, right, far = pack(where, counts, dest, coords, patches, values, upstream, nx)
    left, right = ring(left, "x", steps[1]), ring(right, "x", steps[2])

    head = core * nx + here
    slice_q = lax.dynamic_slice_in_dim(weight, head * HD, HD, axis=1)
    slice_k = lax.dynamic_slice_in_dim(weight, value_width + head * HD, HD, axis=1)
    own_w = jnp.concatenate([slice_q, slice_k], axis=1)
    own_w = spread(own_w, "zh")
    far = ring(after(own_w, far), "x", steps[3])
    own_w = jnp.transpose(own_w, (1, 0, 2)).reshape(depth, nz * 2 * HD)
    own_w = spread(own_w, "y").reshape(ny * depth, nz * 2 * HD)
    weights = (own_w, core_swap(own_w))
    left, right, far = after(own_w, (left, right, far))
    low = ring(right[:row_total], "x", steps[2])
    high = ring(left[row_total : 2 * row_total], "x", steps[1])

    all_dest = [dest[:, 0]]
    for piece in (left, right, far):
        at = piece.shape[0] - EXTRA + 3
        all_dest.append(piece[at, :window_count].astype(jnp.int32))
    all_dest = jnp.concatenate(all_dest)
    step_of = lax.rem(all_dest // nc + nx - here, nx)
    slot_of = jnp.zeros_like(step_of)
    for at, step in enumerate(steps):
        slot_of = jnp.where(step_of == step, at, slot_of)
    away = jnp.where(lax.rem(all_dest, nc) == core, 0, nx)
    slot_of = (away + slot_of) * copies + all_dest // (nc * nx)

    *contexts, grad, sent = some_heads(
        after(slot_of, where),
        weights,
        rotary_table(),
        (patches, own, left, right, low, high, far),
        patch_len,
    )
    grad = (grad.astype(F32) + core_swap(sent).astype(F32)).astype(BF16)
    contexts = after(grad, contexts)
    kept, sent = route(slot_of, contexts, slots, patch_len)
    pieces = join(kept, core_swap(sent), nx)
    pieces = [ring(piece, "x", step) for piece, step in zip(pieces, steps)]
    pieces = regroup(where, pieces)
    pieces = [ring(piece, "zl", step) for step, piece in enumerate(pieces)]
    places = [lax.rem(here - sender + nx, nx) for sender in range(nx)]
    places = [sum(jnp.where(at == steps[k], k, 0) for k in range(nx)) for at in places]
    places = jnp.stack(places).astype(jnp.int32)
    placed = settle(where, places, pieces)

    grad = exchange(grad.reshape(ny, depth, nz * 2 * HD), "y")
    grad = jnp.sum(grad.astype(F32), axis=0).astype(BF16)
    grad = jnp.transpose(grad.reshape(depth, nz, 2 * HD), (1, 0, 2))
    grad = jnp.broadcast_to(grad[None], (copies,) + grad.shape)
    grad = exchange(grad.reshape(copies * nz, depth, 2 * HD), ("zl", "zh"))
    grad = jnp.sum(grad.astype(F32), axis=0).astype(BF16)
    return (placed, finish(spread(grad, ("x", "c")), nc))


def solution(mesh):
    fine = Mesh(mesh.devices.reshape(SPLIT), AXES)
    return jax.shard_map(
        per_device,
        mesh=fine,
        in_specs=(
            P(AXES, None, None),
            P(AXES, None, None),
            P(AXES, None, None),
            P(AXES, None, None),
            P(AXES),
            P(AXES, None),
            P(("zh", "y"), None),
        ),
        out_specs=(P(AXES, None, None), P(("zh", "y"), None)),
        check_vma=False,
    )
```

```python
import functools
import math

import jax
import jax.numpy as jnp
from jax import lax
from jax.experimental import pallas as pl
from jax.experimental.pallas import tpu as pltpu
from jax.sharding import Mesh
from jax.sharding import PartitionSpec as P

HD = 80
LANES = 128
POSITIONS = 32
EXTRA = 16
SPLIT = (3, 4, 2, 4, 8)
AXES = ("zl", "x", "c", "zh", "y")
PEERS = ("zl", "x", "c")
BF16 = jnp.bfloat16
F32 = jnp.float32
VMEM_BYTES = 60 * 1024 * 1024


def core_swap(array):
    return lax.ppermute(array, "c", [(0, 1), (1, 0)])


def ring(array, axis, step):
    count = lax.axis_size(axis)
    if step == 0:
        return array
    return lax.ppermute(array, axis, [(i, (i + step) % count) for i in range(count)])


def exchange(array, axes):
    return lax.all_to_all(array, axes, split_axis=0, concat_axis=0, tiled=True)


def spread(array, axes):
    count = lax.axis_size(axes)
    return exchange(jnp.broadcast_to(array[None], (count,) + array.shape), axes)


def after(first, arrays):
    return lax.optimization_barrier((first, arrays))[1]


def dot(a, b, dims):
    return lax.dot_general(a, b, (dims, ((), ())), preferred_element_type=F32)


def head_of(place, cores, heads):
    return place % cores * (heads // cores) + place // cores


def partner(array):
    quarter = HD // 4
    lane = lax.broadcasted_iota(jnp.int32, array.shape, 1)
    front = lax.rem(lane, 2 * quarter) < quarter
    ahead = pltpu.roll(array, LANES - quarter, 1)
    behind = pltpu.roll(array, quarter, 1)
    return jnp.where(front, -ahead, behind)


def ring_steps(count):
    return [0, count - 1, 1] + list(range(2, count - 1))


def pack_kernel(
    where,
    counts,
    dest,
    coords_ref,
    patches_ref,
    values_ref,
    upstream_ref,
    own_ref,
    left_ref,
    right_ref,
    far_ref,
    notes_ref,
):
    packed_refs = (own_ref, left_ref, right_ref, far_ref)
    count = len(packed_refs)
    steps = ring_steps(count)
    rows, width = values_ref.shape
    windows, _, patch_len = coords_ref.shape
    lane = lax.broadcasted_iota(jnp.int32, (1, width), 1)
    live = jnp.zeros((1, width), jnp.int32)
    slot = jnp.zeros((1, width), jnp.int32)
    notes_ref[...] = jnp.zeros_like(notes_ref)
    for window in range(windows):
        at = window * patch_len
        for axis in range(2):
            coord = coords_ref[window, axis : axis + 1, :].astype(F32)
            notes_ref[axis : axis + 1, at : at + patch_len] = coord
        live = jnp.where((lane >= at) & (lane < at + counts[window]), 1, live)
        slot = jnp.where(lane == window, dest[window, 0], slot)
    notes_ref[2:3, :] = live.astype(F32)
    notes_ref[3:4, :] = slot.astype(F32)
    for packed_ref in packed_refs[1:]:
        packed_ref[:rows, :] = patches_ref[:, :width]
        packed_ref[rows : 2 * rows, :] = patches_ref[:, width:]
    parts = width // (2 * HD)
    depth = rows // parts
    kinds = width // HD // count
    tops = [ref.shape[0] - EXTRA - kinds * depth for ref in packed_refs]
    for here in range(count):

        @pl.when(where[0] == here)
        def _():
            for packed_ref, step, top in zip(packed_refs, steps, tops):
                for kind in range(kinds):
                    head = kind * count + (here + step) % count
                    lanes = pl.ds(head * HD, HD)
                    for part in range(parts):
                        span, at = pl.ds(part * depth, depth), part * 2 * HD
                        out = pl.ds(top + kind * depth, depth)
                        packed_ref[out, pl.ds(at, HD)] = values_ref[span, lanes]
                        packed_ref[out, pl.ds(at + HD, HD)] = upstream_ref[span, lanes]

    notes = notes_ref[...].astype(BF16)
    for packed_ref in packed_refs:
        packed_ref[packed_ref.shape[0] - EXTRA :, :] = notes


def pack(where, counts, dest, coords, patches, values, upstream, count):
    rows, width = values.shape
    depth = width // HD // count * rows // (width // (2 * HD)) + EXTRA
    vmem = pl.BlockSpec(memory_space=pltpu.VMEM)
    smem = pl.BlockSpec(memory_space=pltpu.SMEM)
    small = jax.ShapeDtypeStruct((depth, width), BF16)
    large = jax.ShapeDtypeStruct((2 * rows + depth, width), BF16)
    return pl.pallas_call(
        pack_kernel,
        in_specs=[smem] * 3 + [vmem] * 4,
        out_specs=[vmem] * 4,
        out_shape=[small, large, large, large],
        scratch_shapes=[pltpu.VMEM((EXTRA, width), F32)],
        compiler_params=pltpu.CompilerParams(vmem_limit_bytes=VMEM_BYTES),
        name="pack",
    )(where, counts, dest, coords, patches, values, upstream)


def heads_kernel(patch_len, group, where, *refs):
    refs = list(refs)
    take = lambda count: [refs.pop(0) for _ in range(count)]
    own_hbm, other_hbm, table_hbm, patches_hbm, packed_hbm = take(5)
    remote_hbm = take(3)
    context_refs = take(4)
    results = take(2)
    own_ref, other_ref, table_ref, whole_ref = take(4)
    packed_refs = take(4)
    full_ref, sum_ref, dproj_ref, values_ref, upstream_ref, arrivals = take(6)
    sources = len(packed_refs)
    rows, width = patches_hbm.shape[0], packed_hbm.shape[1]
    depth = packed_hbm.shape[0]
    patches_refs = [whole_ref.at[pl.ds(at * rows, rows), :] for at in range(sources)]
    halves = [[ref.at[:, pl.ds(at * width, width)] for at in range(2)] for ref in patches_refs]
    moves = [(own_hbm, own_ref), (other_hbm, other_ref), (table_hbm, table_ref)]
    waits = [[(patches_hbm, patches_refs[0])], [(packed_hbm, packed_refs[0])]]
    for at, source_hbm in enumerate(remote_hbm, 1):
        cut = [source_hbm.at[pl.ds(half * rows, rows), :] for half in range(2)]
        waits.append(list(zip(cut, halves[at])))
        waits.append([(source_hbm.at[pl.ds(2 * rows, depth), :], packed_refs[at])])
    waits = [[move] for move in moves] + waits
    number = 0
    copies = []
    for moves in waits:
        copies.append([])
        for source, target in moves:
            copy = pltpu.make_async_copy(source, target, arrivals.at[number])
            copy.start()
            copies[-1].append(copy)
            number += 1

    def arrive(at):
        for copy in copies[at]:
            copy.wait()

    strip, strips = own_ref.shape[0], own_ref.shape[1] // (2 * HD)
    block = group * patch_len
    scale = 1.0 / math.sqrt(HD)
    full_ref[...] = jnp.zeros_like(full_ref)
    values_ref[...] = jnp.zeros_like(values_ref)
    upstream_ref[...] = jnp.zeros_like(upstream_ref)
    is_first = where[1] == 0
    arrive(0)
    arrive(1)
    for z in range(strips):
        span = pl.ds(z * strip, strip)
        for part in range(2):
            lanes = pl.ds((2 * z + part) * HD, HD)
            own, other = own_ref[:, lanes], other_ref[:, lanes]
            full_ref[span, pl.ds(part * LANES, HD)] = jnp.where(is_first, own, other)
            full_ref[span, pl.ds((2 + part) * LANES, HD)] = jnp.where(is_first, other, own)
    arrive(2)
    row_win = lax.broadcasted_iota(jnp.int32, (block, block), 0) // patch_len
    key_win = lax.broadcasted_iota(jnp.int32, (block, block), 1) // patch_len
    same = row_win == key_win
    kind = lax.broadcasted_iota(jnp.int32, (3 * POSITIONS, rows), 0)
    wanted = lax.rem(kind, POSITIONS).astype(F32)
    starts = [at for at in range(0, rows, block)]
    chains = [(head, at) for head in range(2) for at in range(len(starts))]
    each = range(len(chains))
    for source in range(sources):
        patches_ref, packed_ref = patches_refs[source], packed_refs[source]
        arrive(3 + 2 * source)
        proj = dot(patches_ref[...], full_ref[...], ((1,), (0,)))
        arrive(4 + 2 * source)
        depth = (packed_ref.shape[0] - EXTRA) // 2
        notes = packed_ref[2 * depth :, :rows].astype(F32)
        live_keys = notes[2:3, :]
        by_row = jnp.where(notes[0:1, :] == wanted, 1.0, 0.0)
        by_col = jnp.where(notes[1:2, :] == wanted, 1.0, 0.0)
        chosen = jnp.where(kind < 2 * POSITIONS, by_col, live_keys)
        chosen = jnp.where(kind < POSITIONS, by_row, chosen).astype(BF16)
        tables = dot(chosen, table_ref[0], ((0,), (0,)))
        tables += dot(chosen, table_ref[1], ((0,), (0,)))
        tables += dot(chosen, table_ref[2], ((0,), (0,)))
        for head in range(2):
            out, come = pl.ds(head * LANES, HD), pl.ds(head * depth, depth)
            for part in range(rows // depth):
                span, at = pl.ds(part * depth, depth), part * 2 * HD
                values_ref[span, out] = packed_ref[come, pl.ds(at, HD)]
                upstream_ref[span, out] = packed_ref[come, pl.ds(at + HD, HD)]
        cosines = [tables[s : s + block, :LANES] for s in starts]
        sines = [tables[s : s + block, LANES:] for s in starts]
        masks = [same & (live_keys[:, s : s + block] > 0.5) for s in starts]
        lives = [cosine[:, HD : HD + 1] for cosine in cosines]
        spans = [pl.ds(starts[at], block) for _, at in chains]
        lanes = [pl.ds(head * LANES, LANES) for head, _ in chains]
        blocks = [at for _, at in chains]
        q = [proj[starts[at] : starts[at] + block, 2 * h * LANES :][:, :LANES] for h, at in chains]
        k = [
            proj[starts[at] : starts[at] + block, (2 * h + 1) * LANES :][:, :LANES]
            for h, at in chains
        ]
        turn = lambda x, at: x * cosines[at] + partner(x) * sines[at]
        q = [turn(q[i], blocks[i]).astype(BF16) for i in each]
        k = [turn(k[i], blocks[i]).astype(BF16) for i in each]
        scores = [dot(q[i], k[i], ((1,), (1,))) * scale for i in each]
        v = [values_ref[spans[i], lanes[i]] for i in each]
        dprobs = [dot(upstream_ref[spans[i], lanes[i]], v[i], ((1,), (1,))) for i in each]
        scores = [jnp.where(masks[blocks[i]], scores[i], -1e30) for i in each]
        tops = [jnp.max(scores[i], axis=1, keepdims=True) for i in each]
        exps = [jnp.exp(scores[i] - tops[i]) for i in each]
        sums = [jnp.sum(exps[i], axis=1, keepdims=True) for i in each]
        probs = [exps[i] * (lives[blocks[i]] / sums[i]) for i in each]
        context = [dot(probs[i].astype(BF16), v[i], ((1,), (0,))) for i in each]
        delta = [jnp.sum(probs[i] * dprobs[i], axis=1, keepdims=True) for i in each]
        dscores = [(probs[i] * (dprobs[i] - delta[i]) * scale).astype(BF16) for i in each]
        dquery = [dot(dscores[i], k[i], ((1,), (0,))) for i in each]
        dkey = [dot(dscores[i], q[i], ((0,), (0,))) for i in each]
        back = lambda x, at: (x * cosines[at] - partner(x) * sines[at]).astype(BF16)
        for i in each:
            context_refs[source][spans[i], lanes[i]] = context[i].astype(BF16)
            at = 2 * chains[i][0] * LANES
            here = pl.ds(source * rows + starts[blocks[i]], block)
            dproj_ref[here, pl.ds(at, LANES)] = back(dquery[i], blocks[i])
            dproj_ref[here, pl.ds(at + LANES, LANES)] = back(dkey[i], blocks[i])
    sum_ref[...] = dot(dproj_ref[...], whole_ref[...], ((0,), (0,)))
    for z in range(strips):
        part = jnp.transpose(sum_ref[:, z * strip : (z + 1) * strip]).astype(BF16)
        for at in range(2):
            low = part[:, at * LANES : at * LANES + HD]
            high = part[:, (2 + at) * LANES : (2 + at) * LANES + HD]
            lanes = pl.ds((2 * z + at) * HD, HD)
            results[0][:, lanes] = jnp.where(is_first, low, high)
            results[1][:, lanes] = jnp.where(is_first, high, low)


def some_heads(where, weights, table, arrays, patch_len):
    rows, model_width = arrays[0].shape
    piece = arrays[1].shape
    group = math.gcd(rows // patch_len, max(1, 128 // patch_len))
    vmem = pl.BlockSpec(memory_space=pltpu.VMEM)
    hbm = pl.BlockSpec(memory_space=pltpu.HBM)
    grad_shape = jax.ShapeDtypeStruct(weights[0].shape, BF16)
    return pl.pallas_call(
        functools.partial(heads_kernel, patch_len, group),
        in_specs=[pl.BlockSpec(memory_space=pltpu.SMEM)] + [hbm] * (3 + len(arrays)),
        out_specs=[vmem] * 6,
        out_shape=[jax.ShapeDtypeStruct((rows, 2 * LANES), BF16)] * 4 + [grad_shape] * 2,
        scratch_shapes=[pltpu.VMEM(weights[0].shape, BF16)] * 2
        + [pltpu.VMEM(table.shape, BF16), pltpu.VMEM((4 * rows, model_width), BF16)]
        + [pltpu.VMEM(piece, BF16)] * 4
        + [
            pltpu.VMEM((model_width, 4 * LANES), BF16),
            pltpu.VMEM((4 * LANES, model_width), F32),
            pltpu.VMEM((4 * rows, 4 * LANES), BF16),
            pltpu.VMEM((rows, 2 * LANES), BF16),
            pltpu.VMEM((rows, 2 * LANES), BF16),
            pltpu.SemaphoreType.DMA((14,)),
        ],
        compiler_params=pltpu.CompilerParams(vmem_limit_bytes=VMEM_BYTES),
        cost_estimate=pl.CostEstimate(
            flops=20_000_000_000, bytes_accessed=12_000_000, transcendentals=3_000_000
        ),
        name="heads",
    )(where, *weights, table, *arrays)


def route_kernel(patch_len, slot_of, *refs):
    context_refs, routed_refs, table_ref = refs[:4], refs[4:-1], refs[-1]
    table_ref[...] = jnp.zeros_like(table_ref)
    windows = context_refs[0].shape[0] // patch_len
    for source, context_ref in enumerate(context_refs):
        for window in range(windows):
            slot = slot_of[source * windows + window]
            rows = context_ref[pl.ds(window * patch_len, patch_len), :]
            for head in range(2):
                lanes = pl.ds((2 * source + head) * HD, HD)
                table_ref[slot, :, lanes] = rows[:, head * LANES : head * LANES + HD]
    for at, routed_ref in enumerate(routed_refs):
        count = routed_ref.shape[0]
        routed_ref[...] = table_ref[pl.ds(at * count, count)]


def route(slot_of, contexts, slots, patch_len):
    count = len(contexts)
    vmem = pl.BlockSpec(memory_space=pltpu.VMEM)
    shape = (patch_len, 2 * HD * count)
    return pl.pallas_call(
        functools.partial(route_kernel, patch_len),
        in_specs=[pl.BlockSpec(memory_space=pltpu.SMEM)] + [vmem] * count,
        out_specs=[vmem] * count,
        out_shape=[jax.ShapeDtypeStruct((slots // count,) + shape, BF16)] * count,
        scratch_shapes=[pltpu.VMEM((slots,) + shape, BF16)],
        compiler_params=pltpu.CompilerParams(vmem_limit_bytes=VMEM_BYTES),
        name="route",
    )(slot_of, *contexts)


def regroup_kernel(count, where, *refs):
    inputs, outputs = refs[:count], refs[count:]
    copies = len(outputs) // 2
    for step in range(copies):
        target = lax.rem(where[2] + step, copies)
        for swap in range(2):
            core = where[1] if swap == 0 else 1 - where[1]
            for at, ref in enumerate(inputs):
                outputs[2 * step + swap][at] = ref[2 * target + core]


def regroup(where, pieces):
    slots, patch_len, width = pieces[0].shape
    vmem = pl.BlockSpec(memory_space=pltpu.VMEM)
    piece = jax.ShapeDtypeStruct((len(pieces), patch_len, width), BF16)
    return pl.pallas_call(
        functools.partial(regroup_kernel, len(pieces)),
        in_specs=[pl.BlockSpec(memory_space=pltpu.SMEM)] + [vmem] * len(pieces),
        out_specs=[vmem] * slots,
        out_shape=[piece] * slots,
        compiler_params=pltpu.CompilerParams(vmem_limit_bytes=VMEM_BYTES),
        name="regroup",
    )(where, *pieces)


def hop(array, step, swap):
    copies, cores = lax.axis_size("zl"), lax.axis_size("c")
    if step == 0 and swap == 0:
        return array
    pairs = [
        (z * cores + c, (z + step) % copies * cores + (c + swap) % cores)
        for z in range(copies)
        for c in range(cores)
    ]
    return lax.ppermute(array, ("zl", "c"), pairs)


def settle_kernel(where, places, *refs):
    arrived_refs, placed_ref = refs[:-1], refs[-1]
    copies, nx = len(arrived_refs) // 2, arrived_refs[0].shape[0]
    steps = ring_steps(nx)
    for step in range(copies):
        copy = lax.rem(where[2] + copies - step, copies)
        for swap in range(2):
            core = where[1] if swap == 0 else 1 - where[1]
            for sender in range(nx):
                at = places[sender]
                for source in range(nx):
                    lane = 2 * steps.index((sender - source) % nx)
                    slot = (copy * nx + source) * 2 + core
                    for kind in range(2):
                        here = pl.ds((lane + kind) * HD, HD)
                        rows = arrived_refs[2 * step + swap][at, :, here]
                        placed_ref[slot, :, pl.ds((kind * nx + sender) * HD, HD)] = rows


def settle(where, places, arrived):
    nx, patch_len, width = arrived[0].shape
    vmem = pl.BlockSpec(memory_space=pltpu.VMEM)
    smem = pl.BlockSpec(memory_space=pltpu.SMEM)
    return pl.pallas_call(
        settle_kernel,
        in_specs=[smem, smem] + [vmem] * len(arrived),
        out_specs=vmem,
        out_shape=jax.ShapeDtypeStruct((len(arrived) * nx, patch_len, width), BF16),
        compiler_params=pltpu.CompilerParams(vmem_limit_bytes=VMEM_BYTES),
        name="settle",
    )(where, places, *arrived)


def finish_kernel(cores, arrived_ref, grad_ref):
    heads = arrived_ref.shape[0]
    for place in range(heads):
        head = head_of(place, cores, heads)
        part = arrived_ref[place].astype(F32)
        grad_ref[:, pl.ds(head * HD, HD)] = part[:, :HD]
        grad_ref[:, pl.ds((heads + head) * HD, HD)] = part[:, HD:]


def finish(arrived, cores):
    heads, depth, width = arrived.shape
    vmem = pl.BlockSpec(memory_space=pltpu.VMEM)
    return pl.pallas_call(
        functools.partial(finish_kernel, cores),
        in_specs=[vmem],
        out_specs=vmem,
        out_shape=jax.ShapeDtypeStruct((depth, heads * width), F32),
        compiler_params=pltpu.CompilerParams(vmem_limit_bytes=VMEM_BYTES),
        name="finish",
    )(arrived)


def rotary_table():
    quarter = HD // 4
    lane = jnp.arange(LANES, dtype=jnp.int32)[None, :]
    kind = jnp.arange(3 * POSITIONS, dtype=jnp.int32)[:, None]
    frequency = 10000.0 ** (-(lane % quarter).astype(F32) / quarter)
    angles = (kind % POSITIONS).astype(F32) * frequency
    by_row = (kind < POSITIONS) & (lane < HD // 2)
    by_col = (kind >= POSITIONS) & (kind < 2 * POSITIONS) & (lane >= HD // 2) & (lane < HD)
    used = by_row | by_col
    flag = (kind == 2 * POSITIONS) & (lane == HD)
    cosine = jnp.where(used, jnp.cos(angles), jnp.where(flag, 1.0, 0.0))
    left = jnp.concatenate([cosine, jnp.where(used, jnp.sin(angles), 0.0)], axis=1)
    terms = []
    for _ in range(3):
        term = lax.reduce_precision(left, 8, 7)
        terms.append(term.astype(BF16))
        left = left - term
    return jnp.stack(terms)


def per_device(patches, values, upstream, coords, counts, dest, weight):
    core, here, copy = lax.axis_index("c"), lax.axis_index("x"), lax.axis_index("zl")
    nx, nc, copies = lax.axis_size("x"), lax.axis_size("c"), lax.axis_size("zl")
    ny, nz = lax.axis_size("y"), lax.axis_size("zh")
    heads = nx * nc
    slots = lax.axis_size(PEERS)
    window_count, patch_len, model_width = patches.shape
    value_width = values.shape[-1]
    row_total = window_count * patch_len
    depth = weight.shape[0]

    where = jnp.stack([here, core, copy]).astype(jnp.int32)
    steps = ring_steps(nx)
    patches = patches.reshape(row_total, model_width)
    values = values.reshape(row_total, value_width)
    upstream = upstream.reshape(row_total, value_width)
    own, left, right, far = pack(where, counts, dest, coords, patches, values, upstream, nx)
    left, right = ring(left, "x", steps[1]), ring(right, "x", steps[2])
    far = ring(far, "x", steps[3])

    head = core * nx + here
    slice_q = lax.dynamic_slice_in_dim(weight, head * HD, HD, axis=1)
    slice_k = lax.dynamic_slice_in_dim(weight, value_width + head * HD, HD, axis=1)
    own_w = jnp.concatenate([slice_q, slice_k], axis=1)
    own_w = spread(own_w, "zh")
    own_w = jnp.transpose(own_w, (1, 0, 2)).reshape(depth, nz * 2 * HD)
    own_w = spread(own_w, "y").reshape(ny * depth, nz * 2 * HD)
    weights = (own_w, core_swap(own_w))
    left, right, far = after(own_w, (left, right, far))

    all_dest = [dest[:, 0]]
    for piece in (left, right, far):
        at = piece.shape[0] - EXTRA + 3
        all_dest.append(piece[at, :window_count].astype(jnp.int32))
    all_dest = jnp.concatenate(all_dest)
    step_of = lax.rem(all_dest // nc + nx - here, nx)
    slot_of = jnp.zeros_like(step_of)
    for at, step in enumerate(steps):
        slot_of = jnp.where(step_of == step, at, slot_of)
    slot_of = (slot_of * copies + all_dest // (nc * nx)) * nc + lax.rem(all_dest, nc)

    *contexts, grad, sent = some_heads(
        after(slot_of, where),
        weights,
        rotary_table(),
        (patches, own, left, right, far),
        patch_len,
    )
    grad = (grad.astype(F32) + core_swap(sent).astype(F32)).astype(BF16)
    pieces = route(slot_of, contexts, slots, patch_len)
    grad = after(pieces, grad)
    pieces = [ring(piece, "x", step) for piece, step in zip(pieces, steps)]
    crossed = pieces
    pieces = regroup(where, pieces)
    pieces = [hop(piece, at // 2, at % 2) for at, piece in enumerate(pieces)]
    places = [lax.rem(here - sender + nx, nx) for sender in range(nx)]
    places = [sum(jnp.where(at == steps[k], k, 0) for k in range(nx)) for at in places]
    places = jnp.stack(places).astype(jnp.int32)
    placed = settle(where, places, pieces)

    grad = exchange(grad.reshape(ny, depth, nz * 2 * HD), "y")
    grad = jnp.sum(grad.astype(F32), axis=0).astype(BF16)
    grad = jnp.transpose(grad.reshape(depth, nz, 2 * HD), (1, 0, 2))
    grad = jnp.broadcast_to(after(crossed, grad)[None], (copies,) + grad.shape)
    grad = exchange(grad.reshape(copies * nz, depth, 2 * HD), ("zl", "zh"))
    grad = jnp.sum(grad.astype(F32), axis=0).astype(BF16)
    return (placed, finish(spread(grad, ("x", "c")), nc))


def solution(mesh):
    fine = Mesh(mesh.devices.reshape(SPLIT), AXES)
    return jax.shard_map(
        per_device,
        mesh=fine,
        in_specs=(
            P(AXES, None, None),
            P(AXES, None, None),
            P(AXES, None, None),
            P(AXES, None, None),
            P(AXES),
            P(AXES, None),
            P(("zh", "y"), None),
        ),
        out_specs=(P(AXES, None, None), P(("zh", "y"), None)),
        check_vma=False,
    )
```

```python
import functools
import math

import jax
import jax.numpy as jnp
from jax import lax
from jax.experimental import pallas as pl
from jax.experimental.pallas import tpu as pltpu
from jax.sharding import Mesh
from jax.sharding import PartitionSpec as P

HD = 80
LANES = 128
POSITIONS = 32
EXTRA = 16
SPLIT = (3, 4, 2, 4, 8)
AXES = ("zl", "x", "c", "zh", "y")
PEERS = ("zl", "x", "c")
BF16 = jnp.bfloat16
F32 = jnp.float32
VMEM_BYTES = 60 * 1024 * 1024


def core_swap(array):
    return lax.ppermute(array, "c", [(0, 1), (1, 0)])


def ring(array, axis, step):
    count = lax.axis_size(axis)
    if step == 0:
        return array
    return lax.ppermute(array, axis, [(i, (i + step) % count) for i in range(count)])


def exchange(array, axes):
    return lax.all_to_all(array, axes, split_axis=0, concat_axis=0, tiled=True)


def spread(array, axes):
    count = lax.axis_size(axes)
    return exchange(jnp.broadcast_to(array[None], (count,) + array.shape), axes)


def after(first, arrays):
    return lax.optimization_barrier((first, arrays))[1]


def dot(a, b, dims):
    return lax.dot_general(a, b, (dims, ((), ())), preferred_element_type=F32)


def head_of(place, cores, heads):
    return place % cores * (heads // cores) + place // cores


def partner(array):
    quarter = HD // 4
    lane = lax.broadcasted_iota(jnp.int32, array.shape, 1)
    front = lax.rem(lane, 2 * quarter) < quarter
    ahead = pltpu.roll(array, LANES - quarter, 1)
    behind = pltpu.roll(array, quarter, 1)
    return jnp.where(front, -ahead, behind)


def ring_steps(count):
    return [0, count - 1, 1] + list(range(2, count - 1))


def pack_kernel(
    where,
    counts,
    dest,
    coords_ref,
    patches_ref,
    values_ref,
    upstream_ref,
    own_ref,
    left_ref,
    right_ref,
    far_ref,
    notes_ref,
):
    packed_refs = (own_ref, left_ref, right_ref, far_ref)
    count = len(packed_refs)
    steps = ring_steps(count)
    rows, width = values_ref.shape
    windows, _, patch_len = coords_ref.shape
    lane = lax.broadcasted_iota(jnp.int32, (1, width), 1)
    live = jnp.zeros((1, width), jnp.int32)
    slot = jnp.zeros((1, width), jnp.int32)
    notes_ref[...] = jnp.zeros_like(notes_ref)
    for window in range(windows):
        at = window * patch_len
        for axis in range(2):
            coord = coords_ref[window, axis : axis + 1, :].astype(F32)
            notes_ref[axis : axis + 1, at : at + patch_len] = coord
        live = jnp.where((lane >= at) & (lane < at + counts[window]), 1, live)
        slot = jnp.where(lane == window, dest[window, 0], slot)
    notes_ref[2:3, :] = live.astype(F32)
    notes_ref[3:4, :] = slot.astype(F32)
    for packed_ref in (left_ref, right_ref):
        packed_ref[:rows, :] = patches_ref[:, :width]
        packed_ref[rows : 2 * rows, :] = patches_ref[:, width:]
    parts = width // (2 * HD)
    depth = rows // parts
    kinds = width // HD // count
    tops = [ref.shape[0] - EXTRA - kinds * depth for ref in packed_refs]
    for here in range(count):

        @pl.when(where[0] == here)
        def _():
            for packed_ref, step, top in zip(packed_refs, steps, tops):
                for kind in range(kinds):
                    head = kind * count + (here + step) % count
                    lanes = pl.ds(head * HD, HD)
                    for part in range(parts):
                        span, at = pl.ds(part * depth, depth), part * 2 * HD
                        out = pl.ds(top + kind * depth, depth)
                        packed_ref[out, pl.ds(at, HD)] = values_ref[span, lanes]
                        packed_ref[out, pl.ds(at + HD, HD)] = upstream_ref[span, lanes]

    notes = notes_ref[...].astype(BF16)
    for packed_ref in packed_refs:
        packed_ref[packed_ref.shape[0] - EXTRA :, :] = notes


def pack(where, counts, dest, coords, patches, values, upstream, count):
    rows, width = values.shape
    depth = width // HD // count * rows // (width // (2 * HD)) + EXTRA
    vmem = pl.BlockSpec(memory_space=pltpu.VMEM)
    smem = pl.BlockSpec(memory_space=pltpu.SMEM)
    small = jax.ShapeDtypeStruct((depth, width), BF16)
    large = jax.ShapeDtypeStruct((2 * rows + depth, width), BF16)
    return pl.pallas_call(
        pack_kernel,
        in_specs=[smem] * 3 + [vmem] * 4,
        out_specs=[vmem] * 4,
        out_shape=[small, large, large, small],
        scratch_shapes=[pltpu.VMEM((EXTRA, width), F32)],
        compiler_params=pltpu.CompilerParams(vmem_limit_bytes=VMEM_BYTES),
        name="pack",
    )(where, counts, dest, coords, patches, values, upstream)


def heads_kernel(patch_len, group, where, *refs):
    refs = list(refs)
    take = lambda count: [refs.pop(0) for _ in range(count)]
    own_hbm, other_hbm, table_hbm, patches_hbm, packed_hbm = take(5)
    left_hbm, right_hbm, low_hbm, high_hbm, far_hbm = take(5)
    context_refs = take(4)
    results = take(2)
    own_ref, other_ref, table_ref, whole_ref = take(4)
    packed_refs = take(4)
    full_ref, sum_ref, dproj_ref, values_ref, upstream_ref, arrivals = take(6)
    sources = len(packed_refs)
    rows, width = patches_hbm.shape[0], packed_hbm.shape[1]
    depth = packed_hbm.shape[0]
    patches_refs = [whole_ref.at[pl.ds(at * rows, rows), :] for at in range(sources)]
    halves = [[ref.at[:, pl.ds(at * width, width)] for at in range(2)] for ref in patches_refs]
    moves = [(own_hbm, own_ref), (other_hbm, other_ref), (table_hbm, table_ref)]
    waits = [[(patches_hbm, patches_refs[0])], [(packed_hbm, packed_refs[0])]]
    for at, source_hbm in ((1, left_hbm), (2, right_hbm)):
        cut = [source_hbm.at[pl.ds(half * rows, rows), :] for half in range(2)]
        waits.append(list(zip(cut, halves[at])))
        waits.append([(source_hbm.at[pl.ds(2 * rows, depth), :], packed_refs[at])])
    waits.append([(low_hbm, halves[3][0]), (high_hbm, halves[3][1])])
    waits.append([(far_hbm, packed_refs[3])])
    waits = [[move] for move in moves] + waits
    number = 0
    copies = []
    for moves in waits:
        copies.append([])
        for source, target in moves:
            copy = pltpu.make_async_copy(source, target, arrivals.at[number])
            copy.start()
            copies[-1].append(copy)
            number += 1

    def arrive(at):
        for copy in copies[at]:
            copy.wait()

    strip, strips = own_ref.shape[0], own_ref.shape[1] // (2 * HD)
    block = group * patch_len
    scale = 1.0 / math.sqrt(HD)
    full_ref[...] = jnp.zeros_like(full_ref)
    values_ref[...] = jnp.zeros_like(values_ref)
    upstream_ref[...] = jnp.zeros_like(upstream_ref)
    is_first = where[1] == 0
    arrive(0)
    arrive(1)
    for z in range(strips):
        span = pl.ds(z * strip, strip)
        for part in range(2):
            lanes = pl.ds((2 * z + part) * HD, HD)
            own, other = own_ref[:, lanes], other_ref[:, lanes]
            full_ref[span, pl.ds(part * LANES, HD)] = jnp.where(is_first, own, other)
            full_ref[span, pl.ds((2 + part) * LANES, HD)] = jnp.where(is_first, other, own)
    arrive(2)
    row_win = lax.broadcasted_iota(jnp.int32, (block, block), 0) // patch_len
    key_win = lax.broadcasted_iota(jnp.int32, (block, block), 1) // patch_len
    same = row_win == key_win
    kind = lax.broadcasted_iota(jnp.int32, (3 * POSITIONS, rows), 0)
    wanted = lax.rem(kind, POSITIONS).astype(F32)
    starts = [at for at in range(0, rows, block)]
    chains = [(head, at) for head in range(2) for at in range(len(starts))]
    each = range(len(chains))
    for source in range(sources):
        patches_ref, packed_ref = patches_refs[source], packed_refs[source]
        arrive(3 + 2 * source)
        proj = dot(patches_ref[...], full_ref[...], ((1,), (0,)))
        arrive(4 + 2 * source)
        depth = (packed_ref.shape[0] - EXTRA) // 2
        notes = packed_ref[2 * depth :, :rows].astype(F32)
        live_keys = notes[2:3, :]
        by_row = jnp.where(notes[0:1, :] == wanted, 1.0, 0.0)
        by_col = jnp.where(notes[1:2, :] == wanted, 1.0, 0.0)
        chosen = jnp.where(kind < 2 * POSITIONS, by_col, live_keys)
        chosen = jnp.where(kind < POSITIONS, by_row, chosen).astype(BF16)
        tables = dot(chosen, table_ref[0], ((0,), (0,)))
        tables += dot(chosen, table_ref[1], ((0,), (0,)))
        tables += dot(chosen, table_ref[2], ((0,), (0,)))
        for head in range(2):
            out, come = pl.ds(head * LANES, HD), pl.ds(head * depth, depth)
            for part in range(rows // depth):
                span, at = pl.ds(part * depth, depth), part * 2 * HD
                values_ref[span, out] = packed_ref[come, pl.ds(at, HD)]
                upstream_ref[span, out] = packed_ref[come, pl.ds(at + HD, HD)]
        cosines = [tables[s : s + block, :LANES] for s in starts]
        sines = [tables[s : s + block, LANES:] for s in starts]
        masks = [same & (live_keys[:, s : s + block] > 0.5) for s in starts]
        lives = [cosine[:, HD : HD + 1] for cosine in cosines]
        spans = [pl.ds(starts[at], block) for _, at in chains]
        lanes = [pl.ds(head * LANES, LANES) for head, _ in chains]
        blocks = [at for _, at in chains]
        q = [proj[starts[at] : starts[at] + block, 2 * h * LANES :][:, :LANES] for h, at in chains]
        k = [
            proj[starts[at] : starts[at] + block, (2 * h + 1) * LANES :][:, :LANES]
            for h, at in chains
        ]
        turn = lambda x, at: x * cosines[at] + partner(x) * sines[at]
        q = [turn(q[i], blocks[i]).astype(BF16) for i in each]
        k = [turn(k[i], blocks[i]).astype(BF16) for i in each]
        scores = [dot(q[i], k[i], ((1,), (1,))) * scale for i in each]
        v = [values_ref[spans[i], lanes[i]] for i in each]
        dprobs = [dot(upstream_ref[spans[i], lanes[i]], v[i], ((1,), (1,))) for i in each]
        scores = [jnp.where(masks[blocks[i]], scores[i], -1e30) for i in each]
        tops = [jnp.max(scores[i], axis=1, keepdims=True) for i in each]
        exps = [jnp.exp(scores[i] - tops[i]) for i in each]
        sums = [jnp.sum(exps[i], axis=1, keepdims=True) for i in each]
        probs = [exps[i] * (lives[blocks[i]] / sums[i]) for i in each]
        context = [dot(probs[i].astype(BF16), v[i], ((1,), (0,))) for i in each]
        delta = [jnp.sum(probs[i] * dprobs[i], axis=1, keepdims=True) for i in each]
        dscores = [(probs[i] * (dprobs[i] - delta[i]) * scale).astype(BF16) for i in each]
        dquery = [dot(dscores[i], k[i], ((1,), (0,))) for i in each]
        dkey = [dot(dscores[i], q[i], ((0,), (0,))) for i in each]
        back = lambda x, at: (x * cosines[at] - partner(x) * sines[at]).astype(BF16)
        for i in each:
            context_refs[source][spans[i], lanes[i]] = context[i].astype(BF16)
            at = 2 * chains[i][0] * LANES
            here = pl.ds(source * rows + starts[blocks[i]], block)
            dproj_ref[here, pl.ds(at, LANES)] = back(dquery[i], blocks[i])
            dproj_ref[here, pl.ds(at + LANES, LANES)] = back(dkey[i], blocks[i])
    sum_ref[...] = dot(dproj_ref[...], whole_ref[...], ((0,), (0,)))
    for z in range(strips):
        part = jnp.transpose(sum_ref[:, z * strip : (z + 1) * strip]).astype(BF16)
        for at in range(2):
            low = part[:, at * LANES : at * LANES + HD]
            high = part[:, (2 + at) * LANES : (2 + at) * LANES + HD]
            lanes = pl.ds((2 * z + at) * HD, HD)
            results[0][:, lanes] = jnp.where(is_first, low, high)
            results[1][:, lanes] = jnp.where(is_first, high, low)


def some_heads(where, weights, table, arrays, patch_len):
    rows, model_width = arrays[0].shape
    piece = arrays[1].shape
    group = math.gcd(rows // patch_len, max(1, 128 // patch_len))
    vmem = pl.BlockSpec(memory_space=pltpu.VMEM)
    hbm = pl.BlockSpec(memory_space=pltpu.HBM)
    grad_shape = jax.ShapeDtypeStruct(weights[0].shape, BF16)
    return pl.pallas_call(
        functools.partial(heads_kernel, patch_len, group),
        in_specs=[pl.BlockSpec(memory_space=pltpu.SMEM)] + [hbm] * (3 + len(arrays)),
        out_specs=[vmem] * 6,
        out_shape=[jax.ShapeDtypeStruct((rows, 2 * LANES), BF16)] * 4 + [grad_shape] * 2,
        scratch_shapes=[pltpu.VMEM(weights[0].shape, BF16)] * 2
        + [pltpu.VMEM(table.shape, BF16), pltpu.VMEM((4 * rows, model_width), BF16)]
        + [pltpu.VMEM(piece, BF16)] * 4
        + [
            pltpu.VMEM((model_width, 4 * LANES), BF16),
            pltpu.VMEM((4 * LANES, model_width), F32),
            pltpu.VMEM((4 * rows, 4 * LANES), BF16),
            pltpu.VMEM((rows, 2 * LANES), BF16),
            pltpu.VMEM((rows, 2 * LANES), BF16),
            pltpu.SemaphoreType.DMA((14,)),
        ],
        compiler_params=pltpu.CompilerParams(vmem_limit_bytes=VMEM_BYTES),
        cost_estimate=pl.CostEstimate(
            flops=20_000_000_000, bytes_accessed=12_000_000, transcendentals=3_000_000
        ),
        name="heads",
    )(where, *weights, table, *arrays)


def route_kernel(patch_len, slot_of, *refs):
    context_refs, routed_refs, table_ref = refs[:4], refs[4:-1], refs[-1]
    table_ref[...] = jnp.zeros_like(table_ref)
    windows = context_refs[0].shape[0] // patch_len
    for source, context_ref in enumerate(context_refs):
        for window in range(windows):
            slot = slot_of[source * windows + window]
            rows = context_ref[pl.ds(window * patch_len, patch_len), :]
            for head in range(2):
                lanes = pl.ds((2 * source + head) * HD, HD)
                table_ref[slot, :, lanes] = rows[:, head * LANES : head * LANES + HD]
    for at, routed_ref in enumerate(routed_refs):
        count = routed_ref.shape[0]
        routed_ref[...] = table_ref[pl.ds(at * count, count)]


def route(slot_of, contexts, slots, patch_len):
    count = len(contexts)
    vmem = pl.BlockSpec(memory_space=pltpu.VMEM)
    shape = (patch_len, 2 * HD * count)
    return pl.pallas_call(
        functools.partial(route_kernel, patch_len),
        in_specs=[pl.BlockSpec(memory_space=pltpu.SMEM)] + [vmem] * count,
        out_specs=[vmem] * count,
        out_shape=[jax.ShapeDtypeStruct((slots // count,) + shape, BF16)] * count,
        scratch_shapes=[pltpu.VMEM((slots,) + shape, BF16)],
        compiler_params=pltpu.CompilerParams(vmem_limit_bytes=VMEM_BYTES),
        name="route",
    )(slot_of, *contexts)


def regroup_kernel(count, where, *refs):
    inputs, outputs = refs[:count], refs[count:]
    copies = len(outputs) // 2
    for step in range(copies):
        target = lax.rem(where[2] + step, copies)
        for swap in range(2):
            core = where[1] if swap == 0 else 1 - where[1]
            for at, ref in enumerate(inputs):
                outputs[2 * step + swap][at] = ref[2 * target + core]


def regroup(where, pieces):
    slots, patch_len, width = pieces[0].shape
    vmem = pl.BlockSpec(memory_space=pltpu.VMEM)
    piece = jax.ShapeDtypeStruct((len(pieces), patch_len, width), BF16)
    return pl.pallas_call(
        functools.partial(regroup_kernel, len(pieces)),
        in_specs=[pl.BlockSpec(memory_space=pltpu.SMEM)] + [vmem] * len(pieces),
        out_specs=[vmem] * slots,
        out_shape=[piece] * slots,
        compiler_params=pltpu.CompilerParams(vmem_limit_bytes=VMEM_BYTES),
        name="regroup",
    )(where, *pieces)


def hop(array, step, swap):
    copies, cores = lax.axis_size("zl"), lax.axis_size("c")
    if step == 0 and swap == 0:
        return array
    pairs = [
        (z * cores + c, (z + step) % copies * cores + (c + swap) % cores)
        for z in range(copies)
        for c in range(cores)
    ]
    return lax.ppermute(array, ("zl", "c"), pairs)


def settle_kernel(where, places, *refs):
    arrived_refs, placed_ref = refs[:-1], refs[-1]
    copies, nx = len(arrived_refs) // 2, arrived_refs[0].shape[0]
    steps = ring_steps(nx)
    for step in range(copies):
        copy = lax.rem(where[2] + copies - step, copies)
        for swap in range(2):
            core = where[1] if swap == 0 else 1 - where[1]
            for sender in range(nx):
                at = places[sender]
                for source in range(nx):
                    lane = 2 * steps.index((sender - source) % nx)
                    slot = (copy * nx + source) * 2 + core
                    for kind in range(2):
                        here = pl.ds((lane + kind) * HD, HD)
                        rows = arrived_refs[2 * step + swap][at, :, here]
                        placed_ref[slot, :, pl.ds((kind * nx + sender) * HD, HD)] = rows


def settle(where, places, arrived):
    nx, patch_len, width = arrived[0].shape
    vmem = pl.BlockSpec(memory_space=pltpu.VMEM)
    smem = pl.BlockSpec(memory_space=pltpu.SMEM)
    return pl.pallas_call(
        settle_kernel,
        in_specs=[smem, smem] + [vmem] * len(arrived),
        out_specs=vmem,
        out_shape=jax.ShapeDtypeStruct((len(arrived) * nx, patch_len, width), BF16),
        compiler_params=pltpu.CompilerParams(vmem_limit_bytes=VMEM_BYTES),
        name="settle",
    )(where, places, *arrived)


def finish_kernel(cores, arrived_ref, grad_ref):
    heads = arrived_ref.shape[0]
    for place in range(heads):
        head = head_of(place, cores, heads)
        part = arrived_ref[place].astype(F32)
        grad_ref[:, pl.ds(head * HD, HD)] = part[:, :HD]
        grad_ref[:, pl.ds((heads + head) * HD, HD)] = part[:, HD:]


def finish(arrived, cores):
    heads, depth, width = arrived.shape
    vmem = pl.BlockSpec(memory_space=pltpu.VMEM)
    return pl.pallas_call(
        functools.partial(finish_kernel, cores),
        in_specs=[vmem],
        out_specs=vmem,
        out_shape=jax.ShapeDtypeStruct((depth, heads * width), F32),
        compiler_params=pltpu.CompilerParams(vmem_limit_bytes=VMEM_BYTES),
        name="finish",
    )(arrived)


def rotary_table():
    quarter = HD // 4
    lane = jnp.arange(LANES, dtype=jnp.int32)[None, :]
    kind = jnp.arange(3 * POSITIONS, dtype=jnp.int32)[:, None]
    frequency = 10000.0 ** (-(lane % quarter).astype(F32) / quarter)
    angles = (kind % POSITIONS).astype(F32) * frequency
    by_row = (kind < POSITIONS) & (lane < HD // 2)
    by_col = (kind >= POSITIONS) & (kind < 2 * POSITIONS) & (lane >= HD // 2) & (lane < HD)
    used = by_row | by_col
    flag = (kind == 2 * POSITIONS) & (lane == HD)
    cosine = jnp.where(used, jnp.cos(angles), jnp.where(flag, 1.0, 0.0))
    left = jnp.concatenate([cosine, jnp.where(used, jnp.sin(angles), 0.0)], axis=1)
    terms = []
    for _ in range(3):
        term = lax.reduce_precision(left, 8, 7)
        terms.append(term.astype(BF16))
        left = left - term
    return jnp.stack(terms)


def per_device(patches, values, upstream, coords, counts, dest, weight):
    core, here, copy = lax.axis_index("c"), lax.axis_index("x"), lax.axis_index("zl")
    nx, nc, copies = lax.axis_size("x"), lax.axis_size("c"), lax.axis_size("zl")
    ny, nz = lax.axis_size("y"), lax.axis_size("zh")
    heads = nx * nc
    slots = lax.axis_size(PEERS)
    window_count, patch_len, model_width = patches.shape
    value_width = values.shape[-1]
    row_total = window_count * patch_len
    depth = weight.shape[0]

    head = core * nx + here
    slice_q = lax.dynamic_slice_in_dim(weight, head * HD, HD, axis=1)
    slice_k = lax.dynamic_slice_in_dim(weight, value_width + head * HD, HD, axis=1)
    own_w = jnp.concatenate([slice_q, slice_k], axis=1)
    own_w = jnp.broadcast_to(own_w[None], (nz,) + own_w.shape)
    where = jnp.stack([here, core, copy]).astype(jnp.int32)
    steps = ring_steps(nx)
    patches = patches.reshape(row_total, model_width)
    values = values.reshape(row_total, value_width)
    upstream = upstream.reshape(row_total, value_width)
    own, left, right, far = pack(where, counts, dest, coords, patches, values, upstream, nx)
    left, right = ring(left, "x", steps[1]), ring(right, "x", steps[2])

    own_w = exchange(own_w, "zh")
    far = ring(after(own_w, far), "x", steps[3])
    own_w = jnp.transpose(own_w, (1, 0, 2)).reshape(depth, nz * 2 * HD)
    low, high = right[:row_total], left[row_total : 2 * row_total]
    own_w = after((low, high), own_w)
    low, high = ring(low, "x", steps[2]), ring(high, "x", steps[1])
    own_w = spread(own_w, "y").reshape(ny * depth, nz * 2 * HD)
    weights = (own_w, core_swap(own_w))
    left, right, far = after(own_w, (left, right, far))

    all_dest = [dest[:, 0]]
    for piece in (left, right, far):
        at = piece.shape[0] - EXTRA + 3
        all_dest.append(piece[at, :window_count].astype(jnp.int32))
    all_dest = jnp.concatenate(all_dest)
    step_of = lax.rem(all_dest // nc + nx - here, nx)
    slot_of = jnp.zeros_like(step_of)
    for at, step in enumerate(steps):
        slot_of = jnp.where(step_of == step, at, slot_of)
    slot_of = (slot_of * copies + all_dest // (nc * nx)) * nc + lax.rem(all_dest, nc)

    *contexts, grad, sent = some_heads(
        after(slot_of, where),
        weights,
        rotary_table(),
        (patches, own, left, right, low, high, far),
        patch_len,
    )
    grad = (grad.astype(F32) + core_swap(sent).astype(F32)).astype(BF16)
    pieces = route(slot_of, contexts, slots, patch_len)
    grad = after(pieces, grad)
    pieces = [ring(piece, "x", step) for piece, step in zip(pieces, steps)]
    crossed = pieces
    pieces = regroup(where, pieces)
    pieces = [hop(piece, at // 2, at % 2) for at, piece in enumerate(pieces)]
    places = [lax.rem(here - sender + nx, nx) for sender in range(nx)]
    places = [sum(jnp.where(at == steps[k], k, 0) for k in range(nx)) for at in places]
    places = jnp.stack(places).astype(jnp.int32)
    placed = settle(where, places, pieces)

    grad = exchange(grad.reshape(ny, depth, nz * 2 * HD), "y")
    grad = jnp.sum(grad.astype(F32), axis=0).astype(BF16)
    grad = jnp.transpose(grad.reshape(depth, nz, 2 * HD), (1, 0, 2))
    grad = jnp.broadcast_to(after(crossed, grad)[None], (copies,) + grad.shape)
    grad = exchange(grad.reshape(copies * nz, depth, 2 * HD), ("zl", "zh"))
    grad = jnp.sum(grad.astype(F32), axis=0).astype(BF16)
    return (placed, finish(spread(grad, ("x", "c")), nc))


def solution(mesh):
    fine = Mesh(mesh.devices.reshape(SPLIT), AXES)
    return jax.shard_map(
        per_device,
        mesh=fine,
        in_specs=(
            P(AXES, None, None),
            P(AXES, None, None),
            P(AXES, None, None),
            P(AXES, None, None),
            P(AXES),
            P(AXES, None),
            P(("zh", "y"), None),
        ),
        out_specs=(P(AXES, None, None), P(("zh", "y"), None)),
        check_vma=False,
    )
```

```python
import functools
import math

import jax
import jax.numpy as jnp
from jax import lax
from jax.experimental import pallas as pl
from jax.experimental.pallas import tpu as pltpu
from jax.sharding import Mesh
from jax.sharding import PartitionSpec as P

HD = 80
LANES = 128
POSITIONS = 32
EXTRA = 16
SPLIT = (3, 4, 2, 4, 8)
AXES = ("zl", "x", "c", "zh", "y")
PEERS = ("zl", "x", "c")
BF16 = jnp.bfloat16
F32 = jnp.float32
VMEM_BYTES = 60 * 1024 * 1024


def core_swap(array):
    return lax.ppermute(array, "c", [(0, 1), (1, 0)])


def ring(array, axis, step):
    count = lax.axis_size(axis)
    if step == 0:
        return array
    return lax.ppermute(array, axis, [(i, (i + step) % count) for i in range(count)])


def exchange(array, axes):
    return lax.all_to_all(array, axes, split_axis=0, concat_axis=0, tiled=True)


def spread(array, axes):
    count = lax.axis_size(axes)
    return exchange(jnp.broadcast_to(array[None], (count,) + array.shape), axes)


def after(first, arrays):
    return lax.optimization_barrier((first, arrays))[1]


def dot(a, b, dims):
    return lax.dot_general(a, b, (dims, ((), ())), preferred_element_type=F32)


def head_of(place, cores, heads):
    return place % cores * (heads // cores) + place // cores


def partner(array):
    quarter = HD // 4
    lane = lax.broadcasted_iota(jnp.int32, array.shape, 1)
    front = lax.rem(lane, 2 * quarter) < quarter
    ahead = pltpu.roll(array, LANES - quarter, 1)
    behind = pltpu.roll(array, quarter, 1)
    return jnp.where(front, -ahead, behind)


def ring_steps(count):
    return [0, count - 1, 1] + list(range(2, count - 1))


def pack_kernel(
    where,
    counts,
    dest,
    coords_ref,
    patches_ref,
    values_ref,
    upstream_ref,
    own_ref,
    left_ref,
    right_ref,
    far_ref,
    notes_ref,
):
    packed_refs = (own_ref, left_ref, right_ref, far_ref)
    count = len(packed_refs)
    steps = ring_steps(count)
    rows, width = values_ref.shape
    windows, _, patch_len = coords_ref.shape
    lane = lax.broadcasted_iota(jnp.int32, (1, width), 1)
    live = jnp.zeros((1, width), jnp.int32)
    slot = jnp.zeros((1, width), jnp.int32)
    notes_ref[...] = jnp.zeros_like(notes_ref)
    for window in range(windows):
        at = window * patch_len
        for axis in range(2):
            coord = coords_ref[window, axis : axis + 1, :].astype(F32)
            notes_ref[axis : axis + 1, at : at + patch_len] = coord
        live = jnp.where((lane >= at) & (lane < at + counts[window]), 1, live)
        slot = jnp.where(lane == window, dest[window, 0], slot)
    notes_ref[2:3, :] = live.astype(F32)
    notes_ref[3:4, :] = slot.astype(F32)
    for packed_ref in packed_refs[1:]:
        packed_ref[:rows, :] = patches_ref[:, :width]
        packed_ref[rows : 2 * rows, :] = patches_ref[:, width:]
    parts = width // (2 * HD)
    depth = rows // parts
    kinds = width // HD // count
    tops = [ref.shape[0] - EXTRA - kinds * depth for ref in packed_refs]
    for here in range(count):

        @pl.when(where[0] == here)
        def _():
            for packed_ref, step, top in zip(packed_refs, steps, tops):
                for kind in range(kinds):
                    head = kind * count + (here + step) % count
                    lanes = pl.ds(head * HD, HD)
                    for part in range(parts):
                        span, at = pl.ds(part * depth, depth), part * 2 * HD
                        out = pl.ds(top + kind * depth, depth)
                        packed_ref[out, pl.ds(at, HD)] = values_ref[span, lanes]
                        packed_ref[out, pl.ds(at + HD, HD)] = upstream_ref[span, lanes]

    notes = notes_ref[...].astype(BF16)
    for packed_ref in packed_refs:
        packed_ref[packed_ref.shape[0] - EXTRA :, :] = notes


def pack(where, counts, dest, coords, patches, values, upstream, count):
    rows, width = values.shape
    depth = width // HD // count * rows // (width // (2 * HD)) + EXTRA
    vmem = pl.BlockSpec(memory_space=pltpu.VMEM)
    smem = pl.BlockSpec(memory_space=pltpu.SMEM)
    small = jax.ShapeDtypeStruct((depth, width), BF16)
    large = jax.ShapeDtypeStruct((2 * rows + depth, width), BF16)
    return pl.pallas_call(
        pack_kernel,
        in_specs=[smem] * 3 + [vmem] * 4,
        out_specs=[vmem] * 4,
        out_shape=[small, large, large, large],
        scratch_shapes=[pltpu.VMEM((EXTRA, width), F32)],
        compiler_params=pltpu.CompilerParams(vmem_limit_bytes=VMEM_BYTES),
        name="pack",
    )(where, counts, dest, coords, patches, values, upstream)


def heads_kernel(patch_len, group, sources, last, where, *refs):
    refs = list(refs)
    take = lambda count: [refs.pop(0) for _ in range(count)]
    own_hbm, other_hbm, table_hbm = take(3)
    near_hbm = [] if last else take(2)
    remote_hbm = take(sources - (not last))
    total_hbm = take(1) if last else []
    context_refs = take(sources)
    results = take(2 if last else 1)
    own_ref, other_ref, table_ref, whole_ref = take(4)
    packed_refs = take(sources)
    full_ref, sum_ref, dproj_ref, values_ref, upstream_ref, arrivals = take(6)
    depth, width = packed_refs[0].shape
    rows = whole_ref.shape[0] // sources
    patches_refs = [whole_ref.at[pl.ds(at * rows, rows), :] for at in range(sources)]
    halves = [[ref.at[:, pl.ds(at * width, width)] for at in range(2)] for ref in patches_refs]
    moves = [(own_hbm, own_ref), (other_hbm, other_ref), (table_hbm, table_ref)]
    waits = [] if last else [[(near_hbm[0], patches_refs[0])], [(near_hbm[1], packed_refs[0])]]
    for at, source_hbm in enumerate(remote_hbm, sources - len(remote_hbm)):
        cut = [source_hbm.at[pl.ds(half * rows, rows), :] for half in range(2)]
        waits.append(list(zip(cut, halves[at])))
        waits.append([(source_hbm.at[pl.ds(2 * rows, depth), :], packed_refs[at])])
    waits = [[move] for move in moves] + waits
    if last:
        waits.append([(total_hbm[0], sum_ref)])
    number = 0
    copies = []
    for moves in waits:
        copies.append([])
        for source, target in moves:
            copy = pltpu.make_async_copy(source, target, arrivals.at[number])
            copy.start()
            copies[-1].append(copy)
            number += 1

    def arrive(at):
        for copy in copies[at]:
            copy.wait()

    strip, strips = own_ref.shape[0], own_ref.shape[1] // (2 * HD)
    block = group * patch_len
    scale = 1.0 / math.sqrt(HD)
    full_ref[...] = jnp.zeros_like(full_ref)
    values_ref[...] = jnp.zeros_like(values_ref)
    upstream_ref[...] = jnp.zeros_like(upstream_ref)
    is_first = where[1] == 0
    arrive(0)
    arrive(1)
    for z in range(strips):
        span = pl.ds(z * strip, strip)
        for part in range(2):
            lanes = pl.ds((2 * z + part) * HD, HD)
            own, other = own_ref[:, lanes], other_ref[:, lanes]
            full_ref[span, pl.ds(part * LANES, HD)] = jnp.where(is_first, own, other)
            full_ref[span, pl.ds((2 + part) * LANES, HD)] = jnp.where(is_first, other, own)
    arrive(2)
    row_win = lax.broadcasted_iota(jnp.int32, (block, block), 0) // patch_len
    key_win = lax.broadcasted_iota(jnp.int32, (block, block), 1) // patch_len
    same = row_win == key_win
    kind = lax.broadcasted_iota(jnp.int32, (3 * POSITIONS, rows), 0)
    wanted = lax.rem(kind, POSITIONS).astype(F32)
    starts = [at for at in range(0, rows, block)]
    chains = [(head, at) for head in range(2) for at in range(len(starts))]
    each = range(len(chains))
    for source in range(sources):
        patches_ref, packed_ref = patches_refs[source], packed_refs[source]
        arrive(3 + 2 * source)
        proj = dot(patches_ref[...], full_ref[...], ((1,), (0,)))
        arrive(4 + 2 * source)
        depth = (packed_ref.shape[0] - EXTRA) // 2
        notes = packed_ref[2 * depth :, :rows].astype(F32)
        live_keys = notes[2:3, :]
        by_row = jnp.where(notes[0:1, :] == wanted, 1.0, 0.0)
        by_col = jnp.where(notes[1:2, :] == wanted, 1.0, 0.0)
        chosen = jnp.where(kind < 2 * POSITIONS, by_col, live_keys)
        chosen = jnp.where(kind < POSITIONS, by_row, chosen).astype(BF16)
        tables = dot(chosen, table_ref[0], ((0,), (0,)))
        tables += dot(chosen, table_ref[1], ((0,), (0,)))
        tables += dot(chosen, table_ref[2], ((0,), (0,)))
        for head in range(2):
            out, come = pl.ds(head * LANES, HD), pl.ds(head * depth, depth)
            for part in range(rows // depth):
                span, at = pl.ds(part * depth, depth), part * 2 * HD
                values_ref[span, out] = packed_ref[come, pl.ds(at, HD)]
                upstream_ref[span, out] = packed_ref[come, pl.ds(at + HD, HD)]
        cosines = [tables[s : s + block, :LANES] for s in starts]
        sines = [tables[s : s + block, LANES:] for s in starts]
        masks = [same & (live_keys[:, s : s + block] > 0.5) for s in starts]
        lives = [cosine[:, HD : HD + 1] for cosine in cosines]
        spans = [pl.ds(starts[at], block) for _, at in chains]
        lanes = [pl.ds(head * LANES, LANES) for head, _ in chains]
        blocks = [at for _, at in chains]
        q = [proj[starts[at] : starts[at] + block, 2 * h * LANES :][:, :LANES] for h, at in chains]
        k = [
            proj[starts[at] : starts[at] + block, (2 * h + 1) * LANES :][:, :LANES]
            for h, at in chains
        ]
        turn = lambda x, at: x * cosines[at] + partner(x) * sines[at]
        q = [turn(q[i], blocks[i]).astype(BF16) for i in each]
        k = [turn(k[i], blocks[i]).astype(BF16) for i in each]
        scores = [dot(q[i], k[i], ((1,), (1,))) * scale for i in each]
        v = [values_ref[spans[i], lanes[i]] for i in each]
        dprobs = [dot(upstream_ref[spans[i], lanes[i]], v[i], ((1,), (1,))) for i in each]
        scores = [jnp.where(masks[blocks[i]], scores[i], -1e30) for i in each]
        tops = [jnp.max(scores[i], axis=1, keepdims=True) for i in each]
        exps = [jnp.exp(scores[i] - tops[i]) for i in each]
        sums = [jnp.sum(exps[i], axis=1, keepdims=True) for i in each]
        probs = [exps[i] * (lives[blocks[i]] / sums[i]) for i in each]
        context = [dot(probs[i].astype(BF16), v[i], ((1,), (0,))) for i in each]
        delta = [jnp.sum(probs[i] * dprobs[i], axis=1, keepdims=True) for i in each]
        dscores = [(probs[i] * (dprobs[i] - delta[i]) * scale).astype(BF16) for i in each]
        dquery = [dot(dscores[i], k[i], ((1,), (0,))) for i in each]
        dkey = [dot(dscores[i], q[i], ((0,), (0,))) for i in each]
        back = lambda x, at: (x * cosines[at] - partner(x) * sines[at]).astype(BF16)
        for i in each:
            context_refs[source][spans[i], lanes[i]] = context[i].astype(BF16)
            at = 2 * chains[i][0] * LANES
            here = pl.ds(source * rows + starts[blocks[i]], block)
            dproj_ref[here, pl.ds(at, LANES)] = back(dquery[i], blocks[i])
            dproj_ref[here, pl.ds(at + LANES, LANES)] = back(dkey[i], blocks[i])
    grown = dot(dproj_ref[...], whole_ref[...], ((0,), (0,)))
    if not last:
        results[0][...] = grown
        return
    arrive(-1)
    sum_ref[...] += grown
    for z in range(strips):
        part = jnp.transpose(sum_ref[:, z * strip : (z + 1) * strip]).astype(BF16)
        for at in range(2):
            low = part[:, at * LANES : at * LANES + HD]
            high = part[:, (2 + at) * LANES : (2 + at) * LANES + HD]
            lanes = pl.ds((2 * z + at) * HD, HD)
            results[0][:, lanes] = jnp.where(is_first, low, high)
            results[1][:, lanes] = jnp.where(is_first, high, low)


def some_heads(where, weights, table, arrays, total, rows, piece, patch_len):
    last = total is not None
    sources = len(arrays) - (not last)
    model_width = weights[0].size // (2 * HD)
    arrays = arrays + ((total,) if last else ())
    moves = 3 + (2 * (not last)) + 3 * (sources - (not last)) + last
    group = math.gcd(rows // patch_len, max(1, 128 // patch_len))
    vmem = pl.BlockSpec(memory_space=pltpu.VMEM)
    hbm = pl.BlockSpec(memory_space=pltpu.HBM)
    grad_shape = jax.ShapeDtypeStruct(weights[0].shape, BF16)
    sum_shape = jax.ShapeDtypeStruct((4 * LANES, model_width), F32)
    return pl.pallas_call(
        functools.partial(heads_kernel, patch_len, group, sources, last),
        in_specs=[pl.BlockSpec(memory_space=pltpu.SMEM)] + [hbm] * (3 + len(arrays)),
        out_specs=[vmem] * (sources + 1 + last),
        out_shape=[jax.ShapeDtypeStruct((rows, 2 * LANES), BF16)] * sources
        + ([grad_shape] * 2 if last else [sum_shape]),
        scratch_shapes=[pltpu.VMEM(weights[0].shape, BF16)] * 2
        + [pltpu.VMEM(table.shape, BF16), pltpu.VMEM((sources * rows, model_width), BF16)]
        + [pltpu.VMEM(piece, BF16)] * sources
        + [
            pltpu.VMEM((model_width, 4 * LANES), BF16),
            pltpu.VMEM((4 * LANES, model_width), F32),
            pltpu.VMEM((sources * rows, 4 * LANES), BF16),
            pltpu.VMEM((rows, 2 * LANES), BF16),
            pltpu.VMEM((rows, 2 * LANES), BF16),
            pltpu.SemaphoreType.DMA((moves,)),
        ],
        compiler_params=pltpu.CompilerParams(vmem_limit_bytes=VMEM_BYTES),
        cost_estimate=pl.CostEstimate(
            flops=5_000_000_000 if last else 1_000,
            bytes_accessed=3_000_000 if last else 1_000,
            transcendentals=800_000 if last else 0,
        ),
        name="heads",
    )(where, *weights, table, *arrays)


def route_kernel(patch_len, slot_of, *refs):
    context_refs, routed_refs, table_ref = refs[:4], refs[4:-1], refs[-1]
    table_ref[...] = jnp.zeros_like(table_ref)
    windows = context_refs[0].shape[0] // patch_len
    for source, context_ref in enumerate(context_refs):
        for window in range(windows):
            slot = slot_of[source * windows + window]
            rows = context_ref[pl.ds(window * patch_len, patch_len), :]
            for head in range(2):
                lanes = pl.ds((2 * source + head) * HD, HD)
                table_ref[slot, :, lanes] = rows[:, head * LANES : head * LANES + HD]
    for at, routed_ref in enumerate(routed_refs):
        count = routed_ref.shape[0]
        routed_ref[...] = table_ref[pl.ds(at * count, count)]


def route(slot_of, contexts, slots, patch_len):
    count = len(contexts)
    vmem = pl.BlockSpec(memory_space=pltpu.VMEM)
    shape = (patch_len, 2 * HD * count)
    return pl.pallas_call(
        functools.partial(route_kernel, patch_len),
        in_specs=[pl.BlockSpec(memory_space=pltpu.SMEM)] + [vmem] * count,
        out_specs=[vmem] * count,
        out_shape=[jax.ShapeDtypeStruct((slots // count,) + shape, BF16)] * count,
        scratch_shapes=[pltpu.VMEM((slots,) + shape, BF16)],
        compiler_params=pltpu.CompilerParams(vmem_limit_bytes=VMEM_BYTES),
        name="route",
    )(slot_of, *contexts)


def regroup_kernel(count, where, *refs):
    inputs, outputs = refs[:count], refs[count:]
    copies = len(outputs) // 2
    for step in range(copies):
        target = lax.rem(where[2] + step, copies)
        for swap in range(2):
            core = where[1] if swap == 0 else 1 - where[1]
            for at, ref in enumerate(inputs):
                outputs[2 * step + swap][at] = ref[2 * target + core]


def regroup(where, pieces):
    slots, patch_len, width = pieces[0].shape
    vmem = pl.BlockSpec(memory_space=pltpu.VMEM)
    piece = jax.ShapeDtypeStruct((len(pieces), patch_len, width), BF16)
    return pl.pallas_call(
        functools.partial(regroup_kernel, len(pieces)),
        in_specs=[pl.BlockSpec(memory_space=pltpu.SMEM)] + [vmem] * len(pieces),
        out_specs=[vmem] * slots,
        out_shape=[piece] * slots,
        compiler_params=pltpu.CompilerParams(vmem_limit_bytes=VMEM_BYTES),
        name="regroup",
    )(where, *pieces)


def hop(array, step, swap):
    copies, cores = lax.axis_size("zl"), lax.axis_size("c")
    if step == 0 and swap == 0:
        return array
    pairs = [
        (z * cores + c, (z + step) % copies * cores + (c + swap) % cores)
        for z in range(copies)
        for c in range(cores)
    ]
    return lax.ppermute(array, ("zl", "c"), pairs)


def settle_kernel(where, places, *refs):
    arrived_refs, placed_ref = refs[:-1], refs[-1]
    copies, nx = len(arrived_refs) // 2, arrived_refs[0].shape[0]
    steps = ring_steps(nx)
    for step in range(copies):
        copy = lax.rem(where[2] + copies - step, copies)
        for swap in range(2):
            core = where[1] if swap == 0 else 1 - where[1]
            for sender in range(nx):
                at = places[sender]
                for source in range(nx):
                    lane = 2 * steps.index((sender - source) % nx)
                    slot = (copy * nx + source) * 2 + core
                    for kind in range(2):
                        here = pl.ds((lane + kind) * HD, HD)
                        rows = arrived_refs[2 * step + swap][at, :, here]
                        placed_ref[slot, :, pl.ds((kind * nx + sender) * HD, HD)] = rows


def settle(where, places, arrived):
    nx, patch_len, width = arrived[0].shape
    vmem = pl.BlockSpec(memory_space=pltpu.VMEM)
    smem = pl.BlockSpec(memory_space=pltpu.SMEM)
    return pl.pallas_call(
        settle_kernel,
        in_specs=[smem, smem] + [vmem] * len(arrived),
        out_specs=vmem,
        out_shape=jax.ShapeDtypeStruct((len(arrived) * nx, patch_len, width), BF16),
        compiler_params=pltpu.CompilerParams(vmem_limit_bytes=VMEM_BYTES),
        name="settle",
    )(where, places, *arrived)


def finish_kernel(cores, arrived_ref, grad_ref):
    heads = arrived_ref.shape[0]
    for place in range(heads):
        head = head_of(place, cores, heads)
        part = arrived_ref[place].astype(F32)
        grad_ref[:, pl.ds(head * HD, HD)] = part[:, :HD]
        grad_ref[:, pl.ds((heads + head) * HD, HD)] = part[:, HD:]


def finish(arrived, cores):
    heads, depth, width = arrived.shape
    vmem = pl.BlockSpec(memory_space=pltpu.VMEM)
    return pl.pallas_call(
        functools.partial(finish_kernel, cores),
        in_specs=[vmem],
        out_specs=vmem,
        out_shape=jax.ShapeDtypeStruct((depth, heads * width), F32),
        compiler_params=pltpu.CompilerParams(vmem_limit_bytes=VMEM_BYTES),
        name="finish",
    )(arrived)


def rotary_table():
    quarter = HD // 4
    lane = jnp.arange(LANES, dtype=jnp.int32)[None, :]
    kind = jnp.arange(3 * POSITIONS, dtype=jnp.int32)[:, None]
    frequency = 10000.0 ** (-(lane % quarter).astype(F32) / quarter)
    angles = (kind % POSITIONS).astype(F32) * frequency
    by_row = (kind < POSITIONS) & (lane < HD // 2)
    by_col = (kind >= POSITIONS) & (kind < 2 * POSITIONS) & (lane >= HD // 2) & (lane < HD)
    used = by_row | by_col
    flag = (kind == 2 * POSITIONS) & (lane == HD)
    cosine = jnp.where(used, jnp.cos(angles), jnp.where(flag, 1.0, 0.0))
    left = jnp.concatenate([cosine, jnp.where(used, jnp.sin(angles), 0.0)], axis=1)
    terms = []
    for _ in range(3):
        term = lax.reduce_precision(left, 8, 7)
        terms.append(term.astype(BF16))
        left = left - term
    return jnp.stack(terms)


def per_device(patches, values, upstream, coords, counts, dest, weight):
    core, here, copy = lax.axis_index("c"), lax.axis_index("x"), lax.axis_index("zl")
    nx, nc, copies = lax.axis_size("x"), lax.axis_size("c"), lax.axis_size("zl")
    ny, nz = lax.axis_size("y"), lax.axis_size("zh")
    heads = nx * nc
    slots = lax.axis_size(PEERS)
    window_count, patch_len, model_width = patches.shape
    value_width = values.shape[-1]
    row_total = window_count * patch_len
    depth = weight.shape[0]

    where = jnp.stack([here, core, copy]).astype(jnp.int32)
    steps = ring_steps(nx)
    patches = patches.reshape(row_total, model_width)
    values = values.reshape(row_total, value_width)
    upstream = upstream.reshape(row_total, value_width)
    own, left, right, far = pack(where, counts, dest, coords, patches, values, upstream, nx)
    left, right = ring(left, "x", steps[1]), ring(right, "x", steps[2])

    head = core * nx + here
    slice_q = lax.dynamic_slice_in_dim(weight, head * HD, HD, axis=1)
    slice_k = lax.dynamic_slice_in_dim(weight, value_width + head * HD, HD, axis=1)
    own_w = jnp.concatenate([slice_q, slice_k], axis=1)
    own_w = spread(own_w, "zh")
    far = ring(after(own_w, far), "x", steps[3])
    own_w = jnp.transpose(own_w, (1, 0, 2)).reshape(depth, nz * 2 * HD)
    own_w = spread(own_w, "y").reshape(ny * depth, nz * 2 * HD)
    weights = (own_w, core_swap(own_w))

    table = rotary_table()
    *contexts, total = some_heads(
        where,
        weights,
        table,
        (patches, own, left, right),
        None,
        row_total,
        own.shape,
        patch_len,
    )
    far = after(total, far)
    all_dest = [dest[:, 0]]
    for piece in (left, right, far):
        at = piece.shape[0] - EXTRA + 3
        all_dest.append(piece[at, :window_count].astype(jnp.int32))
    all_dest = jnp.concatenate(all_dest)
    step_of = lax.rem(all_dest // nc + nx - here, nx)
    slot_of = jnp.zeros_like(step_of)
    for at, step in enumerate(steps):
        slot_of = jnp.where(step_of == step, at, slot_of)
    slot_of = (slot_of * copies + all_dest // (nc * nx)) * nc + lax.rem(all_dest, nc)

    context, grad, sent = some_heads(
        where, weights, table, (far,), total, row_total, own.shape, patch_len
    )
    contexts = contexts + [context]
    grad = (grad.astype(F32) + core_swap(sent).astype(F32)).astype(BF16)
    pieces = route(slot_of, contexts, slots, patch_len)
    grad = after(pieces, grad)
    pieces = [ring(piece, "x", step) for piece, step in zip(pieces, steps)]
    crossed = pieces
    pieces = regroup(where, pieces)
    pieces = [hop(piece, at // 2, at % 2) for at, piece in enumerate(pieces)]
    places = [lax.rem(here - sender + nx, nx) for sender in range(nx)]
    places = [sum(jnp.where(at == steps[k], k, 0) for k in range(nx)) for at in places]
    places = jnp.stack(places).astype(jnp.int32)
    placed = settle(where, places, pieces)

    grad = exchange(grad.reshape(ny, depth, nz * 2 * HD), "y")
    grad = jnp.sum(grad.astype(F32), axis=0).astype(BF16)
    grad = jnp.transpose(grad.reshape(depth, nz, 2 * HD), (1, 0, 2))
    grad = jnp.broadcast_to(after(crossed, grad)[None], (copies,) + grad.shape)
    grad = exchange(grad.reshape(copies * nz, depth, 2 * HD), ("zl", "zh"))
    grad = jnp.sum(grad.astype(F32), axis=0).astype(BF16)
    return (placed, finish(spread(grad, ("x", "c")), nc))


def solution(mesh):
    fine = Mesh(mesh.devices.reshape(SPLIT), AXES)
    return jax.shard_map(
        per_device,
        mesh=fine,
        in_specs=(
            P(AXES, None, None),
            P(AXES, None, None),
            P(AXES, None, None),
            P(AXES, None, None),
            P(AXES),
            P(AXES, None),
            P(("zh", "y"), None),
        ),
        out_specs=(P(AXES, None, None), P(("zh", "y"), None)),
        check_vma=False,
    )
```

```python
import functools
import math

import jax
import jax.numpy as jnp
from jax import lax
from jax.experimental import pallas as pl
from jax.experimental.pallas import tpu as pltpu
from jax.sharding import Mesh
from jax.sharding import PartitionSpec as P

HD = 80
LANES = 128
POSITIONS = 32
EXTRA = 16
SPLIT = (3, 4, 2, 4, 8)
AXES = ("zl", "x", "c", "zh", "y")
PEERS = ("zl", "x", "c")
BF16 = jnp.bfloat16
F32 = jnp.float32
VMEM_BYTES = 60 * 1024 * 1024


def core_swap(array):
    return lax.ppermute(array, "c", [(0, 1), (1, 0)])


def ring(array, axis, step):
    count = lax.axis_size(axis)
    if step == 0:
        return array
    return lax.ppermute(array, axis, [(i, (i + step) % count) for i in range(count)])


def exchange(array, axes):
    return lax.all_to_all(array, axes, split_axis=0, concat_axis=0, tiled=True)


def spread(array, axes):
    count = lax.axis_size(axes)
    return exchange(jnp.broadcast_to(array[None], (count,) + array.shape), axes)


def after(first, arrays):
    return lax.optimization_barrier((first, arrays))[1]


def dot(a, b, dims):
    return lax.dot_general(a, b, (dims, ((), ())), preferred_element_type=F32)


def head_of(place, cores, heads):
    return place % cores * (heads // cores) + place // cores


def partner(array):
    quarter = HD // 4
    lane = lax.broadcasted_iota(jnp.int32, array.shape, 1)
    front = lax.rem(lane, 2 * quarter) < quarter
    ahead = pltpu.roll(array, LANES - quarter, 1)
    behind = pltpu.roll(array, quarter, 1)
    return jnp.where(front, -ahead, behind)


def ring_steps(count):
    return [0, count - 1, 1] + list(range(2, count - 1))


def pack_kernel(
    where,
    counts,
    dest,
    coords_ref,
    patches_ref,
    values_ref,
    upstream_ref,
    own_ref,
    left_ref,
    right_ref,
    far_ref,
    notes_ref,
):
    packed_refs = (own_ref, left_ref, right_ref, far_ref)
    count = len(packed_refs)
    steps = ring_steps(count)
    rows, width = values_ref.shape
    windows, _, patch_len = coords_ref.shape
    lane = lax.broadcasted_iota(jnp.int32, (1, width), 1)
    live = jnp.zeros((1, width), jnp.int32)
    slot = jnp.zeros((1, width), jnp.int32)
    notes_ref[...] = jnp.zeros_like(notes_ref)
    for window in range(windows):
        at = window * patch_len
        for axis in range(2):
            coord = coords_ref[window, axis : axis + 1, :].astype(F32)
            notes_ref[axis : axis + 1, at : at + patch_len] = coord
        live = jnp.where((lane >= at) & (lane < at + counts[window]), 1, live)
        slot = jnp.where(lane == window, dest[window, 0], slot)
    notes_ref[2:3, :] = live.astype(F32)
    notes_ref[3:4, :] = slot.astype(F32)
    for packed_ref in (left_ref, right_ref):
        packed_ref[:rows, :] = patches_ref[:, :width]
        packed_ref[rows : 2 * rows, :] = patches_ref[:, width:]
    parts = width // (2 * HD)
    depth = rows // parts
    kinds = width // HD // count
    tops = [ref.shape[0] - EXTRA - kinds * depth for ref in packed_refs]
    for here in range(count):

        @pl.when(where[0] == here)
        def _():
            for packed_ref, step, top in zip(packed_refs, steps, tops):
                for kind in range(kinds):
                    head = kind * count + (here + step) % count
                    lanes = pl.ds(head * HD, HD)
                    for part in range(parts):
                        span, at = pl.ds(part * depth, depth), part * 2 * HD
                        out = pl.ds(top + kind * depth, depth)
                        packed_ref[out, pl.ds(at, HD)] = values_ref[span, lanes]
                        packed_ref[out, pl.ds(at + HD, HD)] = upstream_ref[span, lanes]

    notes = notes_ref[...].astype(BF16)
    for packed_ref in packed_refs:
        packed_ref[packed_ref.shape[0] - EXTRA :, :] = notes


def pack(where, counts, dest, coords, patches, values, upstream, count):
    rows, width = values.shape
    depth = width // HD // count * rows // (width // (2 * HD)) + EXTRA
    vmem = pl.BlockSpec(memory_space=pltpu.VMEM)
    smem = pl.BlockSpec(memory_space=pltpu.SMEM)
    small = jax.ShapeDtypeStruct((depth, width), BF16)
    large = jax.ShapeDtypeStruct((2 * rows + depth, width), BF16)
    return pl.pallas_call(
        pack_kernel,
        in_specs=[smem] * 3 + [vmem] * 4,
        out_specs=[vmem] * 4,
        out_shape=[small, large, large, small],
        scratch_shapes=[pltpu.VMEM((EXTRA, width), F32)],
        compiler_params=pltpu.CompilerParams(vmem_limit_bytes=VMEM_BYTES),
        name="pack",
    )(where, counts, dest, coords, patches, values, upstream)


def heads_kernel(patch_len, group, where, *refs):
    refs = list(refs)
    take = lambda count: [refs.pop(0) for _ in range(count)]
    own_hbm, other_hbm, table_hbm, patches_hbm, packed_hbm = take(5)
    left_hbm, right_hbm, low_hbm, high_hbm, far_hbm = take(5)
    context_refs = take(4)
    results = take(2)
    own_ref, other_ref, table_ref, whole_ref = take(4)
    packed_refs = take(4)
    full_ref, sum_ref, dproj_ref, values_ref, upstream_ref, arrivals = take(6)
    sources = len(packed_refs)
    rows, width = patches_hbm.shape[0], packed_hbm.shape[1]
    depth = packed_hbm.shape[0]
    patches_refs = [whole_ref.at[pl.ds(at * rows, rows), :] for at in range(sources)]
    halves = [[ref.at[:, pl.ds(at * width, width)] for at in range(2)] for ref in patches_refs]
    moves = [(own_hbm, own_ref), (other_hbm, other_ref), (table_hbm, table_ref)]
    waits = [[(patches_hbm, patches_refs[0])], [(packed_hbm, packed_refs[0])]]
    for at, source_hbm in ((1, left_hbm), (2, right_hbm)):
        cut = [source_hbm.at[pl.ds(half * rows, rows), :] for half in range(2)]
        waits.append(list(zip(cut, halves[at])))
        waits.append([(source_hbm.at[pl.ds(2 * rows, depth), :], packed_refs[at])])
    waits.append([(low_hbm, halves[3][0]), (high_hbm, halves[3][1])])
    waits.append([(far_hbm, packed_refs[3])])
    waits = [[move] for move in moves] + waits
    number = 0
    copies = []
    for moves in waits:
        copies.append([])
        for source, target in moves:
            copy = pltpu.make_async_copy(source, target, arrivals.at[number])
            copy.start()
            copies[-1].append(copy)
            number += 1

    def arrive(at):
        for copy in copies[at]:
            copy.wait()

    strip, strips = own_ref.shape[0], own_ref.shape[1] // (2 * HD)
    block = group * patch_len
    scale = 1.0 / math.sqrt(HD)
    full_ref[...] = jnp.zeros_like(full_ref)
    values_ref[...] = jnp.zeros_like(values_ref)
    upstream_ref[...] = jnp.zeros_like(upstream_ref)
    is_first = where[1] == 0
    arrive(0)
    arrive(1)
    for z in range(strips):
        span = pl.ds(z * strip, strip)
        for part in range(2):
            lanes = pl.ds((2 * z + part) * HD, HD)
            own, other = own_ref[:, lanes], other_ref[:, lanes]
            full_ref[span, pl.ds(part * LANES, HD)] = jnp.where(is_first, own, other)
            full_ref[span, pl.ds((2 + part) * LANES, HD)] = jnp.where(is_first, other, own)
    arrive(2)
    row_win = lax.broadcasted_iota(jnp.int32, (block, block), 0) // patch_len
    key_win = lax.broadcasted_iota(jnp.int32, (block, block), 1) // patch_len
    same = row_win == key_win
    kind = lax.broadcasted_iota(jnp.int32, (3 * POSITIONS, rows), 0)
    wanted = lax.rem(kind, POSITIONS).astype(F32)
    starts = [at for at in range(0, rows, block)]
    chains = [(head, at) for head in range(2) for at in range(len(starts))]
    each = range(len(chains))
    for source in range(sources):
        patches_ref, packed_ref = patches_refs[source], packed_refs[source]
        arrive(3 + 2 * source)
        proj = dot(patches_ref[...], full_ref[...], ((1,), (0,)))
        arrive(4 + 2 * source)
        depth = (packed_ref.shape[0] - EXTRA) // 2
        notes = packed_ref[2 * depth :, :rows].astype(F32)
        live_keys = notes[2:3, :]
        by_row = jnp.where(notes[0:1, :] == wanted, 1.0, 0.0)
        by_col = jnp.where(notes[1:2, :] == wanted, 1.0, 0.0)
        chosen = jnp.where(kind < 2 * POSITIONS, by_col, live_keys)
        chosen = jnp.where(kind < POSITIONS, by_row, chosen).astype(BF16)
        tables = dot(chosen, table_ref[0], ((0,), (0,)))
        tables += dot(chosen, table_ref[1], ((0,), (0,)))
        tables += dot(chosen, table_ref[2], ((0,), (0,)))
        for head in range(2):
            out, come = pl.ds(head * LANES, HD), pl.ds(head * depth, depth)
            for part in range(rows // depth):
                span, at = pl.ds(part * depth, depth), part * 2 * HD
                values_ref[span, out] = packed_ref[come, pl.ds(at, HD)]
                upstream_ref[span, out] = packed_ref[come, pl.ds(at + HD, HD)]
        cosines = [tables[s : s + block, :LANES] for s in starts]
        sines = [tables[s : s + block, LANES:] for s in starts]
        masks = [same & (live_keys[:, s : s + block] > 0.5) for s in starts]
        lives = [cosine[:, HD : HD + 1] for cosine in cosines]
        spans = [pl.ds(starts[at], block) for _, at in chains]
        lanes = [pl.ds(head * LANES, LANES) for head, _ in chains]
        blocks = [at for _, at in chains]
        q = [proj[starts[at] : starts[at] + block, 2 * h * LANES :][:, :LANES] for h, at in chains]
        k = [
            proj[starts[at] : starts[at] + block, (2 * h + 1) * LANES :][:, :LANES]
            for h, at in chains
        ]
        turn = lambda x, at: x * cosines[at] + partner(x) * sines[at]
        q = [turn(q[i], blocks[i]).astype(BF16) for i in each]
        k = [turn(k[i], blocks[i]).astype(BF16) for i in each]
        scores = [dot(q[i], k[i], ((1,), (1,))) * scale for i in each]
        v = [values_ref[spans[i], lanes[i]] for i in each]
        dprobs = [dot(upstream_ref[spans[i], lanes[i]], v[i], ((1,), (1,))) for i in each]
        scores = [jnp.where(masks[blocks[i]], scores[i], -1e30) for i in each]
        tops = [jnp.max(scores[i], axis=1, keepdims=True) for i in each]
        exps = [jnp.exp(scores[i] - tops[i]) for i in each]
        sums = [jnp.sum(exps[i], axis=1, keepdims=True) for i in each]
        probs = [exps[i] * (lives[blocks[i]] / sums[i]) for i in each]
        context = [dot(probs[i].astype(BF16), v[i], ((1,), (0,))) for i in each]
        delta = [jnp.sum(probs[i] * dprobs[i], axis=1, keepdims=True) for i in each]
        dscores = [(probs[i] * (dprobs[i] - delta[i]) * scale).astype(BF16) for i in each]
        dquery = [dot(dscores[i], k[i], ((1,), (0,))) for i in each]
        dkey = [dot(dscores[i], q[i], ((0,), (0,))) for i in each]
        back = lambda x, at: (x * cosines[at] - partner(x) * sines[at]).astype(BF16)
        for i in each:
            context_refs[source][spans[i], lanes[i]] = context[i].astype(BF16)
            at = 2 * chains[i][0] * LANES
            here = pl.ds(source * rows + starts[blocks[i]], block)
            dproj_ref[here, pl.ds(at, LANES)] = back(dquery[i], blocks[i])
            dproj_ref[here, pl.ds(at + LANES, LANES)] = back(dkey[i], blocks[i])
    sum_ref[...] = dot(dproj_ref[...], whole_ref[...], ((0,), (0,)))
    for z in range(strips):
        part = jnp.transpose(sum_ref[:, z * strip : (z + 1) * strip]).astype(BF16)
        for at in range(2):
            low = part[:, at * LANES : at * LANES + HD]
            high = part[:, (2 + at) * LANES : (2 + at) * LANES + HD]
            lanes = pl.ds((2 * z + at) * HD, HD)
            results[0][:, lanes] = jnp.where(is_first, low, high)
            results[1][:, lanes] = jnp.where(is_first, high, low)


def some_heads(where, weights, table, arrays, patch_len):
    rows, model_width = arrays[0].shape
    piece = arrays[1].shape
    group = math.gcd(rows // patch_len, max(1, 128 // patch_len))
    vmem = pl.BlockSpec(memory_space=pltpu.VMEM)
    hbm = pl.BlockSpec(memory_space=pltpu.HBM)
    grad_shape = jax.ShapeDtypeStruct(weights[0].shape, BF16)
    return pl.pallas_call(
        functools.partial(heads_kernel, patch_len, group),
        in_specs=[pl.BlockSpec(memory_space=pltpu.SMEM)] + [hbm] * (3 + len(arrays)),
        out_specs=[vmem] * 6,
        out_shape=[jax.ShapeDtypeStruct((rows, 2 * LANES), BF16)] * 4 + [grad_shape] * 2,
        scratch_shapes=[pltpu.VMEM(weights[0].shape, BF16)] * 2
        + [pltpu.VMEM(table.shape, BF16), pltpu.VMEM((4 * rows, model_width), BF16)]
        + [pltpu.VMEM(piece, BF16)] * 4
        + [
            pltpu.VMEM((model_width, 4 * LANES), BF16),
            pltpu.VMEM((4 * LANES, model_width), F32),
            pltpu.VMEM((4 * rows, 4 * LANES), BF16),
            pltpu.VMEM((rows, 2 * LANES), BF16),
            pltpu.VMEM((rows, 2 * LANES), BF16),
            pltpu.SemaphoreType.DMA((14,)),
        ],
        compiler_params=pltpu.CompilerParams(vmem_limit_bytes=VMEM_BYTES),
        cost_estimate=pl.CostEstimate(
            flops=20_000_000_000, bytes_accessed=12_000_000, transcendentals=3_000_000
        ),
        name="heads",
    )(where, *weights, table, *arrays)


def route_kernel(patch_len, slot_of, *refs):
    context_refs, routed_refs, table_ref = refs[:4], refs[4:-1], refs[-1]
    table_ref[...] = jnp.zeros_like(table_ref)
    windows = context_refs[0].shape[0] // patch_len
    for source, context_ref in enumerate(context_refs):
        for window in range(windows):
            slot = slot_of[source * windows + window]
            rows = context_ref[pl.ds(window * patch_len, patch_len), :]
            for head in range(2):
                lanes = pl.ds((2 * source + head) * HD, HD)
                table_ref[slot, :, lanes] = rows[:, head * LANES : head * LANES + HD]
    for at, routed_ref in enumerate(routed_refs):
        count = routed_ref.shape[0]
        routed_ref[...] = table_ref[pl.ds(at * count, count)]


def route(slot_of, contexts, slots, patch_len):
    count = len(contexts)
    vmem = pl.BlockSpec(memory_space=pltpu.VMEM)
    shape = (patch_len, 2 * HD * count)
    return pl.pallas_call(
        functools.partial(route_kernel, patch_len),
        in_specs=[pl.BlockSpec(memory_space=pltpu.SMEM)] + [vmem] * count,
        out_specs=[vmem] * count,
        out_shape=[jax.ShapeDtypeStruct((slots // count,) + shape, BF16)] * count,
        scratch_shapes=[pltpu.VMEM((slots,) + shape, BF16)],
        compiler_params=pltpu.CompilerParams(vmem_limit_bytes=VMEM_BYTES),
        name="route",
    )(slot_of, *contexts)


def regroup_kernel(count, where, *refs):
    inputs, outputs = refs[:count], refs[count:]
    copies = len(outputs) // 2
    for step in range(copies):
        target = lax.rem(where[2] + step, copies)
        for swap in range(2):
            core = where[1] if swap == 0 else 1 - where[1]
            for at, ref in enumerate(inputs):
                outputs[2 * step + swap][at] = ref[2 * target + core]


def regroup(where, pieces):
    slots, patch_len, width = pieces[0].shape
    vmem = pl.BlockSpec(memory_space=pltpu.VMEM)
    piece = jax.ShapeDtypeStruct((len(pieces), patch_len, width), BF16)
    return pl.pallas_call(
        functools.partial(regroup_kernel, len(pieces)),
        in_specs=[pl.BlockSpec(memory_space=pltpu.SMEM)] + [vmem] * len(pieces),
        out_specs=[vmem] * slots,
        out_shape=[piece] * slots,
        compiler_params=pltpu.CompilerParams(vmem_limit_bytes=VMEM_BYTES),
        name="regroup",
    )(where, *pieces)


def hop(array, step, swap):
    copies, cores = lax.axis_size("zl"), lax.axis_size("c")
    if step == 0 and swap == 0:
        return array
    pairs = [
        (z * cores + c, (z + step) % copies * cores + (c + swap) % cores)
        for z in range(copies)
        for c in range(cores)
    ]
    return lax.ppermute(array, ("zl", "c"), pairs)


def keep_kernel(source_ref, target_ref):
    target_ref[...] = source_ref[...]


def keep(array):
    vmem = pl.BlockSpec(memory_space=pltpu.VMEM)
    return pl.pallas_call(
        keep_kernel,
        in_specs=[vmem],
        out_specs=vmem,
        out_shape=jax.ShapeDtypeStruct(array.shape, array.dtype),
        compiler_params=pltpu.CompilerParams(vmem_limit_bytes=VMEM_BYTES),
        cost_estimate=pl.CostEstimate(
            flops=30_000_000_000, bytes_accessed=2_000_000, transcendentals=0
        ),
        name="keep",
    )(array)


def settle_kernel(where, places, *refs):
    arrived_refs, placed_ref = refs[:-1], refs[-1]
    copies, nx = len(arrived_refs) // 2, arrived_refs[0].shape[0]
    steps = ring_steps(nx)
    for step in range(copies):
        copy = lax.rem(where[2] + copies - step, copies)
        for swap in range(2):
            core = where[1] if swap == 0 else 1 - where[1]
            for sender in range(nx):
                at = places[sender]
                for source in range(nx):
                    lane = 2 * steps.index((sender - source) % nx)
                    slot = (copy * nx + source) * 2 + core
                    for kind in range(2):
                        here = pl.ds((lane + kind) * HD, HD)
                        rows = arrived_refs[2 * step + swap][at, :, here]
                        placed_ref[slot, :, pl.ds((kind * nx + sender) * HD, HD)] = rows


def settle(where, places, arrived):
    nx, patch_len, width = arrived[0].shape
    vmem = pl.BlockSpec(memory_space=pltpu.VMEM)
    smem = pl.BlockSpec(memory_space=pltpu.SMEM)
    return pl.pallas_call(
        settle_kernel,
        in_specs=[smem, smem] + [vmem] * len(arrived),
        out_specs=vmem,
        out_shape=jax.ShapeDtypeStruct((len(arrived) * nx, patch_len, width), BF16),
        compiler_params=pltpu.CompilerParams(vmem_limit_bytes=VMEM_BYTES),
        name="settle",
    )(where, places, *arrived)


def finish_kernel(cores, arrived_ref, grad_ref):
    heads = arrived_ref.shape[0]
    for place in range(heads):
        head = head_of(place, cores, heads)
        part = arrived_ref[place].astype(F32)
        grad_ref[:, pl.ds(head * HD, HD)] = part[:, :HD]
        grad_ref[:, pl.ds((heads + head) * HD, HD)] = part[:, HD:]


def finish(arrived, cores):
    heads, depth, width = arrived.shape
    vmem = pl.BlockSpec(memory_space=pltpu.VMEM)
    return pl.pallas_call(
        functools.partial(finish_kernel, cores),
        in_specs=[vmem],
        out_specs=vmem,
        out_shape=jax.ShapeDtypeStruct((depth, heads * width), F32),
        compiler_params=pltpu.CompilerParams(vmem_limit_bytes=VMEM_BYTES),
        name="finish",
    )(arrived)


def rotary_table():
    quarter = HD // 4
    lane = jnp.arange(LANES, dtype=jnp.int32)[None, :]
    kind = jnp.arange(3 * POSITIONS, dtype=jnp.int32)[:, None]
    frequency = 10000.0 ** (-(lane % quarter).astype(F32) / quarter)
    angles = (kind % POSITIONS).astype(F32) * frequency
    by_row = (kind < POSITIONS) & (lane < HD // 2)
    by_col = (kind >= POSITIONS) & (kind < 2 * POSITIONS) & (lane >= HD // 2) & (lane < HD)
    used = by_row | by_col
    flag = (kind == 2 * POSITIONS) & (lane == HD)
    cosine = jnp.where(used, jnp.cos(angles), jnp.where(flag, 1.0, 0.0))
    left = jnp.concatenate([cosine, jnp.where(used, jnp.sin(angles), 0.0)], axis=1)
    terms = []
    for _ in range(3):
        term = lax.reduce_precision(left, 8, 7)
        terms.append(term.astype(BF16))
        left = left - term
    return jnp.stack(terms)


def per_device(patches, values, upstream, coords, counts, dest, weight):
    core, here, copy = lax.axis_index("c"), lax.axis_index("x"), lax.axis_index("zl")
    nx, nc, copies = lax.axis_size("x"), lax.axis_size("c"), lax.axis_size("zl")
    ny, nz = lax.axis_size("y"), lax.axis_size("zh")
    heads = nx * nc
    slots = lax.axis_size(PEERS)
    window_count, patch_len, model_width = patches.shape
    value_width = values.shape[-1]
    row_total = window_count * patch_len
    depth = weight.shape[0]

    head = core * nx + here
    slice_q = lax.dynamic_slice_in_dim(weight, head * HD, HD, axis=1)
    slice_k = lax.dynamic_slice_in_dim(weight, value_width + head * HD, HD, axis=1)
    own_w = jnp.concatenate([slice_q, slice_k], axis=1)
    own_w = jnp.broadcast_to(own_w[None], (nz,) + own_w.shape)
    patches = after(own_w, patches)
    where = jnp.stack([here, core, copy]).astype(jnp.int32)
    steps = ring_steps(nx)
    patches = patches.reshape(row_total, model_width)
    values = values.reshape(row_total, value_width)
    upstream = upstream.reshape(row_total, value_width)
    own, left, right, far = pack(where, counts, dest, coords, patches, values, upstream, nx)
    left, right = ring(left, "x", steps[1]), ring(right, "x", steps[2])

    own_w = exchange(own_w, "zh")
    far = ring(after(own_w, far), "x", steps[3])
    own_w = jnp.transpose(own_w, (1, 0, 2)).reshape(depth, nz * 2 * HD)
    own_w = spread(own_w, "y").reshape(ny * depth, nz * 2 * HD)
    own_w = keep(own_w)
    weights = (own_w, core_swap(own_w))
    low = ring(right[:row_total], "x", steps[2])
    high = ring(left[row_total : 2 * row_total], "x", steps[1])

    all_dest = [dest[:, 0]]
    for piece in (left, right, far):
        at = piece.shape[0] - EXTRA + 3
        all_dest.append(piece[at, :window_count].astype(jnp.int32))
    all_dest = jnp.concatenate(all_dest)
    step_of = lax.rem(all_dest // nc + nx - here, nx)
    slot_of = jnp.zeros_like(step_of)
    for at, step in enumerate(steps):
        slot_of = jnp.where(step_of == step, at, slot_of)
    slot_of = (slot_of * copies + all_dest // (nc * nx)) * nc + lax.rem(all_dest, nc)

    *contexts, grad, sent = some_heads(
        after(slot_of, where),
        weights,
        rotary_table(),
        (patches, own, left, right, low, high, far),
        patch_len,
    )
    grad = (grad.astype(F32) + core_swap(sent).astype(F32)).astype(BF16)
    pieces = route(slot_of, contexts, slots, patch_len)
    grad = after(pieces, grad)
    pieces = [ring(piece, "x", step) for piece, step in zip(pieces, steps)]
    crossed = pieces
    pieces = regroup(where, pieces)
    pieces = [hop(piece, at // 2, at % 2) for at, piece in enumerate(pieces)]
    places = [lax.rem(here - sender + nx, nx) for sender in range(nx)]
    places = [sum(jnp.where(at == steps[k], k, 0) for k in range(nx)) for at in places]
    places = jnp.stack(places).astype(jnp.int32)
    placed = settle(where, places, pieces)

    grad = exchange(grad.reshape(ny, depth, nz * 2 * HD), "y")
    grad = jnp.sum(grad.astype(F32), axis=0).astype(BF16)
    grad = jnp.transpose(grad.reshape(depth, nz, 2 * HD), (1, 0, 2))
    grad = jnp.broadcast_to(after(crossed, grad)[None], (copies,) + grad.shape)
    grad = exchange(grad.reshape(copies * nz, depth, 2 * HD), ("zl", "zh"))
    grad = jnp.sum(grad.astype(F32), axis=0).astype(BF16)
    return (placed, finish(spread(grad, ("x", "c")), nc))


def solution(mesh):
    fine = Mesh(mesh.devices.reshape(SPLIT), AXES)
    return jax.shard_map(
        per_device,
        mesh=fine,
        in_specs=(
            P(AXES, None, None),
            P(AXES, None, None),
            P(AXES, None, None),
            P(AXES, None, None),
            P(AXES),
            P(AXES, None),
            P(("zh", "y"), None),
        ),
        out_specs=(P(AXES, None, None), P(("zh", "y"), None)),
        check_vma=False,
    )
```

```python
import functools
import math

import jax
import jax.numpy as jnp
from jax import lax
from jax.experimental import pallas as pl
from jax.experimental.pallas import tpu as pltpu
from jax.sharding import Mesh
from jax.sharding import PartitionSpec as P

HD = 80
LANES = 128
POSITIONS = 32
EXTRA = 16
SPLIT = (3, 4, 2, 4, 8)
AXES = ("zl", "x", "c", "zh", "y")
PEERS = ("zl", "x", "c")
BF16 = jnp.bfloat16
F32 = jnp.float32
VMEM_BYTES = 60 * 1024 * 1024


def core_swap(array):
    return lax.ppermute(array, "c", [(0, 1), (1, 0)])


def ring(array, axis, step):
    count = lax.axis_size(axis)
    if step == 0:
        return array
    return lax.ppermute(array, axis, [(i, (i + step) % count) for i in range(count)])


def exchange(array, axes):
    return lax.all_to_all(array, axes, split_axis=0, concat_axis=0, tiled=True)


def spread(array, axes):
    count = lax.axis_size(axes)
    return exchange(jnp.broadcast_to(array[None], (count,) + array.shape), axes)


def after(first, arrays):
    return lax.optimization_barrier((first, arrays))[1]


def dot(a, b, dims):
    return lax.dot_general(a, b, (dims, ((), ())), preferred_element_type=F32)


def head_of(place, cores, heads):
    return place % cores * (heads // cores) + place // cores


def partner(array):
    quarter = HD // 4
    lane = lax.broadcasted_iota(jnp.int32, array.shape, 1)
    front = lax.rem(lane, 2 * quarter) < quarter
    ahead = pltpu.roll(array, LANES - quarter, 1)
    behind = pltpu.roll(array, quarter, 1)
    return jnp.where(front, -ahead, behind)


def ring_steps(count):
    return [0, count - 1, 1] + list(range(2, count - 1))


def pack_kernel(
    where,
    counts,
    dest,
    coords_ref,
    patches_ref,
    values_ref,
    upstream_ref,
    own_ref,
    left_ref,
    right_ref,
    far_ref,
    notes_ref,
):
    packed_refs = (own_ref, left_ref, right_ref, far_ref)
    count = len(packed_refs)
    steps = ring_steps(count)
    rows, width = values_ref.shape
    windows, _, patch_len = coords_ref.shape
    lane = lax.broadcasted_iota(jnp.int32, (1, width), 1)
    live = jnp.zeros((1, width), jnp.int32)
    slot = jnp.zeros((1, width), jnp.int32)
    notes_ref[...] = jnp.zeros_like(notes_ref)
    for window in range(windows):
        at = window * patch_len
        for axis in range(2):
            coord = coords_ref[window, axis : axis + 1, :].astype(F32)
            notes_ref[axis : axis + 1, at : at + patch_len] = coord
        live = jnp.where((lane >= at) & (lane < at + counts[window]), 1, live)
        slot = jnp.where(lane == window, dest[window, 0], slot)
    notes_ref[2:3, :] = live.astype(F32)
    notes_ref[3:4, :] = slot.astype(F32)
    for packed_ref in packed_refs[1:]:
        packed_ref[:rows, :] = patches_ref[:, :width]
        packed_ref[rows : 2 * rows, :] = patches_ref[:, width:]
    parts = width // (2 * HD)
    depth = rows // parts
    kinds = width // HD // count
    tops = [ref.shape[0] - EXTRA - kinds * depth for ref in packed_refs]
    for here in range(count):

        @pl.when(where[0] == here)
        def _():
            for packed_ref, step, top in zip(packed_refs, steps, tops):
                for kind in range(kinds):
                    head = kind * count + (here + step) % count
                    lanes = pl.ds(head * HD, HD)
                    for part in range(parts):
                        span, at = pl.ds(part * depth, depth), part * 2 * HD
                        out = pl.ds(top + kind * depth, depth)
                        packed_ref[out, pl.ds(at, HD)] = values_ref[span, lanes]
                        packed_ref[out, pl.ds(at + HD, HD)] = upstream_ref[span, lanes]

    notes = notes_ref[...].astype(BF16)
    for packed_ref in packed_refs:
        packed_ref[packed_ref.shape[0] - EXTRA :, :] = notes


def pack(where, counts, dest, coords, patches, values, upstream, count):
    rows, width = values.shape
    depth = width // HD // count * rows // (width // (2 * HD)) + EXTRA
    vmem = pl.BlockSpec(memory_space=pltpu.VMEM)
    smem = pl.BlockSpec(memory_space=pltpu.SMEM)
    small = jax.ShapeDtypeStruct((depth, width), BF16)
    large = jax.ShapeDtypeStruct((2 * rows + depth, width), BF16)
    return pl.pallas_call(
        pack_kernel,
        in_specs=[smem] * 3 + [vmem] * 4,
        out_specs=[vmem] * 4,
        out_shape=[small, large, large, large],
        scratch_shapes=[pltpu.VMEM((EXTRA, width), F32)],
        compiler_params=pltpu.CompilerParams(vmem_limit_bytes=VMEM_BYTES),
        name="pack",
    )(where, counts, dest, coords, patches, values, upstream)


def heads_kernel(patch_len, group, where, *refs):
    refs = list(refs)
    take = lambda count: [refs.pop(0) for _ in range(count)]
    own_hbm, other_hbm, table_hbm, patches_hbm, packed_hbm = take(5)
    remote_hbm = take(3)
    context_refs = take(4)
    results = take(2)
    own_ref, other_ref, table_ref, whole_ref = take(4)
    packed_refs = take(4)
    full_ref, sum_ref, dproj_ref, values_ref, upstream_ref, arrivals = take(6)
    sources = len(packed_refs)
    rows, width = patches_hbm.shape[0], packed_hbm.shape[1]
    depth = packed_hbm.shape[0]
    patches_refs = [whole_ref.at[pl.ds(at * rows, rows), :] for at in range(sources)]
    halves = [[ref.at[:, pl.ds(at * width, width)] for at in range(2)] for ref in patches_refs]
    moves = [(own_hbm, own_ref), (other_hbm, other_ref), (table_hbm, table_ref)]
    waits = [[(patches_hbm, patches_refs[0])], [(packed_hbm, packed_refs[0])]]
    for at, source_hbm in enumerate(remote_hbm, 1):
        cut = [source_hbm.at[pl.ds(half * rows, rows), :] for half in range(2)]
        waits.append(list(zip(cut, halves[at])))
        waits.append([(source_hbm.at[pl.ds(2 * rows, depth), :], packed_refs[at])])
    waits = [[move] for move in moves] + waits
    number = 0
    copies = []
    for moves in waits:
        copies.append([])
        for source, target in moves:
            copy = pltpu.make_async_copy(source, target, arrivals.at[number])
            copy.start()
            copies[-1].append(copy)
            number += 1

    def arrive(at):
        for copy in copies[at]:
            copy.wait()

    strip, strips = own_ref.shape[0], own_ref.shape[1] // (2 * HD)
    block = group * patch_len
    scale = 1.0 / math.sqrt(HD)
    full_ref[...] = jnp.zeros_like(full_ref)
    values_ref[...] = jnp.zeros_like(values_ref)
    upstream_ref[...] = jnp.zeros_like(upstream_ref)
    is_first = where[1] == 0
    arrive(0)
    arrive(1)
    for z in range(strips):
        span = pl.ds(z * strip, strip)
        for part in range(2):
            lanes = pl.ds((2 * z + part) * HD, HD)
            own, other = own_ref[:, lanes], other_ref[:, lanes]
            full_ref[span, pl.ds(part * LANES, HD)] = jnp.where(is_first, own, other)
            full_ref[span, pl.ds((2 + part) * LANES, HD)] = jnp.where(is_first, other, own)
    arrive(2)
    row_win = lax.broadcasted_iota(jnp.int32, (block, block), 0) // patch_len
    key_win = lax.broadcasted_iota(jnp.int32, (block, block), 1) // patch_len
    same = row_win == key_win
    kind = lax.broadcasted_iota(jnp.int32, (3 * POSITIONS, rows), 0)
    wanted = lax.rem(kind, POSITIONS).astype(F32)
    starts = [at for at in range(0, rows, block)]
    chains = [(head, at) for head in range(2) for at in range(len(starts))]
    each = range(len(chains))
    for source in range(sources):
        patches_ref, packed_ref = patches_refs[source], packed_refs[source]
        arrive(3 + 2 * source)
        proj = dot(patches_ref[...], full_ref[...], ((1,), (0,)))
        arrive(4 + 2 * source)
        depth = (packed_ref.shape[0] - EXTRA) // 2
        notes = packed_ref[2 * depth :, :rows].astype(F32)
        live_keys = notes[2:3, :]
        by_row = jnp.where(notes[0:1, :] == wanted, 1.0, 0.0)
        by_col = jnp.where(notes[1:2, :] == wanted, 1.0, 0.0)
        chosen = jnp.where(kind < 2 * POSITIONS, by_col, live_keys)
        chosen = jnp.where(kind < POSITIONS, by_row, chosen).astype(BF16)
        tables = dot(chosen, table_ref[0], ((0,), (0,)))
        tables += dot(chosen, table_ref[1], ((0,), (0,)))
        tables += dot(chosen, table_ref[2], ((0,), (0,)))
        for head in range(2):
            out, come = pl.ds(head * LANES, HD), pl.ds(head * depth, depth)
            for part in range(rows // depth):
                span, at = pl.ds(part * depth, depth), part * 2 * HD
                values_ref[span, out] = packed_ref[come, pl.ds(at, HD)]
                upstream_ref[span, out] = packed_ref[come, pl.ds(at + HD, HD)]
        cosines = [tables[s : s + block, :LANES] for s in starts]
        sines = [tables[s : s + block, LANES:] for s in starts]
        masks = [same & (live_keys[:, s : s + block] > 0.5) for s in starts]
        lives = [cosine[:, HD : HD + 1] for cosine in cosines]
        spans = [pl.ds(starts[at], block) for _, at in chains]
        lanes = [pl.ds(head * LANES, LANES) for head, _ in chains]
        blocks = [at for _, at in chains]
        q = [proj[starts[at] : starts[at] + block, 2 * h * LANES :][:, :LANES] for h, at in chains]
        k = [
            proj[starts[at] : starts[at] + block, (2 * h + 1) * LANES :][:, :LANES]
            for h, at in chains
        ]
        turn = lambda x, at: x * cosines[at] + partner(x) * sines[at]
        q = [turn(q[i], blocks[i]).astype(BF16) for i in each]
        k = [turn(k[i], blocks[i]).astype(BF16) for i in each]
        scores = [dot(q[i], k[i], ((1,), (1,))) * scale for i in each]
        v = [values_ref[spans[i], lanes[i]] for i in each]
        dprobs = [dot(upstream_ref[spans[i], lanes[i]], v[i], ((1,), (1,))) for i in each]
        scores = [jnp.where(masks[blocks[i]], scores[i], -1e30) for i in each]
        tops = [jnp.max(scores[i], axis=1, keepdims=True) for i in each]
        exps = [jnp.exp(scores[i] - tops[i]) for i in each]
        sums = [jnp.sum(exps[i], axis=1, keepdims=True) for i in each]
        probs = [exps[i] * (lives[blocks[i]] / sums[i]) for i in each]
        context = [dot(probs[i].astype(BF16), v[i], ((1,), (0,))) for i in each]
        delta = [jnp.sum(probs[i] * dprobs[i], axis=1, keepdims=True) for i in each]
        dscores = [(probs[i] * (dprobs[i] - delta[i]) * scale).astype(BF16) for i in each]
        dquery = [dot(dscores[i], k[i], ((1,), (0,))) for i in each]
        dkey = [dot(dscores[i], q[i], ((0,), (0,))) for i in each]
        back = lambda x, at: (x * cosines[at] - partner(x) * sines[at]).astype(BF16)
        for i in each:
            context_refs[source][spans[i], lanes[i]] = context[i].astype(BF16)
            at = 2 * chains[i][0] * LANES
            here = pl.ds(source * rows + starts[blocks[i]], block)
            dproj_ref[here, pl.ds(at, LANES)] = back(dquery[i], blocks[i])
            dproj_ref[here, pl.ds(at + LANES, LANES)] = back(dkey[i], blocks[i])
    sum_ref[...] = dot(dproj_ref[...], whole_ref[...], ((0,), (0,)))
    for z in range(strips):
        part = jnp.transpose(sum_ref[:, z * strip : (z + 1) * strip]).astype(BF16)
        for at in range(2):
            low = part[:, at * LANES : at * LANES + HD]
            high = part[:, (2 + at) * LANES : (2 + at) * LANES + HD]
            lanes = pl.ds((2 * z + at) * HD, HD)
            results[0][:, lanes] = jnp.where(is_first, low, high)
            results[1][:, lanes] = jnp.where(is_first, high, low)


def some_heads(where, weights, table, arrays, patch_len):
    rows, model_width = arrays[0].shape
    piece = arrays[1].shape
    group = math.gcd(rows // patch_len, max(1, 128 // patch_len))
    vmem = pl.BlockSpec(memory_space=pltpu.VMEM)
    hbm = pl.BlockSpec(memory_space=pltpu.HBM)
    grad_shape = jax.ShapeDtypeStruct(weights[0].shape, BF16)
    return pl.pallas_call(
        functools.partial(heads_kernel, patch_len, group),
        in_specs=[pl.BlockSpec(memory_space=pltpu.SMEM)] + [hbm] * (3 + len(arrays)),
        out_specs=[vmem] * 6,
        out_shape=[jax.ShapeDtypeStruct((rows, 2 * LANES), BF16)] * 4 + [grad_shape] * 2,
        scratch_shapes=[pltpu.VMEM(weights[0].shape, BF16)] * 2
        + [pltpu.VMEM(table.shape, BF16), pltpu.VMEM((4 * rows, model_width), BF16)]
        + [pltpu.VMEM(piece, BF16)] * 4
        + [
            pltpu.VMEM((model_width, 4 * LANES), BF16),
            pltpu.VMEM((4 * LANES, model_width), F32),
            pltpu.VMEM((4 * rows, 4 * LANES), BF16),
            pltpu.VMEM((rows, 2 * LANES), BF16),
            pltpu.VMEM((rows, 2 * LANES), BF16),
            pltpu.SemaphoreType.DMA((14,)),
        ],
        compiler_params=pltpu.CompilerParams(vmem_limit_bytes=VMEM_BYTES),
        cost_estimate=pl.CostEstimate(
            flops=20_000_000_000, bytes_accessed=12_000_000, transcendentals=3_000_000
        ),
        name="heads",
    )(where, *weights, table, *arrays)


def route_kernel(patch_len, slot_of, *refs):
    context_refs, routed_refs, table_ref = refs[:4], refs[4:-1], refs[-1]
    table_ref[...] = jnp.zeros_like(table_ref)
    windows = context_refs[0].shape[0] // patch_len
    for source, context_ref in enumerate(context_refs):
        for window in range(windows):
            slot = slot_of[source * windows + window]
            rows = context_ref[pl.ds(window * patch_len, patch_len), :]
            for head in range(2):
                lanes = pl.ds((2 * source + head) * HD, HD)
                table_ref[slot, :, lanes] = rows[:, head * LANES : head * LANES + HD]
    for at, routed_ref in enumerate(routed_refs):
        count = routed_ref.shape[0]
        routed_ref[...] = table_ref[pl.ds(at * count, count)]


def route(slot_of, contexts, slots, patch_len):
    count = len(contexts)
    vmem = pl.BlockSpec(memory_space=pltpu.VMEM)
    shape = (patch_len, 2 * HD * count)
    return pl.pallas_call(
        functools.partial(route_kernel, patch_len),
        in_specs=[pl.BlockSpec(memory_space=pltpu.SMEM)] + [vmem] * count,
        out_specs=[vmem] * count,
        out_shape=[jax.ShapeDtypeStruct((slots // count,) + shape, BF16)] * count,
        scratch_shapes=[pltpu.VMEM((slots,) + shape, BF16)],
        compiler_params=pltpu.CompilerParams(vmem_limit_bytes=VMEM_BYTES),
        name="route",
    )(slot_of, *contexts)


def regroup_kernel(count, where, *refs):
    inputs, outputs = refs[:count], refs[count:]
    copies = len(outputs) // 2
    for step in range(copies):
        target = lax.rem(where[2] + step, copies)
        for swap in range(2):
            core = where[1] if swap == 0 else 1 - where[1]
            for at, ref in enumerate(inputs):
                outputs[2 * step + swap][at] = ref[2 * target + core]


def regroup(where, pieces):
    slots, patch_len, width = pieces[0].shape
    vmem = pl.BlockSpec(memory_space=pltpu.VMEM)
    piece = jax.ShapeDtypeStruct((len(pieces), patch_len, width), BF16)
    return pl.pallas_call(
        functools.partial(regroup_kernel, len(pieces)),
        in_specs=[pl.BlockSpec(memory_space=pltpu.SMEM)] + [vmem] * len(pieces),
        out_specs=[vmem] * slots,
        out_shape=[piece] * slots,
        compiler_params=pltpu.CompilerParams(vmem_limit_bytes=VMEM_BYTES),
        name="regroup",
    )(where, *pieces)


def hop(array, step, swap):
    copies, cores = lax.axis_size("zl"), lax.axis_size("c")
    if step == 0 and swap == 0:
        return array
    pairs = [
        (z * cores + c, (z + step) % copies * cores + (c + swap) % cores)
        for z in range(copies)
        for c in range(cores)
    ]
    return lax.ppermute(array, ("zl", "c"), pairs)


def settle_kernel(where, places, *refs):
    arrived_refs, placed_ref = refs[:-1], refs[-1]
    copies, nx = len(arrived_refs) // 2, arrived_refs[0].shape[0]
    steps = ring_steps(nx)
    for step in range(copies):
        copy = lax.rem(where[2] + copies - step, copies)
        for swap in range(2):
            core = where[1] if swap == 0 else 1 - where[1]
            for sender in range(nx):
                at = places[sender]
                for source in range(nx):
                    lane = 2 * steps.index((sender - source) % nx)
                    slot = (copy * nx + source) * 2 + core
                    for kind in range(2):
                        here = pl.ds((lane + kind) * HD, HD)
                        rows = arrived_refs[2 * step + swap][at, :, here]
                        placed_ref[slot, :, pl.ds((kind * nx + sender) * HD, HD)] = rows


def settle(where, places, arrived):
    nx, patch_len, width = arrived[0].shape
    vmem = pl.BlockSpec(memory_space=pltpu.VMEM)
    smem = pl.BlockSpec(memory_space=pltpu.SMEM)
    return pl.pallas_call(
        settle_kernel,
        in_specs=[smem, smem] + [vmem] * len(arrived),
        out_specs=vmem,
        out_shape=jax.ShapeDtypeStruct((len(arrived) * nx, patch_len, width), BF16),
        compiler_params=pltpu.CompilerParams(vmem_limit_bytes=VMEM_BYTES),
        name="settle",
    )(where, places, *arrived)


def finish_kernel(cores, arrived_ref, grad_ref):
    heads = arrived_ref.shape[0]
    for place in range(heads):
        head = head_of(place, cores, heads)
        part = arrived_ref[place].astype(F32)
        grad_ref[:, pl.ds(head * HD, HD)] = part[:, :HD]
        grad_ref[:, pl.ds((heads + head) * HD, HD)] = part[:, HD:]


def finish(arrived, cores):
    heads, depth, width = arrived.shape
    vmem = pl.BlockSpec(memory_space=pltpu.VMEM)
    return pl.pallas_call(
        functools.partial(finish_kernel, cores),
        in_specs=[vmem],
        out_specs=vmem,
        out_shape=jax.ShapeDtypeStruct((depth, heads * width), F32),
        compiler_params=pltpu.CompilerParams(vmem_limit_bytes=VMEM_BYTES),
        name="finish",
    )(arrived)


def rotary_table():
    quarter = HD // 4
    lane = jnp.arange(LANES, dtype=jnp.int32)[None, :]
    kind = jnp.arange(3 * POSITIONS, dtype=jnp.int32)[:, None]
    frequency = 10000.0 ** (-(lane % quarter).astype(F32) / quarter)
    angles = (kind % POSITIONS).astype(F32) * frequency
    by_row = (kind < POSITIONS) & (lane < HD // 2)
    by_col = (kind >= POSITIONS) & (kind < 2 * POSITIONS) & (lane >= HD // 2) & (lane < HD)
    used = by_row | by_col
    flag = (kind == 2 * POSITIONS) & (lane == HD)
    cosine = jnp.where(used, jnp.cos(angles), jnp.where(flag, 1.0, 0.0))
    left = jnp.concatenate([cosine, jnp.where(used, jnp.sin(angles), 0.0)], axis=1)
    terms = []
    for _ in range(3):
        term = lax.reduce_precision(left, 8, 7)
        terms.append(term.astype(BF16))
        left = left - term
    return jnp.stack(terms)


def per_device(patches, values, upstream, coords, counts, dest, weight):
    core, here, copy = lax.axis_index("c"), lax.axis_index("x"), lax.axis_index("zl")
    nx, nc, copies = lax.axis_size("x"), lax.axis_size("c"), lax.axis_size("zl")
    ny, nz = lax.axis_size("y"), lax.axis_size("zh")
    heads = nx * nc
    slots = lax.axis_size(PEERS)
    window_count, patch_len, model_width = patches.shape
    value_width = values.shape[-1]
    row_total = window_count * patch_len
    depth = weight.shape[0]

    where = jnp.stack([here, core, copy]).astype(jnp.int32)
    steps = ring_steps(nx)
    patches = patches.reshape(row_total, model_width)
    values = values.reshape(row_total, value_width)
    upstream = upstream.reshape(row_total, value_width)
    own, left, right, far = pack(where, counts, dest, coords, patches, values, upstream, nx)
    left, right = ring(left, "x", steps[1]), ring(right, "x", steps[2])
    far = ring(far, "x", steps[3])

    head = core * nx + here
    slice_q = lax.dynamic_slice_in_dim(weight, head * HD, HD, axis=1)
    slice_k = lax.dynamic_slice_in_dim(weight, value_width + head * HD, HD, axis=1)
    own_w = jnp.concatenate([slice_q, slice_k], axis=1)
    own_w = spread(own_w, "zh")
    own_w = jnp.transpose(own_w, (1, 0, 2)).reshape(depth, nz * 2 * HD)
    own_w = spread(own_w, "y").reshape(ny * depth, nz * 2 * HD)
    weights = (own_w, core_swap(own_w))
    left, right, far = after(own_w, (left, right, far))

    all_dest = [dest[:, 0]]
    for piece in (left, right, far):
        at = piece.shape[0] - EXTRA + 3
        all_dest.append(piece[at, :window_count].astype(jnp.int32))
    all_dest = jnp.concatenate(all_dest)
    step_of = lax.rem(all_dest // nc + nx - here, nx)
    slot_of = jnp.zeros_like(step_of)
    for at, step in enumerate(steps):
        slot_of = jnp.where(step_of == step, at, slot_of)
    slot_of = (slot_of * copies + all_dest // (nc * nx)) * nc + lax.rem(all_dest, nc)

    *contexts, grad, sent = some_heads(
        after(slot_of, where),
        weights,
        rotary_table(),
        (patches, own, left, right, far),
        patch_len,
    )
    grad = (grad.astype(F32) + core_swap(sent).astype(F32)).astype(BF16)
    pieces = route(slot_of, contexts, slots, patch_len)
    grad = after(pieces, grad)
    pieces = [ring(piece, "x", step) for piece, step in zip(pieces, steps)]
    crossed = pieces[1:3]
    pieces = regroup(where, pieces)
    pieces = [hop(piece, at // 2, at % 2) for at, piece in enumerate(pieces)]
    places = [lax.rem(here - sender + nx, nx) for sender in range(nx)]
    places = [sum(jnp.where(at == steps[k], k, 0) for k in range(nx)) for at in places]
    places = jnp.stack(places).astype(jnp.int32)
    placed = settle(where, places, pieces)

    grad = exchange(grad.reshape(ny, depth, nz * 2 * HD), "y")
    grad = jnp.sum(grad.astype(F32), axis=0).astype(BF16)
    grad = jnp.transpose(grad.reshape(depth, nz, 2 * HD), (1, 0, 2))
    grad = jnp.broadcast_to(after(crossed, grad)[None], (copies,) + grad.shape)
    grad = exchange(grad.reshape(copies * nz, depth, 2 * HD), ("zl", "zh"))
    grad = jnp.sum(grad.astype(F32), axis=0).astype(BF16)
    return (placed, finish(spread(grad, ("x", "c")), nc))


def solution(mesh):
    fine = Mesh(mesh.devices.reshape(SPLIT), AXES)
    return jax.shard_map(
        per_device,
        mesh=fine,
        in_specs=(
            P(AXES, None, None),
            P(AXES, None, None),
            P(AXES, None, None),
            P(AXES, None, None),
            P(AXES),
            P(AXES, None),
            P(("zh", "y"), None),
        ),
        out_specs=(P(AXES, None, None), P(("zh", "y"), None)),
        check_vma=False,
    )
```
